256 devices in a mesh: gx: 16 (over y, x), gy: 16 (over z, core).
Axes of the slice: x: 4, y: 4, z: 8, core: 2. Of those that a mesh axis runs over, the one named last changes fastest.
Arguments:
- head_start: float32 [512, 256, 128], P('gx', 'gy'), may hold values from -6 to 6
- recharge: float32 [512, 256, 128], P('gx', 'gy'), may hold values from -12 to 12
- conductivity: float32 [512, 256, 128], P('gx', 'gy'), may hold values from 0.1 to 10
Outputs:
- head: float32 [512, 256, 128], P('gx', 'gy')
The draws below stay inside these ranges and needn't reach their ends.
All inputs are finite; a program needn't handle non-finite values.
Results may differ from the reference program's by a relative error of at most 0.0003.
Values sent between devices are 32-bit elements; how exact they have to be, the bound alone decides.
A program may use at most 64 MiB of HBM per device.

```python
import math
import jax
import jax.numpy as jnp
from jax import lax

CZ = 128
LEVELS = 6
SWEEPS = 2
COARSE_SWEEPS = 16
NX = 512
NY = 256


def block_scale(stream_key, shape, pieces, smallest, high):
    gain = 1.0
    for dim, blocks in pieces:
        draws = jax.random.uniform(jax.random.fold_in(jax.random.fold_in(stream_key, 6), dim), (blocks,), jnp.float32, smallest / len(pieces), high / len(pieces))
        gain = gain * jnp.repeat(jnp.exp(draws), shape[dim] // blocks).reshape((-1,) + (1,) * (len(shape) - 1 - dim))
    return gain


def centred(rng, dims, spread, most, shards=(), kind=jnp.bfloat16):
    result = spread * jax.random.normal(rng, dims, jnp.float32)
    if shards:
        result = result * block_scale(rng, dims, shards, -0.22, 0.18)
    return jnp.clip(result, -most, most).astype(kind)


def setup_inputs(seed: int = 0) -> dict:
    streams_of = jax.random.split(jax.random.key(seed), 4)
    head_start = centred(streams_of[0], (NX, NY, CZ), 1.0, 6.0, ((0, 16), (1, 16)), jnp.float32)
    recharge = centred(streams_of[1], (NX, NY, CZ), 2.0, 12.0, ((0, 16), (1, 16)), jnp.float32)
    conductivity = jnp.clip(jnp.exp(math.log(10.0) - 4.6051702 * jax.random.uniform(streams_of[2], (NX, NY, CZ), jnp.float32) ** block_scale(streams_of[2], (NX, NY, CZ), ((0, 16), (1, 16)), -0.2, 0.2)), 0.1, 10.0)
    return dict(head_start=head_start, recharge=recharge, conductivity=conductivity)


OMEGA = 0.8


def edge_mean(left, right):
    first = jnp.where(left > 0, left, right)
    second = jnp.where(right > 0, right, left)
    return 2.0 * first * second / (first + second)


def face_terms(padded_k):
    face_x = edge_mean(padded_k[:-1, 1:-1, 1:-1], padded_k[1:, 1:-1, 1:-1])
    face_y = edge_mean(padded_k[1:-1, :-1, 1:-1], padded_k[1:-1, 1:, 1:-1])
    face_z = edge_mean(padded_k[1:-1, 1:-1, :-1], padded_k[1:-1, 1:-1, 1:])
    diagonal = face_x[1:] + face_x[:-1] + face_y[:, 1:] + face_y[:, :-1] + face_z[:, :, 1:] + face_z[:, :, :-1]
    return face_x, face_y, face_z, diagonal


def operate(padded, terms, factor):
    face_x, face_y, face_z, diagonal = terms
    inner = padded[1:-1, 1:-1, 1:-1]
    beside_all = face_x[1:] * padded[2:, 1:-1, 1:-1] + face_x[:-1] * padded[:-2, 1:-1, 1:-1]
    beside_all = beside_all + face_y[:, 1:] * padded[1:-1, 2:, 1:-1] + face_y[:, :-1] * padded[1:-1, :-2, 1:-1]
    beside_all = beside_all + face_z[:, :, 1:] * padded[1:-1, 1:-1, 2:] + face_z[:, :, :-1] * padded[1:-1, 1:-1, :-2]
    return factor * (diagonal * inner - beside_all)


def restrict(field):
    a, b, c = field.shape
    return field.reshape(a // 2, 2, b // 2, 2, c // 2, 2).mean(axis=(1, 3, 5))


def prolong(field):
    a, b, c = field.shape
    wide = jnp.broadcast_to(field[:, None, :, None, :, None], (a, 2, b, 2, c, 2))
    return wide.reshape(2 * a, 2 * b, 2 * c)


def smooth(field, source, terms, factor, sweeps):
    first = 0
    if field is None:
        field = OMEGA * source / (factor * terms[3])
        first = 1

    def one_sweep(index, current):
        residue = source - operate(jnp.pad(current, 1), terms, factor)
        return current + OMEGA * residue / (factor * terms[3])

    if sweeps > first:
        field = lax.fori_loop(first, sweeps, one_sweep, field)
    return field


def cycle(level_no, field, source, conduct):
    factor = 0.25 ** level_no
    terms = face_terms(jnp.pad(conduct, 1))
    if level_no == LEVELS - 1:
        return smooth(None, source, terms, factor, COARSE_SWEEPS)
    field = smooth(field, source, terms, factor, SWEEPS)
    residue = source - operate(jnp.pad(field, 1), terms, factor)
    coarse = cycle(level_no + 1, None, restrict(residue), restrict(conduct))
    field = field + prolong(coarse)
    return smooth(field, source, terms, factor, SWEEPS)


def reference(head_start, recharge, conductivity):
    return cycle(0, head_start, recharge, conductivity)
```

```python
from typing import NamedTuple

import jax
import jax.numpy as jnp
from jax import lax
from jax.experimental import pallas as pl
from jax.experimental.pallas import tpu as pltpu
from jax.sharding import PartitionSpec as P

F32 = jnp.float32
LANES = 128
PAD = 8
OMEGA = 0.8
KEEP = 1.0 - OMEGA
COARSE_SWEEPS = 16
BLOCK_X = 32
BLOCK_Y = 16
TALLY_ROWS = 512

class Level(NamedTuple):
    bx: int
    by: int
    hx: int
    rows: int
    first: int
    span: int
    reach: int
    hk: int
    hg: int
    cyrows: int


SPLIT = (
    Level(32, 16, 3, 24, 4, 1, 1, 4, 3, 24),
    Level(16, 8, 4, 16, 4, 2, 1, 5, 4, 24),
    Level(8, 4, 5, 16, 6, 4, 2, 6, 5, 16),
)


def reciprocal(x):
    guess = pltpu.reciprocal(x, approx=True)
    return guess * (2.0 - x * guess)


def face(a, b):
    return (2.0 * a * b) * reciprocal(a + b)


def iota(shape, dim):
    return lax.broadcasted_iota(jnp.int32, shape, dim)


def flag(condition):
    return jnp.where(condition, 1.0, 0.0).astype(F32)


def up(value, shift):
    return pltpu.roll(value, LANES - shift, value.ndim - 1)


def down(value, shift):
    return pltpu.roll(value, shift, value.ndim - 1)


def swap(value, bit):
    if 2 * bit == LANES:
        return down(value, bit)
    lane = iota(value.shape, value.ndim - 1)
    return jnp.where((lane & bit) == 0, up(value, bit), down(value, bit))


def lane_gather(value, index):
    return jnp.take_along_axis(value, index, axis=1)


def segment(step, block, halo):
    low = max(0, step * block - halo)
    high = min(block, (step + 1) * block + halo)
    return low, high - low, low - step * block


def partners(level, halo):
    for dx in (-1, 0, 1):
        for dy in range(-level.reach, level.reach + 1):
            if (dx, dy) != (0, 0):
                yield dx, dy, segment(dx, level.bx, halo), segment(dy, level.by, halo)


def exchange_rows(level, halo):
    return sum(xs[1] * ys[1] for _, _, xs, ys in partners(level, halo))


class Split:
    def __init__(self, level, nx, ny, gx, gy, refs):
        self.at = level
        self.nx, self.ny, self.gx, self.gy = nx, ny, gx, gy
        (self.k, self.va, self.vb, self.g, self.cx, self.cy, self.czl, self.czh, self.w, self.d) = refs

    @staticmethod
    def scratch(level):
        x, rows = level.bx + 2 * level.hx, level.rows
        padded = pltpu.VMEM((x + 2, rows + 2 * PAD, LANES), F32)
        plain = pltpu.VMEM((x, rows, LANES), F32)
        return [
            padded,
            padded,
            padded,
            plain,
            pltpu.VMEM((x + 1, rows, LANES), F32),
            pltpu.VMEM((x, rows + PAD, LANES), F32),
            plain,
            plain,
            plain,
            plain,
        ]

    def x_cut(self, i):
        x = self.gx * self.at.bx + i - self.at.hx
        return flag((x == 0) | (x == self.nx))

    def faces(self):
        lv = self.at
        count, rows, span = lv.bx + 2 * lv.hx, lv.rows, lv.span
        y = self.gy * lv.by + iota((1, lv.cyrows, LANES), 1) - lv.first
        y_open = flag((y != 0) & (y != self.ny))
        y = y[:, :rows]
        lane = iota((1, rows, LANES), 2)
        z_open = flag(lane >= span)
        cuts = flag((y == 0) | (y == self.ny)) + flag((y == -1) | (y == self.ny - 1))
        cuts = cuts + flag(lane < span) + flag(lane >= LANES - span)
        inner = pl.ds(PAD, rows)

        def step(i, carry):
            here, low_x = carry
            beyond = self.k[pl.ds(i + 2, 1), inner, :]
            cut_low, cut_high = self.x_cut(i), self.x_cut(i + 1)
            high_x = face(here, beyond) * (1.0 - cut_high)
            self.cx[pl.ds(i + 1, 1)] = high_x
            low_y = face(
                self.k[pl.ds(i + 1, 1), pl.ds(PAD - 1, lv.cyrows), :],
                self.k[pl.ds(i + 1, 1), pl.ds(PAD, lv.cyrows), :],
            )
            low_y = low_y * y_open
            self.cy[pl.ds(i, 1), pl.ds(0, lv.cyrows), :] = low_y
            low_z = face(down(here, span), here) * z_open
            high_z = up(low_z, span)
            self.czl[pl.ds(i, 1)] = low_z
            self.czh[pl.ds(i, 1)] = high_z
            high_y = self.cy[pl.ds(i, 1), pl.ds(1, rows), :]
            total = low_x + high_x + low_y[:, :rows] + high_y + low_z + high_z
            total = total + here * (cuts + (cut_low + cut_high))
            self.d[pl.ds(i, 1)] = total
            self.w[pl.ds(i, 1)] = OMEGA * reciprocal(total)
            return beyond, high_x

        start = self.k[pl.ds(1, 1), inner, :]
        edge = face(self.k[pl.ds(0, 1), inner, :], start) * (1.0 - self.x_cut(0))
        self.cx[pl.ds(0, 1)] = edge
        lax.fori_loop(0, count, step, (start, edge), unroll=2)

    def stencil(self, v, low, high, row, rows, use):
        span = self.at.span
        inner = pl.ds(PAD + row, rows)
        own = pl.ds(row, rows)

        def step(i, carry):
            before, here, low_x = carry
            after = v[pl.ds(i + 2, 1), inner, :]
            high_x = self.cx[pl.ds(i + 1, 1), own, :]
            total = low_x * before + high_x * after
            total = total + (
                self.cy[pl.ds(i, 1), own, :] * v[pl.ds(i + 1, 1), pl.ds(PAD + row - 1, rows), :]
                + self.cy[pl.ds(i, 1), pl.ds(row + 1, rows), :]
                * v[pl.ds(i + 1, 1), pl.ds(PAD + row + 1, rows), :]
            )
            total = total + (
                self.czl[pl.ds(i, 1), own, :] * down(here, span)
                + self.czh[pl.ds(i, 1), own, :] * up(here, span)
            )
            use(i, here, total)
            return here, after, high_x

        start = (
            v[pl.ds(low, 1), inner, :],
            v[pl.ds(low + 1, 1), inner, :],
            self.cx[pl.ds(low, 1), own, :],
        )
        lax.fori_loop(low, high, step, start, unroll=2)

    def first_sweep(self, dst):
        count, rows = self.at.bx + 2 * self.at.hx, self.at.rows

        def step(i, carry):
            dst[pl.ds(i + 1, 1), pl.ds(PAD, rows), :] = self.w[pl.ds(i, 1)] * self.g[pl.ds(i, 1)]
            return carry

        lax.fori_loop(0, count, step, 0, unroll=2)

    def sweep(self, src, dst, halo):
        lv = self.at

        def use(i, here, total):
            dst[pl.ds(i + 1, 1), pl.ds(PAD, lv.rows), :] = KEEP * here + self.w[pl.ds(i, 1)] * (
                self.g[pl.ds(i, 1)] + total
            )

        self.stencil(src, lv.hx - halo, lv.hx + lv.bx + halo, 0, lv.rows, use)

    def last_sweep(self, src, out):
        lv = self.at
        own = pl.ds(lv.first, lv.by)

        def use(i, here, total):
            out[pl.ds(i - lv.hx, 1)] = KEEP * here + self.w[pl.ds(i, 1), own, :] * (
                self.g[pl.ds(i, 1), own, :] + total
            )

        self.stencil(src, lv.hx, lv.hx + lv.bx, lv.first, lv.by, use)

    def residual(self, v, out):
        lv = self.at
        own = pl.ds(lv.first, lv.by)

        def use(i, here, total):
            out[pl.ds(i - lv.hx, 1)] = (
                self.g[pl.ds(i, 1), own, :] + total - self.d[pl.ds(i, 1), own, :] * here
            )

        self.stencil(v, lv.hx, lv.hx + lv.bx, lv.first, lv.by, use)

    def correct(self, v, coarse, xlow, xcount, xshift, rowshift, wide):
        lv = self.at
        half = lv.rows // 2

        def step(j, carry):
            rows = coarse(j, rowshift, half)
            wide[pl.ds(j, 1), pl.ds(0, half, stride=2), :] = rows
            wide[pl.ds(j, 1), pl.ds(1, half, stride=2), :] = rows
            copies = wide[pl.ds(j, 1)]
            for child in range(2):
                place = (pl.ds(2 * (xlow + j) + xshift + child, 1), pl.ds(PAD, lv.rows))
                v[place] = v[place] + copies
            return carry

        lax.fori_loop(0, xcount, step, 0, unroll=2)


def restrict(read, count, rows, span, scale, write):
    def step(j, carry):
        total = (read(2 * j, 0) + read(2 * j, 1)) + (read(2 * j + 1, 0) + read(2 * j + 1, 1))
        write(j, scale * (total + swap(total, span)))
        return carry

    lax.fori_loop(0, count, step, 0, unroll=2)


class Whole:
    def __init__(self, number, nx, ny, refs):
        self.number, self.nx, self.ny = number, nx, ny
        self.k, self.va, self.vb, self.g, self.c, self.w, self.d = refs

    @staticmethod
    def scratch(nx, ny):
        padded = pltpu.VMEM((nx + 2, ny + 2 * PAD, LANES), F32)
        plain = pltpu.VMEM((nx, ny, LANES), F32)
        return [padded, padded, padded, plain, pltpu.VMEM((6, nx, ny, LANES), F32), plain, plain]

    def clear_edges(self):
        for ref in (self.k, self.va, self.vb):
            for x in (0, self.nx + 1):
                ref[x] = jnp.zeros((self.ny + 2 * PAD, LANES), F32)
            for row in (0, PAD + self.ny):
                ref[:, pl.ds(row, PAD), :] = jnp.zeros((self.nx + 2, PAD, LANES), F32)

    def neighbours(self, v, i):
        inner = pl.ds(PAD, self.ny)
        here = v[pl.ds(i + 1, 1), inner, :]
        before = v[pl.ds(i, 1), inner, :]
        after = v[pl.ds(i + 2, 1), inner, :]
        under = v[pl.ds(i + 1, 1), pl.ds(PAD - 1, self.ny), :]
        over = v[pl.ds(i + 1, 1), pl.ds(PAD + 1, self.ny), :]
        lane = iota(here.shape, 2)
        if self.number == 3:
            before = down(jnp.where(lane >= 96, before, here), 32)
            after = up(jnp.where(lane < 32, after, here), 32)
            odd = (lane & 16) != 0
            under = swap(jnp.where(odd, under, here), 16)
            over = swap(jnp.where(odd, here, over), 16)
            span = 1
        else:
            before = down(jnp.where(lane >= 64, before, here), 64)
            after = up(jnp.where(lane < 64, after, here), 64)
            span = 2
        return (before, after, under, over, down(here, span), up(here, span)), here

    def faces(self):
        shape = (1, self.ny, LANES)
        lane, row = iota(shape, 2), iota(shape, 1)
        z = lane & 15
        if self.number == 3:
            first_x, last_x, first_y, last_y = lane < 32, lane >= 96, (lane & 16) == 0, (lane & 16) != 0
            first_z, last_z = z == 0, z == 15
            first_y, last_y = (row == 0) & first_y, (row == self.ny - 1) & last_y
        else:
            first_x, last_x, first_y, last_y = lane < 64, lane >= 64, row == 0, row == self.ny - 1
            first_z, last_z = z < 2, z >= 14
        cuts_x = (flag(first_x), flag(last_x))
        cuts_yz = tuple(flag(c) for c in (first_y, last_y, first_z, last_z))

        def step(i, carry):
            sides, here = self.neighbours(self.k, i)
            cuts = (cuts_x[0] * flag(i == 0), cuts_x[1] * flag(i == self.nx - 1)) + cuts_yz
            total = jnp.zeros(shape, F32)
            for n in range(6):
                value = face(here, sides[n]) * (1.0 - cuts[n])
                self.c[n, pl.ds(i, 1)] = value
                total = total + (value + here * cuts[n])
            self.d[pl.ds(i, 1)] = total
            self.w[pl.ds(i, 1)] = OMEGA * reciprocal(total)
            return carry

        lax.fori_loop(0, self.nx, step, 0, unroll=2)

    def beside(self, v, i):
        sides, here = self.neighbours(v, i)
        parts = [self.c[n, pl.ds(i, 1)] * sides[n] for n in range(6)]
        return here, (parts[0] + parts[1]) + (parts[2] + parts[3]) + (parts[4] + parts[5])

    def first_sweep(self, dst):
        dst[pl.ds(1, self.nx), pl.ds(PAD, self.ny), :] = self.w[...] * self.g[...]

    def sweep(self, src, dst):
        def step(i, carry):
            here, total = self.beside(src, i)
            dst[pl.ds(i + 1, 1), pl.ds(PAD, self.ny), :] = KEEP * here + self.w[pl.ds(i, 1)] * (
                self.g[pl.ds(i, 1)] + total
            )
            return carry

        lax.fori_loop(0, self.nx, step, 0, unroll=4)

    def residual(self, v, use):
        def step(i, carry):
            here, total = self.beside(v, i)
            use(i, self.g[pl.ds(i, 1)] + total - self.d[pl.ds(i, 1)] * here)
            return carry

        lax.fori_loop(0, self.nx, step, 0, unroll=4)

    def correct(self, v, rows_of):
        inner = pl.ds(PAD, self.ny)

        def step(i, carry):
            v[pl.ds(i + 1, 1), inner, :] = v[pl.ds(i + 1, 1), inner, :] + rows_of(i)
            return carry

        lax.fori_loop(0, self.nx, step, 0, unroll=4)


def octet_3(value):
    value = value + swap(value, 1)
    value = value + swap(value, 16)
    return value + swap(value, 32)


def pack_5(ref, fill, scale, nx, ny):
    half = ny // 2
    shape = (half, LANES)
    lane = iota(shape, 1)
    index = (lane & 3) * 4
    packed = jnp.full(shape, fill, F32)
    for i in range(nx):
        rows = ref[i, pl.ds(0, half, stride=2), :] + ref[i, pl.ds(1, half, stride=2), :]
        rows = rows + swap(rows, 2)
        rows = scale * (rows + swap(rows, 64))
        packed = jnp.where((lane >> 2) == i, lane_gather(rows, index), packed)
    return packed


def solve_5(k, g, nx):
    shape = k.shape
    lane, row = iota(shape, 1), iota(shape, 0)
    rows = shape[0]
    x, z = lane >> 2, lane & 3

    def sides(v):
        return (
            down(v, 4),
            up(v, 4),
            pltpu.roll(v, 1, 0),
            pltpu.roll(v, rows - 1, 0),
            down(v, 1),
            up(v, 1),
        )

    cuts = (x == 0, x == nx - 1, row == 0, row == rows - 1, z == 0, z == 3)
    total = jnp.zeros(shape, F32)
    faces = []
    for cut, beyond in zip(cuts, sides(k)):
        value = face(k, beyond)
        faces.append(jnp.where(cut, 0.0, value))
        total = total + jnp.where(cut, k, value)
    weight = OMEGA * reciprocal(total)
    faces = [weight * value for value in faces]
    start = weight * g

    def step(_, v):
        parts = [c * beyond for c, beyond in zip(faces, sides(v))]
        return (KEEP * v + start) + ((parts[0] + parts[1]) + (parts[2] + parts[3]) + (parts[4] + parts[5]))

    return lax.fori_loop(0, COARSE_SWEEPS - 1, step, start)


N_SPLIT = 10
N_WHOLE = 7


def kernel(gx_size, gy_size, head, recharge, conductivity, out, *refs):
    refs = list(refs)
    gx, gy = lax.axis_index("gx"), lax.axis_index("gy")
    split = []
    for number, level in enumerate(SPLIT):
        nx, ny = gx_size * level.bx, gy_size * level.by
        split.append(Split(level, nx, ny, gx, gy, refs[:N_SPLIT]))
        del refs[:N_SPLIT]
    whole = []
    for number in (3, 4):
        whole.append(Whole(number, gx_size, gy_size, refs[:N_WHOLE]))
        del refs[:N_WHOLE]
    (
        res0,
        res1,
        res2,
        wide0,
        wide1,
        rows_k,
        rows_g,
        strip_k,
        strip_g,
        rest,
        coarse5,
        tally,
        local_sem,
        send_sem,
        recv_sem,
    ) = refs
    zero, one, two = split
    three, four = whole

    def device(dx, dy):
        return {
            "gx": lax.rem(gx + (dx + gx_size), gx_size),
            "gy": lax.rem(gy + (dy + gy_size), gy_size),
        }

    barrier = pltpu.get_barrier_semaphore()

    def greet(dx, dy):
        pl.semaphore_signal(
            barrier, inc=1, device_id=device(dx, dy), device_id_type=pl.DeviceIdType.MESH
        )

    local = [
        pltpu.make_async_copy(
            conductivity,
            zero.k.at[pl.ds(4, BLOCK_X), pl.ds(PAD + 4, BLOCK_Y), :],
            local_sem.at[0],
        ),
        pltpu.make_async_copy(
            head, zero.va.at[pl.ds(4, BLOCK_X), pl.ds(PAD + 4, BLOCK_Y), :], local_sem.at[1]
        ),
        pltpu.make_async_copy(
            recharge, zero.g.at[pl.ds(3, BLOCK_X), pl.ds(4, BLOCK_Y), :], local_sem.at[2]
        ),
    ]
    for copy in local:
        copy.start()

    greeted = 0
    for dx, dy, _, _ in partners(SPLIT[2], 6):
        greet(dx, dy)
        greeted += 1

    def greet_y(k, carry):
        greet(0, k)
        return carry

    def greet_x(k, carry):
        greet(k, 0)
        return carry

    if gy_size > 5:
        lax.fori_loop(3, gy_size - 2, greet_y, 0)
        greeted += gy_size - 5
    if gx_size > 3:
        lax.fori_loop(2, gx_size - 1, greet_x, 0)
        greeted += gx_size - 3

    for ref in whole:
        ref.clear_edges()
    pl.semaphore_wait(barrier, greeted)

    def push(src, dst, stage, dx, dy):
        pltpu.make_async_remote_copy(
            src_ref=src,
            dst_ref=dst,
            send_sem=send_sem.at[stage],
            recv_sem=recv_sem.at[stage],
            device_id=device(dx, dy),
            device_id_type=pl.DeviceIdType.MESH,
        ).start()

    def exchange(level, halo, stage, src, src_x, src_row, dst, dst_x, dst_row):
        for dx, dy, xs, ys in partners(level, halo):
            push(
                src.at[pl.ds(src_x + xs[0], xs[1]), pl.ds(src_row + ys[0], ys[1]), :],
                dst.at[pl.ds(dst_x + xs[2], xs[1]), pl.ds(dst_row + ys[2], ys[1]), :],
                stage,
                dx,
                dy,
            )

    def arrived(stage, rows):
        block = tally.at[pl.ds(0, rows), :]
        pltpu.make_async_copy(block, block, recv_sem.at[stage]).wait()

    def sent(stage, rows):
        block = tally.at[pl.ds(0, rows), :]
        pltpu.make_async_copy(block, block, send_sem.at[stage]).wait()

    def gather_y(strip, stage):
        def step(k, carry):
            push(strip.at[pl.ds(gy, 1), :], strip.at[pl.ds(gy, 1), :], stage, 0, k)
            return carry

        lax.fori_loop(1, gy_size, step, 0)

    def gather_x(strip, place, stage):
        def step(k, carry):
            push(strip, place, stage, k, 0)
            return carry

        lax.fori_loop(1, gx_size, step, 0)

    lv0, lv1, lv2 = SPLIT
    exchange(lv0, lv0.hk, 0, conductivity, 0, 0, zero.k, 4, PAD + 4)
    exchange(lv0, 4, 1, head, 0, 0, zero.va, 4, PAD + 4)
    exchange(lv0, lv0.hg, 2, recharge, 0, 0, zero.g, 3, 4)

    def reader(ref, x0, row0, rows):
        return lambda x, offset: ref[pl.ds(x0 + x, 1), pl.ds(row0 + offset, rows, stride=2), :]

    def writer(ref, x0, row0, rows):
        def write(x, value):
            ref[pl.ds(x0 + x, 1), pl.ds(row0, rows), :] = value

        return write

    def pack_3(rows):
        lane, row = iota((8, LANES), 1), iota((8, LANES), 0)
        picked = lane_gather(rows[...], (lane & 15) * 8)
        return jnp.sum(jnp.where((lane >> 4) == row, picked, 0.0), axis=0, keepdims=True)

    def row_writer(ref):
        def write(x, value):
            ref[pl.ds(2 * x, 2), :] = value.reshape(2, LANES)

        return write

    local[0].wait()
    restrict(reader(zero.k, 4, PAD + 4, 8), 16, 8, 1, 0.125, writer(one.k, 5, PAD + 4, 8))
    restrict(reader(one.k, 5, PAD + 4, 4), 8, 4, 2, 0.125, writer(two.k, 6, PAD + 6, 4))
    restrict(reader(two.k, 6, PAD + 6, 2), 4, 2, 4, 0.125, row_writer(rows_k))
    exchange(lv1, lv1.hk, 3, one.k, 5, PAD + 4, one.k, 5, PAD + 4)
    strip_k[pl.ds(gy, 1), :] = pack_3(rows_k)
    gather_y(strip_k, 7)
    exchange(lv2, lv2.hk, 5, two.k, 6, PAD + 6, two.k, 6, PAD + 6)

    arrived(0, exchange_rows(lv0, lv0.hk))
    zero.faces()
    arrived(7, gy_size - 1)
    inner = pl.ds(PAD, gy_size)
    three.k[pl.ds(gx + 1, 1), inner, :] = strip_k[...].reshape(1, gy_size, LANES)
    gather_x(strip_k, three.k.at[gx + 1, inner, :], 8)
    local[1].wait()
    local[2].wait()
    arrived(1, exchange_rows(lv0, 4))
    arrived(2, exchange_rows(lv0, lv0.hg))
    zero.sweep(zero.va, zero.vb, 3)
    zero.sweep(zero.vb, zero.va, 2)
    zero.residual(zero.va, res0)
    restrict(reader(res0, 0, 0, 8), 16, 8, 1, 0.5, writer(one.g, 4, 4, 8))

    exchange(lv1, lv1.hg, 4, one.g, 4, 4, one.g, 4, 4)
    arrived(3, exchange_rows(lv1, lv1.hk))
    one.faces()
    arrived(4, exchange_rows(lv1, lv1.hg))
    one.first_sweep(one.va)
    one.sweep(one.va, one.vb, 3)
    one.residual(one.vb, res1)
    restrict(reader(res1, 0, 0, 4), 8, 4, 2, 0.5, writer(two.g, 5, 6, 4))

    exchange(lv2, lv2.hg, 6, two.g, 5, 6, two.g, 5, 6)
    arrived(5, exchange_rows(lv2, lv2.hk))
    two.faces()
    arrived(6, exchange_rows(lv2, lv2.hg))
    two.first_sweep(two.va)
    two.sweep(two.va, two.vb, 4)
    two.residual(two.vb, res2)
    restrict(reader(res2, 0, 0, 2), 4, 2, 4, 0.5, row_writer(rows_g))

    strip_g[pl.ds(gy, 1), :] = pack_3(rows_g)
    gather_y(strip_g, 9)
    arrived(8, (gx_size - 1) * gy_size)
    three.faces()

    def coarser_k(i, carry):
        four.k[pl.ds(i + 1, 1), inner, :] = 0.125 * octet_3(three.k[pl.ds(i + 1, 1), inner, :])
        return carry

    lax.fori_loop(0, gx_size, coarser_k, 0, unroll=4)
    rest[...] = four.k[pl.ds(1, gx_size), inner, :]
    k5 = pack_5(rest, 1.0, 0.125, gx_size, gy_size)
    four.faces()
    arrived(9, gy_size - 1)
    three.g[pl.ds(gx, 1)] = strip_g[...].reshape(1, gy_size, LANES)
    gather_x(strip_g, three.g.at[gx], 10)
    arrived(10, (gx_size - 1) * gy_size)

    three.first_sweep(three.va)
    three.sweep(three.va, three.vb)

    def to_four(i, value):
        four.g[pl.ds(i, 1)] = 0.5 * octet_3(value)

    three.residual(three.vb, to_four)
    four.first_sweep(four.va)
    four.sweep(four.va, four.vb)

    def to_five(i, value):
        rest[pl.ds(i, 1)] = value

    four.residual(four.vb, to_five)
    v5 = solve_5(k5, pack_5(rest, 0.0, 0.5, gx_size, gy_size), gx_size)

    coarse5[pl.ds(0, gy_size // 2, stride=2), :] = v5
    coarse5[pl.ds(1, gy_size // 2, stride=2), :] = v5
    wide5 = coarse5[...]

    def from_five(i):
        index = i * 4 + ((iota((gy_size, LANES), 1) & 15) >> 2)
        return lane_gather(wide5, index).reshape(1, gy_size, LANES)

    four.correct(four.vb, from_five)
    four.sweep(four.vb, four.va)
    four.sweep(four.va, four.vb)
    three.correct(three.vb, lambda i: four.vb[pl.ds(i + 1, 1), inner, :])
    three.sweep(three.vb, three.va)
    three.sweep(three.va, three.vb)

    row = iota((lv2.rows, LANES), 0)
    lane = iota((lv2.rows, LANES), 1)
    y3 = (row >> 1) - 1
    for dx in (-1, 0, 1):
        gxn = lax.rem(gx + (dx + gx_size), gx_size) + 1
        near = []
        for dy in (-1, 0, 1):
            gyn = lax.rem(gy + (dy + gy_size), gy_size) + PAD
            near.append(three.vb[pl.ds(gxn, 1), pl.ds(gyn, 1), :].reshape(1, LANES))
        rows = jnp.where(y3 < 2, near[0], jnp.where(y3 < 4, near[1], near[2]))
        for x in ((2, 3), (0, 1, 2, 3), (0, 1))[dx + 1]:
            copies = lane_gather(rows, (2 * x + (y3 & 1)) * 16 + (lane >> 3))
            for child in range(2):
                place = (2 * (4 * dx + x) + child + 6, pl.ds(PAD, lv2.rows))
                two.vb[place] = two.vb[place] + copies
    two.sweep(two.vb, two.va, 3)
    two.sweep(two.va, two.vb, 2)

    def coarse_rows(ref, x0):
        return lambda j, row0, rows: ref[pl.ds(x0 + j, 1), pl.ds(PAD + row0, rows), :]

    one.correct(one.vb, coarse_rows(two.vb, 6 - 2), -2, 12, 5, 4, wide1)
    one.sweep(one.vb, one.va, 2)
    one.sweep(one.va, one.vb, 1)
    zero.correct(zero.va, coarse_rows(one.vb, 5 - 1), -1, 18, 4, 2, wide0)
    zero.sweep(zero.va, zero.vb, 1)
    zero.last_sweep(zero.vb, out)

    sent(0, exchange_rows(lv0, lv0.hk))
    sent(1, exchange_rows(lv0, 4))
    sent(2, exchange_rows(lv0, lv0.hg))
    sent(3, exchange_rows(lv1, lv1.hk))
    sent(4, exchange_rows(lv1, lv1.hg))
    sent(5, exchange_rows(lv2, lv2.hk))
    sent(6, exchange_rows(lv2, lv2.hg))
    sent(7, gy_size - 1)
    sent(8, (gx_size - 1) * gy_size)
    sent(9, gy_size - 1)
    sent(10, (gx_size - 1) * gy_size)


def on_device(gx_size, gy_size, head, recharge, conductivity):
    scratch = []
    for level in SPLIT:
        scratch += Split.scratch(level)
    for _ in range(2):
        scratch += Whole.scratch(gx_size, gy_size)
    scratch += [
        pltpu.VMEM((32, 16, LANES), F32),
        pltpu.VMEM((16, 8, LANES), F32),
        pltpu.VMEM((8, 4, LANES), F32),
        pltpu.VMEM((18, 24, LANES), F32),
        pltpu.VMEM((12, 16, LANES), F32),
        pltpu.VMEM((8, LANES), F32),
        pltpu.VMEM((8, LANES), F32),
        pltpu.VMEM((gy_size, LANES), F32),
        pltpu.VMEM((gy_size, LANES), F32),
        pltpu.VMEM((gx_size, gy_size, LANES), F32),
        pltpu.VMEM((gy_size, LANES), F32),
        pltpu.VMEM((TALLY_ROWS, LANES), F32),
        pltpu.SemaphoreType.DMA((3,)),
        pltpu.SemaphoreType.DMA((11,)),
        pltpu.SemaphoreType.DMA((11,)),
    ]

    def body(*refs):
        kernel(gx_size, gy_size, *refs)

    return pl.pallas_call(
        body,
        out_shape=jax.ShapeDtypeStruct(head.shape, F32),
        in_specs=[pl.BlockSpec(memory_space=pl.ANY)] * 3,
        out_specs=pl.BlockSpec(memory_space=pltpu.VMEM),
        scratch_shapes=scratch,
        compiler_params=pltpu.CompilerParams(
            collective_id=0, has_side_effects=True, vmem_limit_bytes=40 * 1024 * 1024
        ),
        name="vcycle",
    )(head, recharge, conductivity)


def solution(mesh):
    gx_size, gy_size = mesh.shape["gx"], mesh.shape["gy"]

    def one_device(head, recharge, conductivity):
        return on_device(gx_size, gy_size, head, recharge, conductivity)

    spec = P("gx", "gy", None)
    return jax.shard_map(
        one_device, mesh=mesh, in_specs=(spec, spec, spec), out_specs=spec, check_vma=False
    )
```

```python
from typing import NamedTuple

import jax
import jax.numpy as jnp
from jax import lax
from jax.experimental import pallas as pl
from jax.experimental.pallas import tpu as pltpu
from jax.sharding import PartitionSpec as P

F32 = jnp.float32
LANES = 128
PAD = 8
OMEGA = 0.8
KEEP = 1.0 - OMEGA
COARSE_SWEEPS = 16
BLOCK_X = 32
BLOCK_Y = 16
TALLY_ROWS = 512

class Level(NamedTuple):
    bx: int
    by: int
    hx: int
    rows: int
    first: int
    span: int
    reach: int
    hk: int
    hg: int
    cyrows: int


SPLIT = (
    Level(32, 16, 3, 24, 4, 1, 1, 4, 3, 24),
    Level(16, 8, 4, 16, 4, 2, 1, 5, 4, 24),
    Level(8, 4, 5, 16, 6, 4, 2, 6, 5, 16),
)


def reciprocal(x):
    guess = pltpu.reciprocal(x, approx=True)
    return guess * (2.0 - x * guess)


def face(a, b):
    return (2.0 * a * b) * reciprocal(a + b)


def iota(shape, dim):
    return lax.broadcasted_iota(jnp.int32, shape, dim)


def flag(condition):
    return jnp.where(condition, 1.0, 0.0).astype(F32)


def up(value, shift):
    return pltpu.roll(value, LANES - shift, value.ndim - 1)


def down(value, shift):
    return pltpu.roll(value, shift, value.ndim - 1)


def swap(value, bit):
    if 2 * bit == LANES:
        return down(value, bit)
    lane = iota(value.shape, value.ndim - 1)
    return jnp.where((lane & bit) == 0, up(value, bit), down(value, bit))


def lane_gather(value, index):
    return jnp.take_along_axis(value, index, axis=1)


def segment(step, block, halo):
    low = max(0, step * block - halo)
    high = min(block, (step + 1) * block + halo)
    return low, high - low, low - step * block


def partners(level, halo):
    for dx in (-1, 0, 1):
        for dy in range(-level.reach, level.reach + 1):
            if (dx, dy) != (0, 0):
                yield dx, dy, segment(dx, level.bx, halo), segment(dy, level.by, halo)


def exchange_rows(level, halo):
    return sum(xs[1] * ys[1] for _, _, xs, ys in partners(level, halo))


class Split:
    def __init__(self, level, nx, ny, gx, gy, refs):
        self.at = level
        self.nx, self.ny, self.gx, self.gy = nx, ny, gx, gy
        (self.k, self.va, self.vb, self.g, self.cx, self.cy, self.czl, self.czh, self.w, self.d) = refs

    @staticmethod
    def scratch(level):
        x, rows = level.bx + 2 * level.hx, level.rows
        padded = pltpu.VMEM((x + 2, rows + 2 * PAD, LANES), F32)
        plain = pltpu.VMEM((x, rows, LANES), F32)
        return [
            padded,
            padded,
            padded,
            plain,
            pltpu.VMEM((x + 1, rows, LANES), F32),
            pltpu.VMEM((x, rows + PAD, LANES), F32),
            plain,
            plain,
            plain,
            plain,
        ]

    def faces(self):
        lv = self.at
        count, rows, span = lv.bx + 2 * lv.hx, lv.rows, lv.span
        y = self.gy * lv.by + iota((1, lv.cyrows, LANES), 1) - lv.first
        y_open = flag((y != 0) & (y != self.ny))
        y = y[:, :rows]
        lane = iota((1, rows, LANES), 2)
        z_open = flag(lane >= span)
        cuts = flag((y == 0) | (y == self.ny)) + flag((y == -1) | (y == self.ny - 1))
        cuts = cuts + flag(lane < span) + flag(lane >= LANES - span)
        inner = pl.ds(PAD, rows)
        all_x = pl.ds(1, count)
        here = self.k[all_x, inner, :]
        self.cx[...] = face(
            self.k[pl.ds(0, count + 1), inner, :], self.k[pl.ds(1, count + 1), inner, :]
        )
        cut_low, cut_high = flag(self.gx == 0), flag(self.gx * lv.bx + lv.bx == self.nx)
        for i, cut in ((lv.hx, cut_low), (lv.hx + lv.bx, cut_high)):
            self.cx[i] = self.cx[i] * (1.0 - cut)
        self.cy[:, pl.ds(0, lv.cyrows), :] = y_open * face(
            self.k[all_x, pl.ds(PAD - 1, lv.cyrows), :], self.k[all_x, pl.ds(PAD, lv.cyrows), :]
        )
        low_z = face(down(here, span), here) * z_open
        high_z = up(low_z, span)
        self.czl[...] = low_z
        self.czh[...] = high_z
        total = self.cx[pl.ds(0, count)] + self.cx[pl.ds(1, count)]
        total = total + (self.cy[:, pl.ds(0, rows), :] + self.cy[:, pl.ds(1, rows), :])
        self.d[...] = (total + (low_z + high_z)) + here * cuts
        for i, cut in ((lv.hx, cut_low), (lv.hx + lv.bx - 1, cut_high)):
            self.d[i] = self.d[i] + self.k[i + 1, inner, :] * cut
        self.w[...] = OMEGA * reciprocal(self.d[...])

    def beside(self, v, low, count, row, rows):
        span = self.at.span
        inner, own = pl.ds(PAD + row, rows), pl.ds(row, rows)
        x, mid = pl.ds(low, count), pl.ds(low + 1, count)
        here = v[mid, inner, :]
        along_x = self.cx[x, own, :] * v[x, inner, :] + self.cx[mid, own, :] * v[pl.ds(low + 2, count), inner, :]
        along_y = (
            self.cy[x, own, :] * v[mid, pl.ds(PAD + row - 1, rows), :]
            + self.cy[x, pl.ds(row + 1, rows), :] * v[mid, pl.ds(PAD + row + 1, rows), :]
        )
        along_z = self.czl[x, own, :] * down(here, span) + self.czh[x, own, :] * up(here, span)
        return here, (along_x + along_y) + along_z

    def first_sweep(self, dst):
        dst[pl.ds(1, self.at.bx + 2 * self.at.hx), pl.ds(PAD, self.at.rows), :] = self.w[...] * self.g[...]

    def sweep(self, src, dst, halo):
        lv = self.at
        low, count = lv.hx - halo, lv.bx + 2 * halo
        here, total = self.beside(src, low, count, 0, lv.rows)
        x = pl.ds(low, count)
        dst[pl.ds(low + 1, count), pl.ds(PAD, lv.rows), :] = KEEP * here + self.w[x] * (self.g[x] + total)

    def last_sweep(self, src, out):
        lv = self.at
        x, own = pl.ds(lv.hx, lv.bx), pl.ds(lv.first, lv.by)
        here, total = self.beside(src, lv.hx, lv.bx, lv.first, lv.by)
        out[...] = KEEP * here + self.w[x, own, :] * (self.g[x, own, :] + total)

    def residual(self, v):
        lv = self.at
        x, own = pl.ds(lv.hx, lv.bx), pl.ds(lv.first, lv.by)
        here, total = self.beside(v, lv.hx, lv.bx, lv.first, lv.by)
        return self.g[x, own, :] + total - self.d[x, own, :] * here

    def correct(self, v, coarse, x0, count, wide):
        rows = self.at.rows
        half = rows // 2
        wide[:, pl.ds(0, half, stride=2), :] = coarse
        wide[:, pl.ds(1, half, stride=2), :] = coarse
        place = (pl.ds(x0, 2 * count), pl.ds(PAD, rows))
        copies = jnp.broadcast_to(wide[...][:, None], (count, 2, rows, LANES))
        v[place] = v[place] + copies.reshape(2 * count, rows, LANES)


def restrict(value, half, span, scale):
    x, y, _ = value.shape
    value = value.reshape(x // 2, 2, y, LANES)
    half[...] = value[:, 0] + value[:, 1]
    total = half[:, pl.ds(0, y // 2, stride=2), :] + half[:, pl.ds(1, y // 2, stride=2), :]
    return scale * (total + swap(total, span))


class Whole:
    def __init__(self, number, nx, ny, refs):
        self.number, self.nx, self.ny = number, nx, ny
        self.k, self.va, self.vb, self.g, self.c, self.w, self.d = refs

    @staticmethod
    def scratch(nx, ny):
        padded = pltpu.VMEM((nx + 2, ny + 2 * PAD, LANES), F32)
        plain = pltpu.VMEM((nx, ny, LANES), F32)
        return [padded, padded, padded, plain, pltpu.VMEM((6, nx, ny, LANES), F32), plain, plain]

    def clear_edges(self):
        for ref in (self.k, self.va, self.vb):
            for x in (0, self.nx + 1):
                ref[x] = jnp.zeros((self.ny + 2 * PAD, LANES), F32)
            for row in (0, PAD + self.ny):
                ref[:, pl.ds(row, PAD), :] = jnp.zeros((self.nx + 2, PAD, LANES), F32)

    def inside(self, ref):
        return ref.at[pl.ds(1, self.nx), pl.ds(PAD, self.ny), :]

    def neighbours(self, v):
        inner, all_x = pl.ds(PAD, self.ny), pl.ds(1, self.nx)
        here = v[all_x, inner, :]
        before = v[pl.ds(0, self.nx), inner, :]
        after = v[pl.ds(2, self.nx), inner, :]
        under = v[all_x, pl.ds(PAD - 1, self.ny), :]
        over = v[all_x, pl.ds(PAD + 1, self.ny), :]
        lane = iota((1, self.ny, LANES), 2)
        if self.number == 3:
            before = down(jnp.where(lane >= 96, before, here), 32)
            after = up(jnp.where(lane < 32, after, here), 32)
            odd = (lane & 16) != 0
            under = swap(jnp.where(odd, under, here), 16)
            over = swap(jnp.where(odd, here, over), 16)
            span = 1
        else:
            before = down(jnp.where(lane >= 64, before, here), 64)
            after = up(jnp.where(lane < 64, after, here), 64)
            span = 2
        return (before, after, under, over, down(here, span), up(here, span)), here

    def faces(self):
        shape = (self.nx, self.ny, LANES)
        lane, row, x = iota(shape, 2), iota(shape, 1), iota(shape, 0)
        z = lane & 15
        if self.number == 3:
            first_x, last_x, first_y, last_y = lane < 32, lane >= 96, (lane & 16) == 0, (lane & 16) != 0
            first_z, last_z = z == 0, z == 15
            first_y, last_y = (row == 0) & first_y, (row == self.ny - 1) & last_y
        else:
            first_x, last_x, first_y, last_y = lane < 64, lane >= 64, row == 0, row == self.ny - 1
            first_z, last_z = z < 2, z >= 14
        first_x, last_x = (x == 0) & first_x, (x == self.nx - 1) & last_x
        sides, here = self.neighbours(self.k)
        total = jnp.zeros(shape, F32)
        for n, cut in enumerate((first_x, last_x, first_y, last_y, first_z, last_z)):
            value = face(here, sides[n])
            self.c[n] = jnp.where(cut, 0.0, value)
            total = total + jnp.where(cut, here, value)
        self.d[...] = total
        self.w[...] = OMEGA * reciprocal(total)

    def beside(self, v):
        sides, here = self.neighbours(v)
        parts = [self.c[n] * sides[n] for n in range(6)]
        return here, (parts[0] + parts[1]) + (parts[2] + parts[3]) + (parts[4] + parts[5])

    def first_sweep(self, dst):
        self.inside(dst)[...] = self.w[...] * self.g[...]

    def sweep(self, src, dst):
        here, total = self.beside(src)
        self.inside(dst)[...] = KEEP * here + self.w[...] * (self.g[...] + total)

    def residual(self, v):
        here, total = self.beside(v)
        return self.g[...] + total - self.d[...] * here

    def correct(self, v, values):
        place = self.inside(v)
        place[...] = place[...] + values


def octet_3(value):
    value = value + swap(value, 1)
    value = value + swap(value, 16)
    return value + swap(value, 32)


def pack_5(ref, fill, scale, nx, ny):
    half = ny // 2
    shape = (nx, half, LANES)
    rows = ref[:, pl.ds(0, half, stride=2), :] + ref[:, pl.ds(1, half, stride=2), :]
    rows = rows + swap(rows, 2)
    rows = scale * (rows + swap(rows, 64))
    index = (iota((nx * half, LANES), 1) & 3) * 4
    rows = lane_gather(rows.reshape(nx * half, LANES), index).reshape(shape)
    packed = jnp.sum(jnp.where((iota(shape, 2) >> 2) == iota(shape, 0), rows, 0.0), axis=0)
    return packed + jnp.where(iota((half, LANES), 1) >= 4 * nx, fill, 0.0)


def faces_5(k, nx):
    shape = k.shape
    lane, row = iota(shape, 1), iota(shape, 0)
    x, z = lane >> 2, lane & 3
    cuts = (x == 0, x == nx - 1, row == 0, row == shape[0] - 1, z == 0, z == 3)
    total = jnp.zeros(shape, F32)
    faces = []
    for cut, beyond in zip(cuts, sides_5(k)):
        value = face(k, beyond)
        faces.append(jnp.where(cut, 0.0, value))
        total = total + jnp.where(cut, k, value)
    weight = OMEGA * reciprocal(total)
    return weight, [weight * value for value in faces]


def sides_5(v):
    rows = v.shape[0]
    return (down(v, 4), up(v, 4), pltpu.roll(v, 1, 0), pltpu.roll(v, rows - 1, 0), down(v, 1), up(v, 1))


def solve_5(weight, faces, g):
    start = weight * g

    def step(_, v):
        parts = [c * beyond for c, beyond in zip(faces, sides_5(v))]
        return (KEEP * v + start) + ((parts[0] + parts[1]) + (parts[2] + parts[3]) + (parts[4] + parts[5]))

    return lax.fori_loop(0, COARSE_SWEEPS - 1, step, start)


N_SPLIT = 10
N_WHOLE = 7


def kernel(gx_size, gy_size, head, recharge, conductivity, out, *refs):
    refs = list(refs)
    gx, gy = lax.axis_index("gx"), lax.axis_index("gy")
    split = []
    for number, level in enumerate(SPLIT):
        nx, ny = gx_size * level.bx, gy_size * level.by
        split.append(Split(level, nx, ny, gx, gy, refs[:N_SPLIT]))
        del refs[:N_SPLIT]
    whole = []
    for number in (3, 4):
        whole.append(Whole(number, gx_size, gy_size, refs[:N_WHOLE]))
        del refs[:N_WHOLE]
    (
        half0,
        half1,
        half2,
        wide0,
        wide1,
        rows_k,
        rows_g,
        strip_k,
        strip_g,
        rest,
        coarse5,
        tally,
        local_sem,
        send_sem,
        recv_sem,
    ) = refs
    zero, one, two = split
    three, four = whole

    def device(dx, dy):
        return {
            "gx": lax.rem(gx + (dx + gx_size), gx_size),
            "gy": lax.rem(gy + (dy + gy_size), gy_size),
        }

    barrier = pltpu.get_barrier_semaphore()

    def greet(dx, dy):
        pl.semaphore_signal(
            barrier, inc=1, device_id=device(dx, dy), device_id_type=pl.DeviceIdType.MESH
        )

    local = [
        pltpu.make_async_copy(
            conductivity,
            zero.k.at[pl.ds(4, BLOCK_X), pl.ds(PAD + 4, BLOCK_Y), :],
            local_sem.at[0],
        ),
        pltpu.make_async_copy(
            head, zero.va.at[pl.ds(4, BLOCK_X), pl.ds(PAD + 4, BLOCK_Y), :], local_sem.at[1]
        ),
        pltpu.make_async_copy(
            recharge, zero.g.at[pl.ds(3, BLOCK_X), pl.ds(4, BLOCK_Y), :], local_sem.at[2]
        ),
    ]
    for copy in local:
        copy.start()

    greeted = 0
    for dx, dy, _, _ in partners(SPLIT[2], 6):
        greet(dx, dy)
        greeted += 1

    def greet_y(k, carry):
        greet(0, k)
        return carry

    def greet_x(k, carry):
        greet(k, 0)
        return carry

    if gy_size > 5:
        lax.fori_loop(3, gy_size - 2, greet_y, 0)
        greeted += gy_size - 5
    if gx_size > 3:
        lax.fori_loop(2, gx_size - 1, greet_x, 0)
        greeted += gx_size - 3

    for ref in whole:
        ref.clear_edges()
    pl.semaphore_wait(barrier, greeted)

    def push(src, dst, stage, dx, dy):
        pltpu.make_async_remote_copy(
            src_ref=src,
            dst_ref=dst,
            send_sem=send_sem.at[stage],
            recv_sem=recv_sem.at[stage],
            device_id=device(dx, dy),
            device_id_type=pl.DeviceIdType.MESH,
        ).start()

    def exchange(level, halo, stage, src, src_x, src_row, dst, dst_x, dst_row):
        for dx, dy, xs, ys in partners(level, halo):
            push(
                src.at[pl.ds(src_x + xs[0], xs[1]), pl.ds(src_row + ys[0], ys[1]), :],
                dst.at[pl.ds(dst_x + xs[2], xs[1]), pl.ds(dst_row + ys[2], ys[1]), :],
                stage,
                dx,
                dy,
            )

    def arrived(stage, rows):
        block = tally.at[pl.ds(0, rows), :]
        pltpu.make_async_copy(block, block, recv_sem.at[stage]).wait()

    def sent(stage, rows):
        block = tally.at[pl.ds(0, rows), :]
        pltpu.make_async_copy(block, block, send_sem.at[stage]).wait()

    def gather_y(strip, stage):
        def step(k, carry):
            push(strip.at[pl.ds(gy, 1), :], strip.at[pl.ds(gy, 1), :], stage, 0, k)
            return carry

        lax.fori_loop(1, gy_size, step, 0)

    def gather_x(strip, place, stage):
        def step(k, carry):
            push(strip, place, stage, k, 0)
            return carry

        lax.fori_loop(1, gx_size, step, 0)

    lv0, lv1, lv2 = SPLIT
    exchange(lv0, lv0.hk, 0, conductivity, 0, 0, zero.k, 4, PAD + 4)
    exchange(lv0, 4, 1, head, 0, 0, zero.va, 4, PAD + 4)
    exchange(lv0, lv0.hg, 2, recharge, 0, 0, zero.g, 3, 4)

    def pack_3(rows):
        lane, row = iota((8, LANES), 1), iota((8, LANES), 0)
        picked = lane_gather(rows[...], (lane & 15) * 8)
        return jnp.sum(jnp.where((lane >> 4) == row, picked, 0.0), axis=0, keepdims=True)

    def to_rows(value, ref):
        for x in range(4):
            ref[pl.ds(2 * x, 2), :] = value[x]

    local[0].wait()
    own0 = (pl.ds(4, BLOCK_X), pl.ds(PAD + 4, BLOCK_Y))
    own1, own2 = (pl.ds(5, 16), pl.ds(PAD + 4, 8)), (pl.ds(6, 8), pl.ds(PAD + 6, 4))
    one.k[own1] = restrict(zero.k[own0], half0, 1, 0.125)
    two.k[own2] = restrict(one.k[own1], half1, 2, 0.125)
    to_rows(restrict(two.k[own2], half2, 4, 0.125), rows_k)
    strip_k[pl.ds(gy, 1), :] = pack_3(rows_k)
    exchange(lv1, lv1.hk, 3, one.k, 5, PAD + 4, one.k, 5, PAD + 4)
    gather_y(strip_k, 7)
    exchange(lv2, lv2.hk, 5, two.k, 6, PAD + 6, two.k, 6, PAD + 6)

    arrived(0, exchange_rows(lv0, lv0.hk))
    zero.faces()
    arrived(7, gy_size - 1)
    inner = pl.ds(PAD, gy_size)
    three.k[pl.ds(gx + 1, 1), inner, :] = strip_k[...].reshape(1, gy_size, LANES)
    gather_x(strip_k, three.k.at[gx + 1, inner, :], 8)
    local[1].wait()
    local[2].wait()
    arrived(1, exchange_rows(lv0, 4))
    arrived(2, exchange_rows(lv0, lv0.hg))
    zero.sweep(zero.va, zero.vb, 3)
    zero.sweep(zero.vb, zero.va, 2)
    one.g[pl.ds(4, 16), pl.ds(4, 8), :] = restrict(zero.residual(zero.va), half0, 1, 0.5)

    exchange(lv1, lv1.hg, 4, one.g, 4, 4, one.g, 4, 4)
    arrived(3, exchange_rows(lv1, lv1.hk))
    one.faces()
    arrived(4, exchange_rows(lv1, lv1.hg))
    one.first_sweep(one.va)
    one.sweep(one.va, one.vb, 3)
    two.g[pl.ds(5, 8), pl.ds(6, 4), :] = restrict(one.residual(one.vb), half1, 2, 0.5)

    exchange(lv2, lv2.hg, 6, two.g, 5, 6, two.g, 5, 6)
    arrived(5, exchange_rows(lv2, lv2.hk))
    two.faces()
    arrived(6, exchange_rows(lv2, lv2.hg))
    two.first_sweep(two.va)
    two.sweep(two.va, two.vb, 4)
    to_rows(restrict(two.residual(two.vb), half2, 4, 0.5), rows_g)
    strip_g[pl.ds(gy, 1), :] = pack_3(rows_g)

    gather_y(strip_g, 9)
    arrived(8, (gx_size - 1) * gy_size)
    three.faces()
    k4 = 0.125 * octet_3(three.inside(three.k)[...])
    four.inside(four.k)[...] = k4
    rest[...] = k4
    weight5, faces5 = faces_5(pack_5(rest, 1.0, 0.125, gx_size, gy_size), gx_size)
    four.faces()
    arrived(9, gy_size - 1)
    three.g[pl.ds(gx, 1)] = strip_g[...].reshape(1, gy_size, LANES)
    gather_x(strip_g, three.g.at[gx], 10)
    arrived(10, (gx_size - 1) * gy_size)

    three.first_sweep(three.va)
    three.sweep(three.va, three.vb)
    four.g[...] = 0.5 * octet_3(three.residual(three.vb))
    four.first_sweep(four.va)
    four.sweep(four.va, four.vb)
    rest[...] = four.residual(four.vb)
    v5 = solve_5(weight5, faces5, pack_5(rest, 0.0, 0.5, gx_size, gy_size))

    coarse5[pl.ds(0, gy_size // 2, stride=2), :] = v5
    coarse5[pl.ds(1, gy_size // 2, stride=2), :] = v5
    shape = (gx_size, gy_size, LANES)
    flat = (gx_size * gy_size, LANES)
    index = iota(shape, 0) * 4 + ((iota(shape, 2) & 15) >> 2)
    wide5 = jnp.broadcast_to(coarse5[...][None], shape).reshape(flat)
    four.correct(four.vb, lane_gather(wide5, index.reshape(flat)).reshape(shape))
    four.sweep(four.vb, four.va)
    four.sweep(four.va, four.vb)
    three.correct(three.vb, four.inside(four.vb)[...])
    three.sweep(three.vb, three.va)
    three.sweep(three.va, three.vb)

    row = iota((lv2.rows, LANES), 0)
    lane = iota((lv2.rows, LANES), 1)
    y3 = (row >> 1) - 1
    for dx in (-1, 0, 1):
        gxn = lax.rem(gx + (dx + gx_size), gx_size) + 1
        near = []
        for dy in (-1, 0, 1):
            gyn = lax.rem(gy + (dy + gy_size), gy_size) + PAD
            near.append(three.vb[pl.ds(gxn, 1), pl.ds(gyn, 1), :].reshape(1, LANES))
        rows = jnp.where(y3 < 2, near[0], jnp.where(y3 < 4, near[1], near[2]))
        for x in ((2, 3), (0, 1, 2, 3), (0, 1))[dx + 1]:
            copies = lane_gather(rows, (2 * x + (y3 & 1)) * 16 + (lane >> 3))
            for child in range(2):
                place = (2 * (4 * dx + x) + child + 6, pl.ds(PAD, lv2.rows))
                two.vb[place] = two.vb[place] + copies
    two.sweep(two.vb, two.va, 3)
    two.sweep(two.va, two.vb, 2)

    one.correct(one.vb, two.vb[pl.ds(4, 12), pl.ds(PAD + 4, 8), :], 1, 12, wide1)
    one.sweep(one.vb, one.va, 2)
    one.sweep(one.va, one.vb, 1)
    zero.correct(zero.va, one.vb[pl.ds(4, 18), pl.ds(PAD + 2, 12), :], 2, 18, wide0)
    zero.sweep(zero.va, zero.vb, 1)
    zero.last_sweep(zero.vb, out)

    sent(0, exchange_rows(lv0, lv0.hk))
    sent(1, exchange_rows(lv0, 4))
    sent(2, exchange_rows(lv0, lv0.hg))
    sent(3, exchange_rows(lv1, lv1.hk))
    sent(4, exchange_rows(lv1, lv1.hg))
    sent(5, exchange_rows(lv2, lv2.hk))
    sent(6, exchange_rows(lv2, lv2.hg))
    sent(7, gy_size - 1)
    sent(8, (gx_size - 1) * gy_size)
    sent(9, gy_size - 1)
    sent(10, (gx_size - 1) * gy_size)


def on_device(gx_size, gy_size, head, recharge, conductivity):
    scratch = []
    for level in SPLIT:
        scratch += Split.scratch(level)
    for _ in range(2):
        scratch += Whole.scratch(gx_size, gy_size)
    scratch += [
        pltpu.VMEM((16, 16, LANES), F32),
        pltpu.VMEM((8, 8, LANES), F32),
        pltpu.VMEM((4, 4, LANES), F32),
        pltpu.VMEM((18, 24, LANES), F32),
        pltpu.VMEM((12, 16, LANES), F32),
        pltpu.VMEM((8, LANES), F32),
        pltpu.VMEM((8, LANES), F32),
        pltpu.VMEM((gy_size, LANES), F32),
        pltpu.VMEM((gy_size, LANES), F32),
        pltpu.VMEM((gx_size, gy_size, LANES), F32),
        pltpu.VMEM((gy_size, LANES), F32),
        pltpu.VMEM((TALLY_ROWS, LANES), F32),
        pltpu.SemaphoreType.DMA((3,)),
        pltpu.SemaphoreType.DMA((11,)),
        pltpu.SemaphoreType.DMA((11,)),
    ]

    def body(*refs):
        kernel(gx_size, gy_size, *refs)

    return pl.pallas_call(
        body,
        out_shape=jax.ShapeDtypeStruct(head.shape, F32),
        in_specs=[pl.BlockSpec(memory_space=pl.ANY)] * 3,
        out_specs=pl.BlockSpec(memory_space=pltpu.VMEM),
        scratch_shapes=scratch,
        compiler_params=pltpu.CompilerParams(
            collective_id=0, has_side_effects=True, vmem_limit_bytes=62 * 1024 * 1024
        ),
        name="vcycle",
    )(head, recharge, conductivity)


def solution(mesh):
    gx_size, gy_size = mesh.shape["gx"], mesh.shape["gy"]

    def one_device(head, recharge, conductivity):
        return on_device(gx_size, gy_size, head, recharge, conductivity)

    spec = P("gx", "gy", None)
    return jax.shard_map(
        one_device, mesh=mesh, in_specs=(spec, spec, spec), out_specs=spec, check_vma=False
    )
```

```python
from typing import NamedTuple

import jax
import jax.numpy as jnp
from jax import lax
from jax.experimental import pallas as pl
from jax.experimental.pallas import tpu as pltpu
from jax.sharding import PartitionSpec as P

F32 = jnp.float32
LANES = 128
PAD = 8
OMEGA = 0.8
KEEP = 1.0 - OMEGA
COARSE_SWEEPS = 16
BLOCK_X = 32
BLOCK_Y = 16
TALLY_ROWS = 512

class Level(NamedTuple):
    bx: int
    by: int
    hx: int
    rows: int
    first: int
    span: int
    reach: int
    hk: int
    hg: int
    cyrows: int


SPLIT = (
    Level(32, 16, 3, 24, 4, 1, 1, 4, 3, 24),
    Level(16, 8, 4, 16, 4, 2, 1, 5, 4, 24),
    Level(8, 4, 5, 16, 6, 4, 2, 6, 5, 16),
)


def reciprocal(x):
    guess = pltpu.reciprocal(x, approx=True)
    return guess * (2.0 - x * guess)


def face(a, b):
    return (2.0 * a * b) * reciprocal(a + b)


def iota(shape, dim):
    return lax.broadcasted_iota(jnp.int32, shape, dim)


def flag(condition):
    return jnp.where(condition, 1.0, 0.0).astype(F32)


def up(value, shift):
    return pltpu.roll(value, LANES - shift, value.ndim - 1)


def down(value, shift):
    return pltpu.roll(value, shift, value.ndim - 1)


def swap(value, bit):
    if 2 * bit == LANES:
        return down(value, bit)
    flat = value.reshape(-1, LANES)
    return lane_gather(flat, iota(flat.shape, 1) ^ bit).reshape(value.shape)


def lane_gather(value, index):
    return jnp.take_along_axis(value, index, axis=1)


def segment(step, block, halo):
    low = max(0, step * block - halo)
    high = min(block, (step + 1) * block + halo)
    return low, high - low, low - step * block


def partners(level, halo):
    found = []
    for dx in (-1, 0, 1):
        for dy in range(-level.reach, level.reach + 1):
            if (dx, dy) != (0, 0):
                near = halo - 1 if dx and dy and level.span == 1 else halo
                found.append((dx, dy, segment(dx, level.bx, near), segment(dy, level.by, near)))
    return sorted(found, key=lambda p: -abs(p[0]) - abs(p[1]))


def exchange_rows(level, halo):
    return sum(xs[1] * ys[1] for _, _, xs, ys in partners(level, halo))


class Split:
    def __init__(self, level, nx, ny, gx, gy, refs):
        self.at = level
        self.nx, self.ny, self.gx, self.gy = nx, ny, gx, gy
        (self.k, self.va, self.vb, self.g, self.cx, self.cy, self.czl, self.czh, self.w, self.d) = refs

    @staticmethod
    def scratch(level):
        x, rows = level.bx + 2 * level.hx, level.rows
        padded = pltpu.VMEM((x + 2, rows + 2 * PAD, LANES), F32)
        plain = pltpu.VMEM((x, rows, LANES), F32)
        return [
            padded,
            padded,
            padded,
            plain,
            pltpu.VMEM((x + 1, rows, LANES), F32),
            pltpu.VMEM((x, rows + PAD, LANES), F32),
            plain,
            plain,
            plain,
            plain,
        ]

    def faces(self):
        lv = self.at
        count, rows, span = lv.bx + 2 * lv.hx, lv.rows, lv.span
        y = self.gy * lv.by + iota((1, lv.cyrows, LANES), 1) - lv.first
        y_open = flag((y != 0) & (y != self.ny))
        y = y[:, :rows]
        lane = iota((1, rows, LANES), 2)
        z_open = flag(lane >= span)
        cuts = flag((y == 0) | (y == self.ny)) + flag((y == -1) | (y == self.ny - 1))
        cuts = cuts + flag(lane < span) + flag(lane >= LANES - span)
        inner = pl.ds(PAD, rows)
        all_x = pl.ds(1, count)
        here = self.k[all_x, inner, :]
        self.cx[...] = face(
            self.k[pl.ds(0, count + 1), inner, :], self.k[pl.ds(1, count + 1), inner, :]
        )
        cut_low, cut_high = flag(self.gx == 0), flag(self.gx * lv.bx + lv.bx == self.nx)
        for i, cut in ((lv.hx, cut_low), (lv.hx + lv.bx, cut_high)):
            self.cx[i] = self.cx[i] * (1.0 - cut)
        self.cy[:, pl.ds(0, lv.cyrows), :] = y_open * face(
            self.k[all_x, pl.ds(PAD - 1, lv.cyrows), :], self.k[all_x, pl.ds(PAD, lv.cyrows), :]
        )
        low_z = face(down(here, span), here) * z_open
        high_z = up(low_z, span)
        self.czl[...] = low_z
        self.czh[...] = high_z
        total = self.cx[pl.ds(0, count)] + self.cx[pl.ds(1, count)]
        total = total + (self.cy[:, pl.ds(0, rows), :] + self.cy[:, pl.ds(1, rows), :])
        self.d[...] = (total + (low_z + high_z)) + here * cuts
        for i, cut in ((lv.hx, cut_low), (lv.hx + lv.bx - 1, cut_high)):
            self.d[i] = self.d[i] + self.k[i + 1, inner, :] * cut
        self.w[...] = OMEGA * reciprocal(self.d[...])

    def beside(self, v, low, count, row, rows):
        span = self.at.span
        inner, own = pl.ds(PAD + row, rows), pl.ds(row, rows)
        x, mid = pl.ds(low, count), pl.ds(low + 1, count)
        here = v[mid, inner, :]
        along_x = self.cx[x, own, :] * v[x, inner, :] + self.cx[mid, own, :] * v[pl.ds(low + 2, count), inner, :]
        along_y = (
            self.cy[x, own, :] * v[mid, pl.ds(PAD + row - 1, rows), :]
            + self.cy[x, pl.ds(row + 1, rows), :] * v[mid, pl.ds(PAD + row + 1, rows), :]
        )
        along_z = self.czl[x, own, :] * down(here, span) + self.czh[x, own, :] * up(here, span)
        return here, (along_x + along_y) + along_z

    def first_sweep(self, dst):
        dst[pl.ds(1, self.at.bx + 2 * self.at.hx), pl.ds(PAD, self.at.rows), :] = self.w[...] * self.g[...]

    def sweep(self, src, dst, halo):
        lv = self.at
        low, count = lv.hx - halo, lv.bx + 2 * halo
        here, total = self.beside(src, low, count, 0, lv.rows)
        x = pl.ds(low, count)
        dst[pl.ds(low + 1, count), pl.ds(PAD, lv.rows), :] = KEEP * here + self.w[x] * (self.g[x] + total)

    def last_sweep(self, src, out):
        lv = self.at
        x, own = pl.ds(lv.hx, lv.bx), pl.ds(lv.first, lv.by)
        here, total = self.beside(src, lv.hx, lv.bx, lv.first, lv.by)
        out[...] = KEEP * here + self.w[x, own, :] * (self.g[x, own, :] + total)

    def residual(self, v):
        lv = self.at
        x, own = pl.ds(lv.hx, lv.bx), pl.ds(lv.first, lv.by)
        here, total = self.beside(v, lv.hx, lv.bx, lv.first, lv.by)
        return self.g[x, own, :] + total - self.d[x, own, :] * here

    def correct(self, v, coarse, x0, count, wide):
        rows = self.at.rows
        half = rows // 2
        wide[:, pl.ds(0, half, stride=2), :] = coarse
        wide[:, pl.ds(1, half, stride=2), :] = coarse
        place = (pl.ds(x0, 2 * count), pl.ds(PAD, rows))
        copies = jnp.broadcast_to(wide[...][:, None], (count, 2, rows, LANES))
        v[place] = v[place] + copies.reshape(2 * count, rows, LANES)


def restrict(value, half, span, scale):
    x, y, _ = value.shape
    value = value.reshape(x // 2, 2, y, LANES)
    half[...] = value[:, 0] + value[:, 1]
    total = half[:, pl.ds(0, y // 2, stride=2), :] + half[:, pl.ds(1, y // 2, stride=2), :]
    return scale * (total + swap(total, span))


class Whole:
    def __init__(self, number, nx, ny, refs):
        self.number, self.nx, self.ny = number, nx, ny
        self.k, self.va, self.vb, self.g, self.c, self.w, self.d = refs

    @staticmethod
    def scratch(nx, ny):
        padded = pltpu.VMEM((nx + 2, ny + 2 * PAD, LANES), F32)
        plain = pltpu.VMEM((nx, ny, LANES), F32)
        return [padded, padded, padded, plain, pltpu.VMEM((6, nx, ny, LANES), F32), plain, plain]

    def clear_edges(self):
        for ref in (self.k, self.va, self.vb):
            for x in (0, self.nx + 1):
                ref[x] = jnp.zeros((self.ny + 2 * PAD, LANES), F32)
            for row in (0, PAD + self.ny):
                ref[:, pl.ds(row, PAD), :] = jnp.zeros((self.nx + 2, PAD, LANES), F32)

    def inside(self, ref):
        return ref.at[pl.ds(1, self.nx), pl.ds(PAD, self.ny), :]

    def neighbours(self, v):
        inner, all_x = pl.ds(PAD, self.ny), pl.ds(1, self.nx)
        here = v[all_x, inner, :]
        before = v[pl.ds(0, self.nx), inner, :]
        after = v[pl.ds(2, self.nx), inner, :]
        under = v[all_x, pl.ds(PAD - 1, self.ny), :]
        over = v[all_x, pl.ds(PAD + 1, self.ny), :]
        lane = iota((1, self.ny, LANES), 2)
        if self.number == 3:
            before = down(jnp.where(lane >= 96, before, here), 32)
            after = up(jnp.where(lane < 32, after, here), 32)
            odd = (lane & 16) != 0
            under = swap(jnp.where(odd, under, here), 16)
            over = swap(jnp.where(odd, here, over), 16)
            span = 1
        else:
            before = down(jnp.where(lane >= 64, before, here), 64)
            after = up(jnp.where(lane < 64, after, here), 64)
            span = 2
        return (before, after, under, over, down(here, span), up(here, span)), here

    def faces(self):
        shape = (self.nx, self.ny, LANES)
        lane, row, x = iota(shape, 2), iota(shape, 1), iota(shape, 0)
        z = lane & 15
        if self.number == 3:
            first_x, last_x, first_y, last_y = lane < 32, lane >= 96, (lane & 16) == 0, (lane & 16) != 0
            first_z, last_z = z == 0, z == 15
            first_y, last_y = (row == 0) & first_y, (row == self.ny - 1) & last_y
        else:
            first_x, last_x, first_y, last_y = lane < 64, lane >= 64, row == 0, row == self.ny - 1
            first_z, last_z = z < 2, z >= 14
        first_x, last_x = (x == 0) & first_x, (x == self.nx - 1) & last_x
        sides, here = self.neighbours(self.k)
        total = jnp.zeros(shape, F32)
        for n, cut in enumerate((first_x, last_x, first_y, last_y, first_z, last_z)):
            value = face(here, sides[n])
            self.c[n] = jnp.where(cut, 0.0, value)
            total = total + jnp.where(cut, here, value)
        self.d[...] = total
        self.w[...] = OMEGA * reciprocal(total)

    def beside(self, v):
        sides, here = self.neighbours(v)
        parts = [self.c[n] * sides[n] for n in range(6)]
        return here, (parts[0] + parts[1]) + (parts[2] + parts[3]) + (parts[4] + parts[5])

    def first_sweep(self, dst):
        self.inside(dst)[...] = self.w[...] * self.g[...]

    def sweep(self, src, dst):
        here, total = self.beside(src)
        self.inside(dst)[...] = KEEP * here + self.w[...] * (self.g[...] + total)

    def residual(self, v):
        here, total = self.beside(v)
        return self.g[...] + total - self.d[...] * here

    def correct(self, v, values):
        place = self.inside(v)
        place[...] = place[...] + values


def octet_3(value):
    value = value + swap(value, 1)
    value = value + swap(value, 16)
    return value + swap(value, 32)


def pack_5(ref, fill, scale, nx, ny):
    half = ny // 2
    shape = (nx, half, LANES)
    rows = ref[:, pl.ds(0, half, stride=2), :] + ref[:, pl.ds(1, half, stride=2), :]
    rows = rows + swap(rows, 2)
    rows = scale * (rows + swap(rows, 64))
    index = (iota((nx * half, LANES), 1) & 3) * 4
    rows = lane_gather(rows.reshape(nx * half, LANES), index).reshape(shape)
    packed = jnp.sum(jnp.where((iota(shape, 2) >> 2) == iota(shape, 0), rows, 0.0), axis=0)
    return packed + jnp.where(iota((half, LANES), 1) >= 4 * nx, fill, 0.0)


def faces_5(k, nx):
    shape = k.shape
    lane, row = iota(shape, 1), iota(shape, 0)
    x, z = lane >> 2, lane & 3
    cuts = (x == 0, x == nx - 1, row == 0, row == shape[0] - 1, z == 0, z == 3)
    total = jnp.zeros(shape, F32)
    faces = []
    for cut, beyond in zip(cuts, sides_5(k)):
        value = face(k, beyond)
        faces.append(jnp.where(cut, 0.0, value))
        total = total + jnp.where(cut, k, value)
    weight = OMEGA * reciprocal(total)
    return weight, [weight * value for value in faces]


def sides_5(v):
    rows = v.shape[0]
    return (down(v, 4), up(v, 4), pltpu.roll(v, 1, 0), pltpu.roll(v, rows - 1, 0), down(v, 1), up(v, 1))


def solve_5(weight, faces, g):
    start = weight * g

    v = start
    for _ in range(COARSE_SWEEPS - 1):
        parts = [c * beyond for c, beyond in zip(faces, sides_5(v))]
        v = (KEEP * v + start) + ((parts[0] + parts[1]) + (parts[2] + parts[3]) + (parts[4] + parts[5]))
    return v


N_SPLIT = 10
N_WHOLE = 7


def kernel(gx_size, gy_size, head, recharge, conductivity, out, *refs):
    refs = list(refs)
    gx, gy = lax.axis_index("gx"), lax.axis_index("gy")
    split = []
    for number, level in enumerate(SPLIT):
        nx, ny = gx_size * level.bx, gy_size * level.by
        split.append(Split(level, nx, ny, gx, gy, refs[:N_SPLIT]))
        del refs[:N_SPLIT]
    whole = []
    for number in (3, 4):
        whole.append(Whole(number, gx_size, gy_size, refs[:N_WHOLE]))
        del refs[:N_WHOLE]
    (
        half0,
        half1,
        half2,
        wide0,
        wide1,
        rows_k,
        rows_g,
        strip_k,
        strip_g,
        rest,
        coarse5,
        tally,
        local_sem,
        send_sem,
        recv_sem,
    ) = refs
    zero, one, two = split
    three, four = whole

    def device(dx, dy):
        return {
            "gx": lax.rem(gx + (dx + gx_size), gx_size),
            "gy": lax.rem(gy + (dy + gy_size), gy_size),
        }

    barrier = pltpu.get_barrier_semaphore()

    def greet(dx, dy):
        pl.semaphore_signal(
            barrier, inc=1, device_id=device(dx, dy), device_id_type=pl.DeviceIdType.MESH
        )

    greeted = 0
    for dx, dy, _, _ in partners(SPLIT[2], 6):
        greet(dx, dy)
        greeted += 1
    for k in range(3, gy_size - 2):
        greet(0, k)
        greeted += 1
    for k in range(2, gx_size - 1):
        greet(k, 0)
        greeted += 1

    local = [
        pltpu.make_async_copy(
            conductivity,
            zero.k.at[pl.ds(4, BLOCK_X), pl.ds(PAD + 4, BLOCK_Y), :],
            local_sem.at[0],
        ),
        pltpu.make_async_copy(
            head, zero.va.at[pl.ds(4, BLOCK_X), pl.ds(PAD + 4, BLOCK_Y), :], local_sem.at[1]
        ),
        pltpu.make_async_copy(
            recharge, zero.g.at[pl.ds(3, BLOCK_X), pl.ds(4, BLOCK_Y), :], local_sem.at[2]
        ),
    ]
    for copy in local:
        copy.start()

    for ref in whole:
        ref.clear_edges()
    pl.semaphore_wait(barrier, greeted)

    def push(src, dst, stage, dx, dy):
        pltpu.make_async_remote_copy(
            src_ref=src,
            dst_ref=dst,
            send_sem=send_sem.at[stage],
            recv_sem=recv_sem.at[stage],
            device_id=device(dx, dy),
            device_id_type=pl.DeviceIdType.MESH,
        ).start()

    def exchange(level, halo, stage, src, src_x, src_row, dst, dst_x, dst_row):
        for dx, dy, xs, ys in partners(level, halo):
            push(
                src.at[pl.ds(src_x + xs[0], xs[1]), pl.ds(src_row + ys[0], ys[1]), :],
                dst.at[pl.ds(dst_x + xs[2], xs[1]), pl.ds(dst_row + ys[2], ys[1]), :],
                stage,
                dx,
                dy,
            )

    def arrived(stage, rows):
        block = tally.at[pl.ds(0, rows), :]
        pltpu.make_async_copy(block, block, recv_sem.at[stage]).wait()

    def sent(stage, rows):
        block = tally.at[pl.ds(0, rows), :]
        pltpu.make_async_copy(block, block, send_sem.at[stage]).wait()

    def far_first(count):
        return sorted(range(1, count), key=lambda k: -min(k, count - k))

    def gather_y(strip, stage):
        for k in far_first(gy_size):
            push(strip.at[pl.ds(gy, 1), :], strip.at[pl.ds(gy, 1), :], stage, 0, k)

    def gather_x(strip, place, stage):
        for k in far_first(gx_size):
            push(strip, place, stage, k, 0)

    lv0, lv1, lv2 = SPLIT
    exchange(lv0, lv0.hk, 0, conductivity, 0, 0, zero.k, 4, PAD + 4)
    exchange(lv0, 4, 1, head, 0, 0, zero.va, 4, PAD + 4)
    exchange(lv0, lv0.hg, 2, recharge, 0, 0, zero.g, 3, 4)

    def pack_3(rows):
        lane, row = iota((8, LANES), 1), iota((8, LANES), 0)
        picked = lane_gather(rows[...], (lane & 15) * 8)
        return jnp.sum(jnp.where((lane >> 4) == row, picked, 0.0), axis=0, keepdims=True)

    def to_rows(value, ref):
        for x in range(4):
            ref[pl.ds(2 * x, 2), :] = value[x]

    local[0].wait()
    own0 = (pl.ds(4, BLOCK_X), pl.ds(PAD + 4, BLOCK_Y))
    own1, own2 = (pl.ds(5, 16), pl.ds(PAD + 4, 8)), (pl.ds(6, 8), pl.ds(PAD + 6, 4))
    one.k[own1] = restrict(zero.k[own0], half0, 1, 0.125)
    two.k[own2] = restrict(one.k[own1], half1, 2, 0.125)
    to_rows(restrict(two.k[own2], half2, 4, 0.125), rows_k)
    strip_k[pl.ds(gy, 1), :] = pack_3(rows_k)
    exchange(lv1, lv1.hk, 3, one.k, 5, PAD + 4, one.k, 5, PAD + 4)
    gather_y(strip_k, 7)
    exchange(lv2, lv2.hk, 5, two.k, 6, PAD + 6, two.k, 6, PAD + 6)

    arrived(0, exchange_rows(lv0, lv0.hk))
    zero.faces()
    arrived(7, gy_size - 1)
    inner = pl.ds(PAD, gy_size)
    three.k[pl.ds(gx + 1, 1), inner, :] = strip_k[...].reshape(1, gy_size, LANES)
    gather_x(strip_k, three.k.at[gx + 1, inner, :], 8)
    local[1].wait()
    local[2].wait()
    arrived(1, exchange_rows(lv0, 4))
    arrived(2, exchange_rows(lv0, lv0.hg))
    zero.sweep(zero.va, zero.vb, 3)
    zero.sweep(zero.vb, zero.va, 2)
    one.g[pl.ds(4, 16), pl.ds(4, 8), :] = restrict(zero.residual(zero.va), half0, 1, 0.5)

    exchange(lv1, lv1.hg, 4, one.g, 4, 4, one.g, 4, 4)
    arrived(3, exchange_rows(lv1, lv1.hk))
    one.faces()
    arrived(4, exchange_rows(lv1, lv1.hg))
    one.first_sweep(one.va)
    one.sweep(one.va, one.vb, 3)
    two.g[pl.ds(5, 8), pl.ds(6, 4), :] = restrict(one.residual(one.vb), half1, 2, 0.5)

    exchange(lv2, lv2.hg, 6, two.g, 5, 6, two.g, 5, 6)
    arrived(5, exchange_rows(lv2, lv2.hk))
    two.faces()
    arrived(8, (gx_size - 1) * gy_size)
    three.faces()
    arrived(6, exchange_rows(lv2, lv2.hg))
    two.first_sweep(two.va)
    two.sweep(two.va, two.vb, 4)
    to_rows(restrict(two.residual(two.vb), half2, 4, 0.5), rows_g)
    strip_g[pl.ds(gy, 1), :] = pack_3(rows_g)

    gather_y(strip_g, 9)
    k4 = 0.125 * octet_3(three.inside(three.k)[...])
    four.inside(four.k)[...] = k4
    rest[...] = k4
    weight5, faces5 = faces_5(pack_5(rest, 1.0, 0.125, gx_size, gy_size), gx_size)
    arrived(9, gy_size - 1)
    three.g[pl.ds(gx, 1)] = strip_g[...].reshape(1, gy_size, LANES)
    gather_x(strip_g, three.g.at[gx], 10)
    four.faces()
    arrived(10, (gx_size - 1) * gy_size)

    three.first_sweep(three.va)
    three.sweep(three.va, three.vb)
    four.g[...] = 0.5 * octet_3(three.residual(three.vb))
    four.first_sweep(four.va)
    four.sweep(four.va, four.vb)
    rest[...] = four.residual(four.vb)
    v5 = solve_5(weight5, faces5, pack_5(rest, 0.0, 0.5, gx_size, gy_size))

    coarse5[pl.ds(0, gy_size // 2, stride=2), :] = v5
    coarse5[pl.ds(1, gy_size // 2, stride=2), :] = v5
    shape = (gx_size, gy_size, LANES)
    flat = (gx_size * gy_size, LANES)
    index = iota(shape, 0) * 4 + ((iota(shape, 2) & 15) >> 2)
    wide5 = jnp.broadcast_to(coarse5[...][None], shape).reshape(flat)
    four.correct(four.vb, lane_gather(wide5, index.reshape(flat)).reshape(shape))
    four.sweep(four.vb, four.va)
    four.sweep(four.va, four.vb)
    three.correct(three.vb, four.inside(four.vb)[...])
    three.sweep(three.vb, three.va)
    three.sweep(three.va, three.vb)

    row = iota((lv2.rows, LANES), 0)
    lane = iota((lv2.rows, LANES), 1)
    y3 = (row >> 1) - 1
    for dx in (-1, 0, 1):
        gxn = lax.rem(gx + (dx + gx_size), gx_size) + 1
        near = []
        for dy in (-1, 0, 1):
            gyn = lax.rem(gy + (dy + gy_size), gy_size) + PAD
            near.append(three.vb[pl.ds(gxn, 1), pl.ds(gyn, 1), :].reshape(1, LANES))
        rows = jnp.where(y3 < 2, near[0], jnp.where(y3 < 4, near[1], near[2]))
        for x in ((2, 3), (0, 1, 2, 3), (0, 1))[dx + 1]:
            copies = lane_gather(rows, (2 * x + (y3 & 1)) * 16 + (lane >> 3))
            for child in range(2):
                place = (2 * (4 * dx + x) + child + 6, pl.ds(PAD, lv2.rows))
                two.vb[place] = two.vb[place] + copies
    two.sweep(two.vb, two.va, 3)
    two.sweep(two.va, two.vb, 2)

    one.correct(one.vb, two.vb[pl.ds(4, 12), pl.ds(PAD + 4, 8), :], 1, 12, wide1)
    one.sweep(one.vb, one.va, 2)
    one.sweep(one.va, one.vb, 1)
    zero.correct(zero.va, one.vb[pl.ds(4, 18), pl.ds(PAD + 2, 12), :], 2, 18, wide0)
    zero.sweep(zero.va, zero.vb, 1)
    zero.last_sweep(zero.vb, out)

    sent(0, exchange_rows(lv0, lv0.hk))
    sent(1, exchange_rows(lv0, 4))
    sent(2, exchange_rows(lv0, lv0.hg))
    sent(3, exchange_rows(lv1, lv1.hk))
    sent(4, exchange_rows(lv1, lv1.hg))
    sent(5, exchange_rows(lv2, lv2.hk))
    sent(6, exchange_rows(lv2, lv2.hg))
    sent(7, gy_size - 1)
    sent(8, (gx_size - 1) * gy_size)
    sent(9, gy_size - 1)
    sent(10, (gx_size - 1) * gy_size)


def on_device(gx_size, gy_size, head, recharge, conductivity):
    scratch = []
    for level in SPLIT:
        scratch += Split.scratch(level)
    for _ in range(2):
        scratch += Whole.scratch(gx_size, gy_size)
    scratch += [
        pltpu.VMEM((16, 16, LANES), F32),
        pltpu.VMEM((8, 8, LANES), F32),
        pltpu.VMEM((4, 4, LANES), F32),
        pltpu.VMEM((18, 24, LANES), F32),
        pltpu.VMEM((12, 16, LANES), F32),
        pltpu.VMEM((8, LANES), F32),
        pltpu.VMEM((8, LANES), F32),
        pltpu.VMEM((gy_size, LANES), F32),
        pltpu.VMEM((gy_size, LANES), F32),
        pltpu.VMEM((gx_size, gy_size, LANES), F32),
        pltpu.VMEM((gy_size, LANES), F32),
        pltpu.VMEM((TALLY_ROWS, LANES), F32),
        pltpu.SemaphoreType.DMA((3,)),
        pltpu.SemaphoreType.DMA((11,)),
        pltpu.SemaphoreType.DMA((11,)),
    ]

    def body(*refs):
        kernel(gx_size, gy_size, *refs)

    return pl.pallas_call(
        body,
        out_shape=jax.ShapeDtypeStruct(head.shape, F32),
        in_specs=[pl.BlockSpec(memory_space=pl.ANY)] * 3,
        out_specs=pl.BlockSpec(memory_space=pltpu.VMEM),
        scratch_shapes=scratch,
        compiler_params=pltpu.CompilerParams(
            collective_id=0, has_side_effects=True, vmem_limit_bytes=62 * 1024 * 1024
        ),
        name="vcycle",
    )(head, recharge, conductivity)


def solution(mesh):
    gx_size, gy_size = mesh.shape["gx"], mesh.shape["gy"]

    def one_device(head, recharge, conductivity):
        return on_device(gx_size, gy_size, head, recharge, conductivity)

    spec = P("gx", "gy", None)
    return jax.shard_map(
        one_device, mesh=mesh, in_specs=(spec, spec, spec), out_specs=spec, check_vma=False
    )
```

```python
from typing import NamedTuple

import jax
import jax.numpy as jnp
from jax import lax
from jax.experimental import pallas as pl
from jax.experimental.pallas import tpu as pltpu
from jax.sharding import PartitionSpec as P

F32 = jnp.float32
LANES = 128
PAD = 8
OMEGA = 0.8
KEEP = 1.0 - OMEGA
COARSE_SWEEPS = 16
BLOCK_X = 32
BLOCK_Y = 16
TALLY_ROWS = 512

class Level(NamedTuple):
    bx: int
    by: int
    hx: int
    rows: int
    first: int
    span: int
    reach: int
    hk: int
    hg: int
    cyrows: int


SPLIT = (
    Level(32, 16, 3, 24, 4, 1, 1, 4, 3, 24),
    Level(16, 8, 6, 24, 8, 2, 1, 7, 6, 24),
    Level(8, 4, 5, 16, 6, 4, 2, 6, 5, 16),
)


def reciprocal(x):
    guess = pltpu.reciprocal(x, approx=True)
    return guess * (2.0 - x * guess)


def face(a, b):
    return (2.0 * a * b) * reciprocal(a + b)


def iota(shape, dim):
    return lax.broadcasted_iota(jnp.int32, shape, dim)


def flag(condition):
    return jnp.where(condition, 1.0, 0.0).astype(F32)


def up(value, shift):
    return pltpu.roll(value, LANES - shift, value.ndim - 1)


def down(value, shift):
    return pltpu.roll(value, shift, value.ndim - 1)


def swap(value, bit):
    if 2 * bit == LANES:
        return down(value, bit)
    flat = value.reshape(-1, LANES)
    return lane_gather(flat, iota(flat.shape, 1) ^ bit).reshape(value.shape)


def lane_gather(value, index):
    return jnp.take_along_axis(value, index, axis=1)


def segment(step, block, halo):
    low = max(0, step * block - halo)
    high = min(block, (step + 1) * block + halo)
    return low, high - low, low - step * block


def partners(level, halo):
    found = []
    for dx in (-1, 0, 1):
        for dy in range(-level.reach, level.reach + 1):
            if (dx, dy) != (0, 0):
                near = halo - 1 if dx and dy and level.span <= 2 else halo
                found.append((dx, dy, segment(dx, level.bx, near), segment(dy, level.by, near)))
    return sorted(found, key=lambda p: -abs(p[0]) - abs(p[1]))


def exchange_rows(level, halo):
    return sum(xs[1] * ys[1] for _, _, xs, ys in partners(level, halo))


class Split:
    def __init__(self, level, nx, ny, gx, gy, refs):
        self.at = level
        self.nx, self.ny, self.gx, self.gy = nx, ny, gx, gy
        (self.k, self.va, self.vb, self.g, self.cx, self.cy, self.czl, self.czh, self.w, self.d) = refs

    @staticmethod
    def scratch(level):
        x, rows = level.bx + 2 * level.hx, level.rows
        padded = pltpu.VMEM((x + 2, rows + 2 * PAD, LANES), F32)
        plain = pltpu.VMEM((x, rows, LANES), F32)
        return [
            padded,
            padded,
            padded,
            plain,
            pltpu.VMEM((x + 1, rows, LANES), F32),
            pltpu.VMEM((x, rows + PAD, LANES), F32),
            plain,
            plain,
            plain,
            plain,
        ]

    def faces(self):
        lv = self.at
        count, rows, span = lv.bx + 2 * lv.hx, lv.rows, lv.span
        y = self.gy * lv.by + iota((1, lv.cyrows, LANES), 1) - lv.first
        y_open = flag((y != 0) & (y != self.ny))
        y = y[:, :rows]
        lane = iota((1, rows, LANES), 2)
        z_open = flag(lane >= span)
        cuts = flag((y == 0) | (y == self.ny)) + flag((y == -1) | (y == self.ny - 1))
        cuts = cuts + flag(lane < span) + flag(lane >= LANES - span)
        inner = pl.ds(PAD, rows)
        all_x = pl.ds(1, count)
        here = self.k[all_x, inner, :]
        self.cx[...] = face(
            self.k[pl.ds(0, count + 1), inner, :], self.k[pl.ds(1, count + 1), inner, :]
        )
        cut_low, cut_high = flag(self.gx == 0), flag(self.gx * lv.bx + lv.bx == self.nx)
        for i, cut in ((lv.hx, cut_low), (lv.hx + lv.bx, cut_high)):
            self.cx[i] = self.cx[i] * (1.0 - cut)
        self.cy[:, pl.ds(0, lv.cyrows), :] = y_open * face(
            self.k[all_x, pl.ds(PAD - 1, lv.cyrows), :], self.k[all_x, pl.ds(PAD, lv.cyrows), :]
        )
        low_z = face(down(here, span), here) * z_open
        high_z = up(low_z, span)
        self.czl[...] = low_z
        self.czh[...] = high_z
        total = self.cx[pl.ds(0, count)] + self.cx[pl.ds(1, count)]
        total = total + (self.cy[:, pl.ds(0, rows), :] + self.cy[:, pl.ds(1, rows), :])
        self.d[...] = (total + (low_z + high_z)) + here * cuts
        for i, cut in ((lv.hx, cut_low), (lv.hx + lv.bx - 1, cut_high)):
            self.d[i] = self.d[i] + self.k[i + 1, inner, :] * cut
        self.w[...] = OMEGA * reciprocal(self.d[...])

    def beside(self, v, low, count, row, rows):
        span = self.at.span
        inner, own = pl.ds(PAD + row, rows), pl.ds(row, rows)
        x, mid = pl.ds(low, count), pl.ds(low + 1, count)
        here = v[mid, inner, :]
        along_x = self.cx[x, own, :] * v[x, inner, :] + self.cx[mid, own, :] * v[pl.ds(low + 2, count), inner, :]
        along_y = (
            self.cy[x, own, :] * v[mid, pl.ds(PAD + row - 1, rows), :]
            + self.cy[x, pl.ds(row + 1, rows), :] * v[mid, pl.ds(PAD + row + 1, rows), :]
        )
        along_z = self.czl[x, own, :] * down(here, span) + self.czh[x, own, :] * up(here, span)
        return here, (along_x + along_y) + along_z

    def first_sweep(self, dst, halo, g):
        low, count = self.at.hx - halo, self.at.bx + 2 * halo
        x = pl.ds(low, count)
        dst[pl.ds(low + 1, count), pl.ds(PAD, self.at.rows), :] = self.w[x] * g[x]

    def sweep(self, src, dst, halo, g):
        lv = self.at
        low, count = lv.hx - halo, lv.bx + 2 * halo
        here, total = self.beside(src, low, count, 0, lv.rows)
        x = pl.ds(low, count)
        dst[pl.ds(low + 1, count), pl.ds(PAD, lv.rows), :] = KEEP * here + self.w[x] * (g[x] + total)

    def last_sweep(self, src, out):
        lv = self.at
        x, own = pl.ds(lv.hx, lv.bx), pl.ds(lv.first, lv.by)
        here, total = self.beside(src, lv.hx, lv.bx, lv.first, lv.by)
        out[...] = KEEP * here + self.w[x, own, :] * (self.g[x, own, :] + total)

    def residual(self, v, halo):
        lv = self.at
        low, count = lv.hx - halo, lv.bx + 2 * halo
        row, rows = lv.first - halo, lv.by + 2 * halo
        x, own = pl.ds(low, count), pl.ds(row, rows)
        here, total = self.beside(v, low, count, row, rows)
        return self.g[x, own, :] + total - self.d[x, own, :] * here

    def correct(self, v, coarse, x0, count, wide):
        rows = self.at.rows
        half = rows // 2
        wide[:, pl.ds(0, half, stride=2), :] = coarse
        wide[:, pl.ds(1, half, stride=2), :] = coarse
        place = (pl.ds(x0, 2 * count), pl.ds(PAD, rows))
        copies = jnp.broadcast_to(wide[...][:, None], (count, 2, rows, LANES))
        v[place] = v[place] + copies.reshape(2 * count, rows, LANES)


def restrict(value, half, span, scale):
    x, y, _ = value.shape
    value = value.reshape(x // 2, 2, y, LANES)
    half[...] = value[:, 0] + value[:, 1]
    total = half[:, pl.ds(0, y // 2, stride=2), :] + half[:, pl.ds(1, y // 2, stride=2), :]
    return scale * (total + swap(total, span))


class Whole:
    def __init__(self, number, nx, ny, refs):
        self.number, self.nx, self.ny = number, nx, ny
        self.k, self.va, self.vb, self.g, self.c, self.w, self.d = refs

    @staticmethod
    def scratch(nx, ny):
        padded = pltpu.VMEM((nx + 2, ny + 2 * PAD, LANES), F32)
        plain = pltpu.VMEM((nx, ny, LANES), F32)
        return [padded, padded, padded, plain, pltpu.VMEM((6, nx, ny, LANES), F32), plain, plain]

    def clear_edges(self):
        for ref in (self.k, self.va, self.vb):
            for x in (0, self.nx + 1):
                ref[x] = jnp.zeros((self.ny + 2 * PAD, LANES), F32)
            for row in (0, PAD + self.ny):
                ref[:, pl.ds(row, PAD), :] = jnp.zeros((self.nx + 2, PAD, LANES), F32)

    def inside(self, ref):
        return ref.at[pl.ds(1, self.nx), pl.ds(PAD, self.ny), :]

    def neighbours(self, v):
        inner, all_x = pl.ds(PAD, self.ny), pl.ds(1, self.nx)
        here = v[all_x, inner, :]
        before = v[pl.ds(0, self.nx), inner, :]
        after = v[pl.ds(2, self.nx), inner, :]
        under = v[all_x, pl.ds(PAD - 1, self.ny), :]
        over = v[all_x, pl.ds(PAD + 1, self.ny), :]
        lane = iota((1, self.ny, LANES), 2)
        if self.number == 3:
            before = down(jnp.where(lane >= 96, before, here), 32)
            after = up(jnp.where(lane < 32, after, here), 32)
            odd = (lane & 16) != 0
            under = swap(jnp.where(odd, under, here), 16)
            over = swap(jnp.where(odd, here, over), 16)
            span = 1
        else:
            before = down(jnp.where(lane >= 64, before, here), 64)
            after = up(jnp.where(lane < 64, after, here), 64)
            span = 2
        return (before, after, under, over, down(here, span), up(here, span)), here

    def faces(self):
        shape = (self.nx, self.ny, LANES)
        lane, row, x = iota(shape, 2), iota(shape, 1), iota(shape, 0)
        z = lane & 15
        if self.number == 3:
            first_x, last_x, first_y, last_y = lane < 32, lane >= 96, (lane & 16) == 0, (lane & 16) != 0
            first_z, last_z = z == 0, z == 15
            first_y, last_y = (row == 0) & first_y, (row == self.ny - 1) & last_y
        else:
            first_x, last_x, first_y, last_y = lane < 64, lane >= 64, row == 0, row == self.ny - 1
            first_z, last_z = z < 2, z >= 14
        first_x, last_x = (x == 0) & first_x, (x == self.nx - 1) & last_x
        sides, here = self.neighbours(self.k)
        total = jnp.zeros(shape, F32)
        for n, cut in enumerate((first_x, last_x, first_y, last_y, first_z, last_z)):
            value = face(here, sides[n])
            self.c[n] = jnp.where(cut, 0.0, value)
            total = total + jnp.where(cut, here, value)
        self.d[...] = total
        self.w[...] = OMEGA * reciprocal(total)

    def beside(self, v):
        sides, here = self.neighbours(v)
        parts = [self.c[n] * sides[n] for n in range(6)]
        return here, (parts[0] + parts[1]) + (parts[2] + parts[3]) + (parts[4] + parts[5])

    def first_sweep(self, dst):
        self.inside(dst)[...] = self.w[...] * self.g[...]

    def sweep(self, src, dst):
        here, total = self.beside(src)
        self.inside(dst)[...] = KEEP * here + self.w[...] * (self.g[...] + total)

    def residual(self, v):
        here, total = self.beside(v)
        return self.g[...] + total - self.d[...] * here

    def correct(self, v, values):
        place = self.inside(v)
        place[...] = place[...] + values


def octet_3(value):
    value = value + swap(value, 1)
    value = value + swap(value, 16)
    return value + swap(value, 32)


def pack_5(ref, fill, scale, nx, ny):
    half = ny // 2
    shape = (nx, half, LANES)
    rows = ref[:, pl.ds(0, half, stride=2), :] + ref[:, pl.ds(1, half, stride=2), :]
    rows = rows + swap(rows, 2)
    rows = scale * (rows + swap(rows, 64))
    index = (iota((nx * half, LANES), 1) & 3) * 4
    rows = lane_gather(rows.reshape(nx * half, LANES), index).reshape(shape)
    packed = jnp.sum(jnp.where((iota(shape, 2) >> 2) == iota(shape, 0), rows, 0.0), axis=0)
    return packed + jnp.where(iota((half, LANES), 1) >= 4 * nx, fill, 0.0)


def faces_5(k, nx):
    shape = k.shape
    lane, row = iota(shape, 1), iota(shape, 0)
    x, z = lane >> 2, lane & 3
    cuts = (x == 0, x == nx - 1, row == 0, row == shape[0] - 1, z == 0, z == 3)
    total = jnp.zeros(shape, F32)
    faces = []
    for cut, beyond in zip(cuts, sides_5(k)):
        value = face(k, beyond)
        faces.append(jnp.where(cut, 0.0, value))
        total = total + jnp.where(cut, k, value)
    weight = OMEGA * reciprocal(total)
    return weight, [weight * value for value in faces]


def sides_5(v):
    rows = v.shape[0]
    return (down(v, 4), up(v, 4), pltpu.roll(v, 1, 0), pltpu.roll(v, rows - 1, 0), down(v, 1), up(v, 1))


def solve_5(weight, faces, g):
    start = weight * g

    v = start
    for _ in range(COARSE_SWEEPS - 1):
        parts = [c * beyond for c, beyond in zip(faces, sides_5(v))]
        v = (KEEP * v + start) + ((parts[0] + parts[1]) + (parts[2] + parts[3]) + (parts[4] + parts[5]))
    return v


N_SPLIT = 10
N_WHOLE = 7


def kernel(gx_size, gy_size, head, recharge, conductivity, out, *refs):
    refs = list(refs)
    gx, gy = lax.axis_index("gx"), lax.axis_index("gy")
    split = []
    for number, level in enumerate(SPLIT):
        nx, ny = gx_size * level.bx, gy_size * level.by
        split.append(Split(level, nx, ny, gx, gy, refs[:N_SPLIT]))
        del refs[:N_SPLIT]
    whole = []
    for number in (3, 4):
        whole.append(Whole(number, gx_size, gy_size, refs[:N_WHOLE]))
        del refs[:N_WHOLE]
    (
        half0,
        half1,
        half1_k,
        half2,
        wide_g,
        wide0,
        wide1,
        rows_k,
        rows_g,
        strip_k,
        strip_g,
        rest,
        coarse5,
        tally,
        local_sem,
        send_sem,
        recv_sem,
    ) = refs
    zero, one, two = split
    three, four = whole

    def device(dx, dy):
        return {
            "gx": lax.rem(gx + (dx + gx_size), gx_size),
            "gy": lax.rem(gy + (dy + gy_size), gy_size),
        }

    barrier = pltpu.get_barrier_semaphore()

    def greet(dx, dy):
        pl.semaphore_signal(
            barrier, inc=1, device_id=device(dx, dy), device_id_type=pl.DeviceIdType.MESH
        )

    greeted = 0
    for dx, dy, _, _ in partners(SPLIT[2], 6):
        greet(dx, dy)
        greeted += 1
    for k in range(3, gy_size - 2):
        greet(0, k)
        greeted += 1
    for k in range(2, gx_size - 1):
        greet(k, 0)
        greeted += 1

    local = [
        pltpu.make_async_copy(
            conductivity,
            zero.k.at[pl.ds(4, BLOCK_X), pl.ds(PAD + 4, BLOCK_Y), :],
            local_sem.at[0],
        ),
        pltpu.make_async_copy(
            head, zero.va.at[pl.ds(4, BLOCK_X), pl.ds(PAD + 4, BLOCK_Y), :], local_sem.at[1]
        ),
        pltpu.make_async_copy(
            recharge, zero.g.at[pl.ds(3, BLOCK_X), pl.ds(4, BLOCK_Y), :], local_sem.at[2]
        ),
    ]
    for copy in local:
        copy.start()

    for ref in whole:
        ref.clear_edges()
    pl.semaphore_wait(barrier, greeted)

    def push(src, dst, stage, dx, dy):
        pltpu.make_async_remote_copy(
            src_ref=src,
            dst_ref=dst,
            send_sem=send_sem.at[stage],
            recv_sem=recv_sem.at[stage],
            device_id=device(dx, dy),
            device_id_type=pl.DeviceIdType.MESH,
        ).start()

    def exchange(level, halo, stage, src, src_x, src_row, dst, dst_x, dst_row):
        for dx, dy, xs, ys in partners(level, halo):
            push(
                src.at[pl.ds(src_x + xs[0], xs[1]), pl.ds(src_row + ys[0], ys[1]), :],
                dst.at[pl.ds(dst_x + xs[2], xs[1]), pl.ds(dst_row + ys[2], ys[1]), :],
                stage,
                dx,
                dy,
            )

    def arrived(stage, rows):
        block = tally.at[pl.ds(0, rows), :]
        pltpu.make_async_copy(block, block, recv_sem.at[stage]).wait()

    def sent(stage, rows):
        block = tally.at[pl.ds(0, rows), :]
        pltpu.make_async_copy(block, block, send_sem.at[stage]).wait()

    def far_first(count):
        return sorted(range(1, count), key=lambda k: -min(k, count - k))

    def gather_y(strip, stage):
        for k in far_first(gy_size):
            push(strip.at[pl.ds(gy, 1), :], strip.at[pl.ds(gy, 1), :], stage, 0, k)

    def gather_x(strip, place, stage):
        for k in far_first(gx_size):
            push(strip, place, stage, k, 0)

    lv0, lv1, lv2 = SPLIT
    exchange(lv0, lv0.hk, 0, conductivity, 0, 0, zero.k, 4, PAD + 4)
    exchange(lv0, 4, 1, head, 0, 0, zero.va, 4, PAD + 4)
    exchange(lv0, lv0.hg, 2, recharge, 0, 0, zero.g, 3, 4)

    def pack_3(rows):
        lane, row = iota((8, LANES), 1), iota((8, LANES), 0)
        picked = lane_gather(rows[...], (lane & 15) * 8)
        return jnp.sum(jnp.where((lane >> 4) == row, picked, 0.0), axis=0, keepdims=True)

    def to_rows(value, ref):
        for x in range(4):
            ref[pl.ds(2 * x, 2), :] = value[x]

    local[0].wait()
    own0 = (pl.ds(4, BLOCK_X), pl.ds(PAD + 4, BLOCK_Y))
    own1, own2 = (pl.ds(7, 16), pl.ds(PAD + 8, 8)), (pl.ds(6, 8), pl.ds(PAD + 6, 4))
    one.k[own1] = restrict(zero.k[own0], half0, 1, 0.125)
    two.k[own2] = restrict(one.k[own1], half1_k, 2, 0.125)
    to_rows(restrict(two.k[own2], half2, 4, 0.125), rows_k)
    strip_k[pl.ds(gy, 1), :] = pack_3(rows_k)
    exchange(lv1, lv1.hk, 3, one.k, 7, PAD + 8, one.k, 7, PAD + 8)
    gather_y(strip_k, 7)
    exchange(lv2, lv2.hk, 5, two.k, 6, PAD + 6, two.k, 6, PAD + 6)

    arrived(0, exchange_rows(lv0, lv0.hk))
    zero.faces()
    arrived(7, gy_size - 1)
    inner = pl.ds(PAD, gy_size)
    three.k[pl.ds(gx + 1, 1), inner, :] = strip_k[...].reshape(1, gy_size, LANES)
    gather_x(strip_k, three.k.at[gx + 1, inner, :], 8)
    local[1].wait()
    local[2].wait()
    arrived(1, exchange_rows(lv0, 4))
    arrived(2, exchange_rows(lv0, lv0.hg))
    zero.sweep(zero.va, zero.vb, 3, zero.g)
    zero.sweep(zero.vb, zero.va, 2, zero.g)
    one.g[pl.ds(6, 16), pl.ds(8, 8), :] = restrict(zero.residual(zero.va, 0), half0, 1, 0.5)

    exchange(lv1, lv1.hg, 4, one.g, 6, 8, one.g, 6, 8)
    arrived(3, exchange_rows(lv1, lv1.hk))
    one.faces()
    arrived(5, exchange_rows(lv2, lv2.hk))
    two.faces()
    arrived(8, (gx_size - 1) * gy_size)
    three.faces()
    arrived(4, exchange_rows(lv1, lv1.hg))
    one.first_sweep(one.va, 6, one.g)
    one.sweep(one.va, one.vb, 5, one.g)
    two.g[pl.ds(3, 12), pl.ds(4, 8), :] = restrict(one.residual(one.vb, 4), half1, 2, 0.5)
    two.first_sweep(two.va, 2, two.g)
    two.sweep(two.va, two.vb, 1, two.g)
    to_rows(restrict(two.residual(two.vb, 0), half2, 4, 0.5), rows_g)
    strip_g[pl.ds(gy, 1), :] = pack_3(rows_g)

    gather_y(strip_g, 9)
    own_g = (pl.ds(5, 8), pl.ds(6, 4))
    wide_g[own_g] = two.g[own_g]
    exchange(lv2, lv2.hg, 6, wide_g, 5, 6, wide_g, 5, 6)
    k4 = 0.125 * octet_3(three.inside(three.k)[...])
    four.inside(four.k)[...] = k4
    rest[...] = k4
    weight5, faces5 = faces_5(pack_5(rest, 1.0, 0.125, gx_size, gy_size), gx_size)
    arrived(9, gy_size - 1)
    three.g[pl.ds(gx, 1)] = strip_g[...].reshape(1, gy_size, LANES)
    gather_x(strip_g, three.g.at[gx], 10)
    arrived(6, exchange_rows(lv2, lv2.hg))
    two.first_sweep(two.va, 5, wide_g)
    two.sweep(two.va, two.vb, 4, wide_g)
    four.faces()
    arrived(10, (gx_size - 1) * gy_size)

    three.first_sweep(three.va)
    three.sweep(three.va, three.vb)
    four.g[...] = 0.5 * octet_3(three.residual(three.vb))
    four.first_sweep(four.va)
    four.sweep(four.va, four.vb)
    rest[...] = four.residual(four.vb)
    v5 = solve_5(weight5, faces5, pack_5(rest, 0.0, 0.5, gx_size, gy_size))

    coarse5[pl.ds(0, gy_size // 2, stride=2), :] = v5
    coarse5[pl.ds(1, gy_size // 2, stride=2), :] = v5
    shape = (gx_size, gy_size, LANES)
    flat = (gx_size * gy_size, LANES)
    index = iota(shape, 0) * 4 + ((iota(shape, 2) & 15) >> 2)
    wide5 = jnp.broadcast_to(coarse5[...][None], shape).reshape(flat)
    four.correct(four.vb, lane_gather(wide5, index.reshape(flat)).reshape(shape))
    four.sweep(four.vb, four.va)
    four.sweep(four.va, four.vb)
    three.correct(three.vb, four.inside(four.vb)[...])
    three.sweep(three.vb, three.va)
    three.sweep(three.va, three.vb)

    row = iota((lv2.rows, LANES), 0)
    lane = iota((lv2.rows, LANES), 1)
    y3 = (row >> 1) - 1
    for dx in (-1, 0, 1):
        gxn = lax.rem(gx + (dx + gx_size), gx_size) + 1
        near = []
        for dy in (-1, 0, 1):
            gyn = lax.rem(gy + (dy + gy_size), gy_size) + PAD
            near.append(three.vb[pl.ds(gxn, 1), pl.ds(gyn, 1), :].reshape(1, LANES))
        rows = jnp.where(y3 < 2, near[0], jnp.where(y3 < 4, near[1], near[2]))
        for x in ((2, 3), (0, 1, 2, 3), (0, 1))[dx + 1]:
            copies = lane_gather(rows, (2 * x + (y3 & 1)) * 16 + (lane >> 3))
            for child in range(2):
                place = (2 * (4 * dx + x) + child + 6, pl.ds(PAD, lv2.rows))
                two.vb[place] = two.vb[place] + copies
    two.sweep(two.vb, two.va, 3, wide_g)
    two.sweep(two.va, two.vb, 2, wide_g)

    one.correct(one.vb, two.vb[pl.ds(4, 12), pl.ds(PAD + 2, 12), :], 3, 12, wide1)
    one.sweep(one.vb, one.va, 2, one.g)
    one.sweep(one.va, one.vb, 1, one.g)
    zero.correct(zero.va, one.vb[pl.ds(6, 18), pl.ds(PAD + 6, 12), :], 2, 18, wide0)
    zero.sweep(zero.va, zero.vb, 1, zero.g)
    zero.last_sweep(zero.vb, out)

    sent(0, exchange_rows(lv0, lv0.hk))
    sent(1, exchange_rows(lv0, 4))
    sent(2, exchange_rows(lv0, lv0.hg))
    sent(3, exchange_rows(lv1, lv1.hk))
    sent(4, exchange_rows(lv1, lv1.hg))
    sent(5, exchange_rows(lv2, lv2.hk))
    sent(6, exchange_rows(lv2, lv2.hg))
    sent(7, gy_size - 1)
    sent(8, (gx_size - 1) * gy_size)
    sent(9, gy_size - 1)
    sent(10, (gx_size - 1) * gy_size)


def on_device(gx_size, gy_size, head, recharge, conductivity):
    scratch = []
    for level in SPLIT:
        scratch += Split.scratch(level)
    for _ in range(2):
        scratch += Whole.scratch(gx_size, gy_size)
    scratch += [
        pltpu.VMEM((16, 16, LANES), F32),
        pltpu.VMEM((12, 16, LANES), F32),
        pltpu.VMEM((8, 8, LANES), F32),
        pltpu.VMEM((4, 4, LANES), F32),
        pltpu.VMEM((18, 16, LANES), F32),
        pltpu.VMEM((18, 24, LANES), F32),
        pltpu.VMEM((12, 24, LANES), F32),
        pltpu.VMEM((8, LANES), F32),
        pltpu.VMEM((8, LANES), F32),
        pltpu.VMEM((gy_size, LANES), F32),
        pltpu.VMEM((gy_size, LANES), F32),
        pltpu.VMEM((gx_size, gy_size, LANES), F32),
        pltpu.VMEM((gy_size, LANES), F32),
        pltpu.VMEM((TALLY_ROWS, LANES), F32),
        pltpu.SemaphoreType.DMA((3,)),
        pltpu.SemaphoreType.DMA((11,)),
        pltpu.SemaphoreType.DMA((11,)),
    ]

    def body(*refs):
        kernel(gx_size, gy_size, *refs)

    return pl.pallas_call(
        body,
        out_shape=jax.ShapeDtypeStruct(head.shape, F32),
        in_specs=[pl.BlockSpec(memory_space=pl.ANY)] * 3,
        out_specs=pl.BlockSpec(memory_space=pltpu.VMEM),
        scratch_shapes=scratch,
        compiler_params=pltpu.CompilerParams(
            collective_id=0, has_side_effects=True, vmem_limit_bytes=62 * 1024 * 1024
        ),
        name="vcycle",
    )(head, recharge, conductivity)


def solution(mesh):
    gx_size, gy_size = mesh.shape["gx"], mesh.shape["gy"]

    def one_device(head, recharge, conductivity):
        return on_device(gx_size, gy_size, head, recharge, conductivity)

    spec = P("gx", "gy", None)
    return jax.shard_map(
        one_device, mesh=mesh, in_specs=(spec, spec, spec), out_specs=spec, check_vma=False
    )
```

```python
from typing import NamedTuple

import jax
import jax.numpy as jnp
from jax import lax
from jax.experimental import pallas as pl
from jax.experimental.pallas import tpu as pltpu
from jax.sharding import PartitionSpec as P

F32 = jnp.float32
LANES = 128
PAD = 8
EDGE = 6
OMEGA = 0.8
KEEP = 1.0 - OMEGA
COARSE_SWEEPS = 16
BLOCK_X = 32
BLOCK_Y = 16
TALLY_ROWS = 512

class Level(NamedTuple):
    bx: int
    by: int
    hx: int
    rows: int
    first: int
    span: int
    reach: int
    hk: int
    hg: int
    cyrows: int


SPLIT = (
    Level(32, 16, 3, 24, 4, 1, 1, 4, 3, 24),
    Level(16, 8, 6, 24, 8, 2, 1, 7, 6, 24),
    Level(8, 4, 5, 16, 6, 4, 2, 6, 5, 16),
)


def reciprocal(x):
    guess = pltpu.reciprocal(x, approx=True)
    return guess * (2.0 - x * guess)


def face(a, b):
    return (2.0 * a * b) * reciprocal(a + b)


def iota(shape, dim):
    return lax.broadcasted_iota(jnp.int32, shape, dim)


def flag(condition):
    return jnp.where(condition, 1.0, 0.0).astype(F32)


def up(value, shift):
    return pltpu.roll(value, LANES - shift, value.ndim - 1)


def down(value, shift):
    return pltpu.roll(value, shift, value.ndim - 1)


def swap(value, bit):
    if 2 * bit == LANES:
        return down(value, bit)
    flat = value.reshape(-1, LANES)
    return lane_gather(flat, iota(flat.shape, 1) ^ bit).reshape(value.shape)


def lane_gather(value, index):
    return jnp.take_along_axis(value, index, axis=1)


def segment(step, block, halo):
    low = max(0, step * block - halo)
    high = min(block, (step + 1) * block + halo)
    return low, high - low, low - step * block


def partners(level, halo):
    found = []
    for dx in (-1, 0, 1):
        for dy in range(-level.reach, level.reach + 1):
            if (dx, dy) != (0, 0):
                near = halo - 1 if dx and dy and level.span <= 2 else halo
                found.append((dx, dy, segment(dx, level.bx, near), segment(dy, level.by, near)))
    return sorted(found, key=lambda p: -abs(p[0]) - abs(p[1]))


def exchange_rows(level, halo):
    return sum(xs[1] * ys[1] for _, _, xs, ys in partners(level, halo))


class Split:
    def __init__(self, level, nx, ny, gx, gy, refs):
        self.at = level
        self.nx, self.ny, self.gx, self.gy = nx, ny, gx, gy
        (self.k, self.va, self.vb, self.g, self.cx, self.cy, self.czl, self.czh, self.w, self.d) = refs

    @staticmethod
    def scratch(level):
        x, rows = level.bx + 2 * level.hx, level.rows
        padded = pltpu.VMEM((x + 2, rows + 2 * PAD, LANES), F32)
        plain = pltpu.VMEM((x, rows, LANES), F32)
        return [
            padded,
            padded,
            padded,
            plain,
            pltpu.VMEM((x + 1, rows, LANES), F32),
            pltpu.VMEM((x, rows + PAD, LANES), F32),
            plain,
            plain,
            plain,
            plain,
        ]

    def faces(self):
        lv = self.at
        count, rows, span = lv.bx + 2 * lv.hx, lv.rows, lv.span
        y = self.gy * lv.by + iota((1, lv.cyrows, LANES), 1) - lv.first
        y_open = flag((y != 0) & (y != self.ny))
        y = y[:, :rows]
        lane = iota((1, rows, LANES), 2)
        z_open = flag(lane >= span)
        cuts = flag((y == 0) | (y == self.ny)) + flag((y == -1) | (y == self.ny - 1))
        cuts = cuts + flag(lane < span) + flag(lane >= LANES - span)
        inner = pl.ds(PAD, rows)
        all_x = pl.ds(1, count)
        here = self.k[all_x, inner, :]
        self.cx[...] = face(
            self.k[pl.ds(0, count + 1), inner, :], self.k[pl.ds(1, count + 1), inner, :]
        )
        cut_low, cut_high = flag(self.gx == 0), flag(self.gx * lv.bx + lv.bx == self.nx)
        for i, cut in ((lv.hx, cut_low), (lv.hx + lv.bx, cut_high)):
            self.cx[i] = self.cx[i] * (1.0 - cut)
        self.cy[:, pl.ds(0, lv.cyrows), :] = y_open * face(
            self.k[all_x, pl.ds(PAD - 1, lv.cyrows), :], self.k[all_x, pl.ds(PAD, lv.cyrows), :]
        )
        low_z = face(down(here, span), here) * z_open
        high_z = up(low_z, span)
        self.czl[...] = low_z
        self.czh[...] = high_z
        total = self.cx[pl.ds(0, count)] + self.cx[pl.ds(1, count)]
        total = total + (self.cy[:, pl.ds(0, rows), :] + self.cy[:, pl.ds(1, rows), :])
        self.d[...] = (total + (low_z + high_z)) + here * cuts
        for i, cut in ((lv.hx, cut_low), (lv.hx + lv.bx - 1, cut_high)):
            self.d[i] = self.d[i] + self.k[i + 1, inner, :] * cut
        self.w[...] = OMEGA * reciprocal(self.d[...])

    def beside(self, v, low, count, row, rows):
        span = self.at.span
        inner, own = pl.ds(PAD + row, rows), pl.ds(row, rows)
        x, mid = pl.ds(low, count), pl.ds(low + 1, count)
        here = v[mid, inner, :]
        along_x = self.cx[x, own, :] * v[x, inner, :] + self.cx[mid, own, :] * v[pl.ds(low + 2, count), inner, :]
        along_y = (
            self.cy[x, own, :] * v[mid, pl.ds(PAD + row - 1, rows), :]
            + self.cy[x, pl.ds(row + 1, rows), :] * v[mid, pl.ds(PAD + row + 1, rows), :]
        )
        along_z = self.czl[x, own, :] * down(here, span) + self.czh[x, own, :] * up(here, span)
        return here, (along_x + along_y) + along_z

    def first_sweep(self, dst, halo, g):
        low, count = self.at.hx - halo, self.at.bx + 2 * halo
        x = pl.ds(low, count)
        dst[pl.ds(low + 1, count), pl.ds(PAD, self.at.rows), :] = self.w[x] * g[x]

    def sweep(self, src, dst, halo, g):
        lv = self.at
        low, count = lv.hx - halo, lv.bx + 2 * halo
        here, total = self.beside(src, low, count, 0, lv.rows)
        x = pl.ds(low, count)
        dst[pl.ds(low + 1, count), pl.ds(PAD, lv.rows), :] = KEEP * here + self.w[x] * (g[x] + total)

    def last_sweep(self, src, out):
        lv = self.at
        x, own = pl.ds(lv.hx, lv.bx), pl.ds(lv.first, lv.by)
        here, total = self.beside(src, lv.hx, lv.bx, lv.first, lv.by)
        out[...] = KEEP * here + self.w[x, own, :] * (self.g[x, own, :] + total)

    def residual(self, v, halo):
        lv = self.at
        low, count = lv.hx - halo, lv.bx + 2 * halo
        row, rows = lv.first - halo, lv.by + 2 * halo
        x, own = pl.ds(low, count), pl.ds(row, rows)
        here, total = self.beside(v, low, count, row, rows)
        return self.g[x, own, :] + total - self.d[x, own, :] * here

    def correct(self, v, coarse, x0, count, wide):
        rows = self.at.rows
        half = rows // 2
        wide[:, pl.ds(0, half, stride=2), :] = coarse
        wide[:, pl.ds(1, half, stride=2), :] = coarse
        place = (pl.ds(x0, 2 * count), pl.ds(PAD, rows))
        copies = jnp.broadcast_to(wide[...][:, None], (count, 2, rows, LANES))
        v[place] = v[place] + copies.reshape(2 * count, rows, LANES)


def restrict(value, half, span, scale):
    x, y, _ = value.shape
    value = value.reshape(x // 2, 2, y, LANES)
    half[...] = value[:, 0] + value[:, 1]
    total = half[:, pl.ds(0, y // 2, stride=2), :] + half[:, pl.ds(1, y // 2, stride=2), :]
    return scale * (total + swap(total, span))


class Whole:
    def __init__(self, number, nx, ny, refs):
        self.number, self.nx, self.ny = number, nx, ny
        self.k, self.va, self.vb, self.g, self.c, self.w, self.d = refs
        self.all = (EDGE, nx)

    @staticmethod
    def scratch(nx, ny):
        x = nx + 2 * EDGE
        padded = pltpu.VMEM((x, ny + 2 * PAD, LANES), F32)
        plain = pltpu.VMEM((x, ny, LANES), F32)
        return [padded, padded, padded, plain, pltpu.VMEM((6, x, ny, LANES), F32), plain, plain]

    def clear_edges(self):
        for x in (0, EDGE + self.nx):
            layers = pl.ds(x, EDGE)
            for ref in (self.k, self.va, self.vb, self.g, self.w):
                ref[layers] = jnp.zeros((EDGE,) + ref.shape[1:], F32)
            self.c[:, layers] = jnp.zeros((6, EDGE, self.ny, LANES), F32)
        for ref in (self.k, self.va, self.vb):
            for row in (0, PAD + self.ny):
                ref[pl.ds(EDGE, self.nx), pl.ds(row, PAD), :] = jnp.zeros((self.nx, PAD, LANES), F32)

    def inside(self, ref, layers=None):
        start, count = layers or self.all
        return ref.at[pl.ds(start, count), pl.ds(PAD, self.ny), :]

    def neighbours(self, v, layers):
        start, count = layers
        inner, mid = pl.ds(PAD, self.ny), pl.ds(start, count)
        here = v[mid, inner, :]
        before = v[pl.ds(start - 1, count), inner, :]
        after = v[pl.ds(start + 1, count), inner, :]
        under = v[mid, pl.ds(PAD - 1, self.ny), :]
        over = v[mid, pl.ds(PAD + 1, self.ny), :]
        lane = iota((1, self.ny, LANES), 2)
        if self.number == 3:
            before = down(jnp.where(lane >= 96, before, here), 32)
            after = up(jnp.where(lane < 32, after, here), 32)
            odd = (lane & 16) != 0
            under = swap(jnp.where(odd, under, here), 16)
            over = swap(jnp.where(odd, here, over), 16)
            span = 1
        else:
            before = down(jnp.where(lane >= 64, before, here), 64)
            after = up(jnp.where(lane < 64, after, here), 64)
            span = 2
        return (before, after, under, over, down(here, span), up(here, span)), here

    def faces(self):
        shape = (self.nx, self.ny, LANES)
        lane, row, x = iota(shape, 2), iota(shape, 1), iota(shape, 0)
        z = lane & 15
        if self.number == 3:
            first_x, last_x, first_y, last_y = lane < 32, lane >= 96, (lane & 16) == 0, (lane & 16) != 0
            first_z, last_z = z == 0, z == 15
            first_y, last_y = (row == 0) & first_y, (row == self.ny - 1) & last_y
        else:
            first_x, last_x, first_y, last_y = lane < 64, lane >= 64, row == 0, row == self.ny - 1
            first_z, last_z = z < 2, z >= 14
        first_x, last_x = (x == 0) & first_x, (x == self.nx - 1) & last_x
        sides, here = self.neighbours(self.k, self.all)
        inside = pl.ds(*self.all)
        total = jnp.zeros(shape, F32)
        for n, cut in enumerate((first_x, last_x, first_y, last_y, first_z, last_z)):
            value = face(here, sides[n])
            self.c[n, inside] = jnp.where(cut, 0.0, value)
            total = total + jnp.where(cut, here, value)
        self.d[inside] = total
        self.w[inside] = OMEGA * reciprocal(total)

    def beside(self, v, layers):
        sides, here = self.neighbours(v, layers)
        parts = [self.c[n, pl.ds(*layers)] * sides[n] for n in range(6)]
        return here, (parts[0] + parts[1]) + (parts[2] + parts[3]) + (parts[4] + parts[5])

    def first_sweep(self, dst):
        x = pl.ds(*self.all)
        self.inside(dst)[...] = self.w[x] * self.g[x]

    def sweep(self, src, dst, layers=None):
        layers = layers or self.all
        x = pl.ds(*layers)
        here, total = self.beside(src, layers)
        self.inside(dst, layers)[...] = KEEP * here + self.w[x] * (self.g[x] + total)

    def residual(self, v):
        x = pl.ds(*self.all)
        here, total = self.beside(v, self.all)
        return self.g[x] + total - self.d[x] * here

    def correct(self, v, layers, values):
        place = self.inside(v, layers)
        place[...] = place[...] + values


def octet_3(value):
    value = value + swap(value, 1)
    value = value + swap(value, 16)
    return value + swap(value, 32)


def pack_5(ref, fill, scale, nx, ny):
    half = ny // 2
    shape = (nx, half, LANES)
    rows = ref[:, pl.ds(0, half, stride=2), :] + ref[:, pl.ds(1, half, stride=2), :]
    rows = scale * rows.reshape(nx * half, LANES)
    index = (iota((nx * half, LANES), 1) & 3) * 4
    children = [lane_gather(rows, index + child) for child in (0, 2, 64, 66)]
    rows = ((children[0] + children[1]) + (children[2] + children[3])).reshape(shape)
    packed = jnp.sum(jnp.where((iota(shape, 2) >> 2) == iota(shape, 0), rows, 0.0), axis=0)
    return packed + jnp.where(iota((half, LANES), 1) >= 4 * nx, fill, 0.0)


def faces_5(k, nx):
    shape = k.shape
    lane, row = iota(shape, 1), iota(shape, 0)
    x, z = lane >> 2, lane & 3
    cuts = (x == 0, x == nx - 1, row == 0, row == shape[0] - 1, z == 0, z == 3)
    total = jnp.zeros(shape, F32)
    faces = []
    for cut, beyond in zip(cuts, sides_5(k)):
        value = face(k, beyond)
        faces.append(jnp.where(cut, 0.0, value))
        total = total + jnp.where(cut, k, value)
    weight = OMEGA * reciprocal(total)
    return weight, [weight * value for value in faces]


def sides_5(v):
    rows = v.shape[0]
    return (down(v, 4), up(v, 4), pltpu.roll(v, 1, 0), pltpu.roll(v, rows - 1, 0), down(v, 1), up(v, 1))


def solve_5(weight, faces, g):
    start = weight * g

    v = start
    for _ in range(COARSE_SWEEPS - 1):
        parts = [c * beyond for c, beyond in zip(faces, sides_5(v))]
        v = (KEEP * v + start) + ((parts[0] + parts[1]) + (parts[2] + parts[3]) + (parts[4] + parts[5]))
    return v


N_SPLIT = 10
N_WHOLE = 7


def kernel(gx_size, gy_size, head, recharge, conductivity, out, *refs):
    refs = list(refs)
    gx, gy = lax.axis_index("gx"), lax.axis_index("gy")
    split = []
    for number, level in enumerate(SPLIT):
        nx, ny = gx_size * level.bx, gy_size * level.by
        split.append(Split(level, nx, ny, gx, gy, refs[:N_SPLIT]))
        del refs[:N_SPLIT]
    whole = []
    for number in (3, 4):
        whole.append(Whole(number, gx_size, gy_size, refs[:N_WHOLE]))
        del refs[:N_WHOLE]
    (
        half0,
        half1,
        half1_k,
        half2,
        wide_g,
        wide0,
        wide1,
        rows_k,
        rows_g,
        strip_k,
        strip_g,
        rest,
        coarse5,
        tally,
        local_sem,
        send_sem,
        recv_sem,
    ) = refs
    zero, one, two = split
    three, four = whole

    def device(dx, dy):
        return {
            "gx": lax.rem(gx + (dx + gx_size), gx_size),
            "gy": lax.rem(gy + (dy + gy_size), gy_size),
        }

    barrier = pltpu.get_barrier_semaphore()

    def greet(dx, dy):
        pl.semaphore_signal(
            barrier, inc=1, device_id=device(dx, dy), device_id_type=pl.DeviceIdType.MESH
        )

    greeted = 0
    for dx, dy, _, _ in partners(SPLIT[2], 6):
        greet(dx, dy)
        greeted += 1
    for k in range(3, gy_size - 2):
        greet(0, k)
        greeted += 1
    for k in range(2, gx_size - 1):
        greet(k, 0)
        greeted += 1

    local = [
        pltpu.make_async_copy(
            conductivity,
            zero.k.at[pl.ds(4, BLOCK_X), pl.ds(PAD + 4, BLOCK_Y), :],
            local_sem.at[0],
        ),
        pltpu.make_async_copy(
            head, zero.va.at[pl.ds(4, BLOCK_X), pl.ds(PAD + 4, BLOCK_Y), :], local_sem.at[1]
        ),
        pltpu.make_async_copy(
            recharge, zero.g.at[pl.ds(3, BLOCK_X), pl.ds(4, BLOCK_Y), :], local_sem.at[2]
        ),
    ]
    for copy in local:
        copy.start()

    pl.semaphore_wait(barrier, greeted)

    def push(src, dst, stage, dx, dy):
        pltpu.make_async_remote_copy(
            src_ref=src,
            dst_ref=dst,
            send_sem=send_sem.at[stage],
            recv_sem=recv_sem.at[stage],
            device_id=device(dx, dy),
            device_id_type=pl.DeviceIdType.MESH,
        ).start()

    def exchange(level, halo, stage, src, src_x, src_row, dst, dst_x, dst_row, far=(True, False)):
        for dx, dy, xs, ys in partners(level, halo):
            if (dx != 0 and dy != 0) in far:
                push(
                    src.at[pl.ds(src_x + xs[0], xs[1]), pl.ds(src_row + ys[0], ys[1]), :],
                    dst.at[pl.ds(dst_x + xs[2], xs[1]), pl.ds(dst_row + ys[2], ys[1]), :],
                    stage,
                    dx,
                    dy,
                )

    def arrived(stage, rows):
        block = tally.at[pl.ds(0, rows), :]
        pltpu.make_async_copy(block, block, recv_sem.at[stage]).wait()

    def sent(stage, rows):
        block = tally.at[pl.ds(0, rows), :]
        pltpu.make_async_copy(block, block, send_sem.at[stage]).wait()

    def far_first(count):
        return sorted(range(1, count), key=lambda k: -min(k, count - k))

    def gather_y(strip, stage):
        for k in far_first(gy_size):
            push(strip.at[pl.ds(gy, 1), :], strip.at[pl.ds(gy, 1), :], stage, 0, k)

    def gather_x(strip, place, stage):
        for k in far_first(gx_size):
            push(strip, place, stage, k, 0)

    lv0, lv1, lv2 = SPLIT
    for far in ((True,), (False,)):
        exchange(lv0, lv0.hk, 0, conductivity, 0, 0, zero.k, 4, PAD + 4, far)
        exchange(lv0, 4, 1, head, 0, 0, zero.va, 4, PAD + 4, far)
        exchange(lv0, lv0.hg, 2, recharge, 0, 0, zero.g, 3, 4, far)

    def pack_3(rows):
        lane, row = iota((8, LANES), 1), iota((8, LANES), 0)
        picked = lane_gather(rows[...], (lane & 15) * 8)
        return jnp.sum(jnp.where((lane >> 4) == row, picked, 0.0), axis=0, keepdims=True)

    def to_rows(value, ref):
        for x in range(4):
            ref[pl.ds(2 * x, 2), :] = value[x]

    local[0].wait()
    own0 = (pl.ds(4, BLOCK_X), pl.ds(PAD + 4, BLOCK_Y))
    own1, own2 = (pl.ds(7, 16), pl.ds(PAD + 8, 8)), (pl.ds(6, 8), pl.ds(PAD + 6, 4))
    one.k[own1] = restrict(zero.k[own0], half0, 1, 0.125)
    two.k[own2] = restrict(one.k[own1], half1_k, 2, 0.125)
    to_rows(restrict(two.k[own2], half2, 4, 0.125), rows_k)
    strip_k[pl.ds(gy, 1), :] = pack_3(rows_k)
    exchange(lv1, lv1.hk, 3, one.k, 7, PAD + 8, one.k, 7, PAD + 8)
    gather_y(strip_k, 7)
    exchange(lv2, lv2.hk, 5, two.k, 6, PAD + 6, two.k, 6, PAD + 6)

    for ref in whole:
        ref.clear_edges()

    arrived(0, exchange_rows(lv0, lv0.hk))
    zero.faces()
    arrived(7, gy_size - 1)
    inner = pl.ds(PAD, gy_size)
    three.k[pl.ds(gx + EDGE, 1), inner, :] = strip_k[...].reshape(1, gy_size, LANES)
    gather_x(strip_k, three.k.at[gx + EDGE, inner, :], 8)
    local[1].wait()
    local[2].wait()
    arrived(1, exchange_rows(lv0, 4))
    arrived(2, exchange_rows(lv0, lv0.hg))
    zero.sweep(zero.va, zero.vb, 3, zero.g)
    zero.sweep(zero.vb, zero.va, 2, zero.g)
    one.g[pl.ds(6, 16), pl.ds(8, 8), :] = restrict(zero.residual(zero.va, 0), half0, 1, 0.5)

    exchange(lv1, lv1.hg, 4, one.g, 6, 8, one.g, 6, 8)
    arrived(3, exchange_rows(lv1, lv1.hk))
    one.faces()
    arrived(5, exchange_rows(lv2, lv2.hk))
    two.faces()
    arrived(8, (gx_size - 1) * gy_size)
    three.faces()
    arrived(4, exchange_rows(lv1, lv1.hg))
    one.first_sweep(one.va, 6, one.g)
    one.sweep(one.va, one.vb, 5, one.g)
    two.g[pl.ds(3, 12), pl.ds(4, 8), :] = restrict(one.residual(one.vb, 4), half1, 2, 0.5)
    two.first_sweep(two.va, 2, two.g)
    two.sweep(two.va, two.vb, 1, two.g)
    to_rows(restrict(two.residual(two.vb, 0), half2, 4, 0.5), rows_g)
    strip_g[pl.ds(gy, 1), :] = pack_3(rows_g)

    gather_y(strip_g, 9)
    own_g = (pl.ds(5, 8), pl.ds(6, 4))
    wide_g[own_g] = two.g[own_g]
    exchange(lv2, lv2.hg, 6, wide_g, 5, 6, wide_g, 5, 6)
    k4 = 0.125 * octet_3(three.inside(three.k)[...])
    four.inside(four.k)[...] = k4
    rest[...] = k4
    weight5, faces5 = faces_5(pack_5(rest, 1.0, 0.125, gx_size, gy_size), gx_size)
    arrived(9, gy_size - 1)
    three.g[pl.ds(gx + EDGE, 1)] = strip_g[...].reshape(1, gy_size, LANES)
    gather_x(strip_g, three.g.at[gx + EDGE], 10)
    arrived(6, exchange_rows(lv2, lv2.hg))
    two.first_sweep(two.va, 5, wide_g)
    two.sweep(two.va, two.vb, 4, wide_g)
    four.faces()
    sent(0, exchange_rows(lv0, lv0.hk))
    sent(1, exchange_rows(lv0, 4))
    sent(2, exchange_rows(lv0, lv0.hg))
    sent(3, exchange_rows(lv1, lv1.hk))
    sent(4, exchange_rows(lv1, lv1.hg))
    sent(5, exchange_rows(lv2, lv2.hk))
    sent(7, gy_size - 1)
    sent(8, (gx_size - 1) * gy_size)
    arrived(10, (gx_size - 1) * gy_size)

    three.first_sweep(three.va)
    three.sweep(three.va, three.vb)
    four.g[pl.ds(*four.all)] = 0.5 * octet_3(three.residual(three.vb))
    four.first_sweep(four.va)
    four.sweep(four.va, four.vb)
    rest[...] = four.residual(four.vb)
    v5 = solve_5(weight5, faces5, pack_5(rest, 0.0, 0.5, gx_size, gy_size))

    coarse5[pl.ds(0, gy_size // 2, stride=2), :] = v5
    coarse5[pl.ds(1, gy_size // 2, stride=2), :] = v5
    def layers(reach):
        return gx + (EDGE - reach), 2 * reach + 1

    shape = (11, gy_size, LANES)
    flat = (11 * gy_size, LANES)
    index = ((gx - 5 + iota(shape, 0)) * 4 + ((iota(shape, 2) & 15) >> 2)) & (LANES - 1)
    wide5 = jnp.broadcast_to(coarse5[...][None], shape).reshape(flat)
    four.correct(four.vb, layers(5), lane_gather(wide5, index.reshape(flat)).reshape(shape))
    four.sweep(four.vb, four.va, layers(4))
    four.sweep(four.va, four.vb, layers(3))
    three.correct(three.vb, layers(3), four.inside(four.vb, layers(3))[...])
    three.sweep(three.vb, three.va, layers(2))
    three.sweep(three.va, three.vb, layers(1))

    row = iota((lv2.rows, LANES), 0)
    lane = iota((lv2.rows, LANES), 1)
    y3 = (row >> 1) - 1
    for dx in (-1, 0, 1):
        near = []
        for dy in (-1, 0, 1):
            place = (pl.ds(gx + (dx + EDGE), 1), pl.ds(gy + (dy + PAD), 1))
            near.append(three.vb[place].reshape(1, LANES))
        rows = jnp.where(y3 < 2, near[0], jnp.where(y3 < 4, near[1], near[2]))
        for x in ((2, 3), (0, 1, 2, 3), (0, 1))[dx + 1]:
            copies = lane_gather(rows, (2 * x + (y3 & 1)) * 16 + (lane >> 3))
            for child in range(2):
                place = (2 * (4 * dx + x) + child + 6, pl.ds(PAD, lv2.rows))
                two.vb[place] = two.vb[place] + copies
    two.sweep(two.vb, two.va, 3, wide_g)
    two.sweep(two.va, two.vb, 2, wide_g)

    one.correct(one.vb, two.vb[pl.ds(4, 12), pl.ds(PAD + 2, 12), :], 3, 12, wide1)
    one.sweep(one.vb, one.va, 2, one.g)
    one.sweep(one.va, one.vb, 1, one.g)
    zero.correct(zero.va, one.vb[pl.ds(6, 18), pl.ds(PAD + 6, 12), :], 2, 18, wide0)
    zero.sweep(zero.va, zero.vb, 1, zero.g)
    zero.last_sweep(zero.vb, out)

    sent(9, gy_size - 1)
    sent(6, exchange_rows(lv2, lv2.hg))
    sent(10, (gx_size - 1) * gy_size)


def on_device(gx_size, gy_size, head, recharge, conductivity):
    scratch = []
    for level in SPLIT:
        scratch += Split.scratch(level)
    for _ in range(2):
        scratch += Whole.scratch(gx_size, gy_size)
    scratch += [
        pltpu.VMEM((16, 16, LANES), F32),
        pltpu.VMEM((12, 16, LANES), F32),
        pltpu.VMEM((8, 8, LANES), F32),
        pltpu.VMEM((4, 4, LANES), F32),
        pltpu.VMEM((18, 16, LANES), F32),
        pltpu.VMEM((18, 24, LANES), F32),
        pltpu.VMEM((12, 24, LANES), F32),
        pltpu.VMEM((8, LANES), F32),
        pltpu.VMEM((8, LANES), F32),
        pltpu.VMEM((gy_size, LANES), F32),
        pltpu.VMEM((gy_size, LANES), F32),
        pltpu.VMEM((gx_size, gy_size, LANES), F32),
        pltpu.VMEM((gy_size, LANES), F32),
        pltpu.VMEM((TALLY_ROWS, LANES), F32),
        pltpu.SemaphoreType.DMA((3,)),
        pltpu.SemaphoreType.DMA((11,)),
        pltpu.SemaphoreType.DMA((11,)),
    ]

    def body(*refs):
        kernel(gx_size, gy_size, *refs)

    return pl.pallas_call(
        body,
        out_shape=jax.ShapeDtypeStruct(head.shape, F32),
        in_specs=[pl.BlockSpec(memory_space=pl.ANY)] * 3,
        out_specs=pl.BlockSpec(memory_space=pltpu.VMEM),
        scratch_shapes=scratch,
        compiler_params=pltpu.CompilerParams(
            collective_id=0, has_side_effects=True, vmem_limit_bytes=62 * 1024 * 1024
        ),
        name="vcycle",
    )(head, recharge, conductivity)


def solution(mesh):
    gx_size, gy_size = mesh.shape["gx"], mesh.shape["gy"]

    def one_device(head, recharge, conductivity):
        return on_device(gx_size, gy_size, head, recharge, conductivity)

    spec = P("gx", "gy", None)
    return jax.shard_map(
        one_device, mesh=mesh, in_specs=(spec, spec, spec), out_specs=spec, check_vma=False
    )
```

```python
from typing import NamedTuple

import jax
import jax.numpy as jnp
from jax import lax
from jax.experimental import pallas as pl
from jax.experimental.pallas import tpu as pltpu
from jax.sharding import PartitionSpec as P

F32 = jnp.float32
LANES = 128
PAD = 8
EDGE = 6
OMEGA = 0.8
KEEP = 1.0 - OMEGA
COARSE_SWEEPS = 16
BLOCK_X = 32
BLOCK_Y = 16
TALLY_ROWS = 512

class Level(NamedTuple):
    bx: int
    by: int
    hx: int
    rows: int
    first: int
    span: int
    reach: int
    hk: int
    hg: int
    cyrows: int


SPLIT = (
    Level(32, 16, 3, 24, 4, 1, 1, 4, 3, 24),
    Level(16, 8, 6, 24, 8, 2, 1, 7, 6, 24),
    Level(8, 4, 5, 16, 6, 4, 2, 6, 5, 16),
)


def reciprocal(x):
    guess = pltpu.reciprocal(x, approx=True)
    return guess * (2.0 - x * guess)


def face(a, b):
    return (2.0 * a * b) * reciprocal(a + b)


def iota(shape, dim):
    return lax.broadcasted_iota(jnp.int32, shape, dim)


def flag(condition):
    return jnp.where(condition, 1.0, 0.0).astype(F32)


def up(value, shift):
    return pltpu.roll(value, LANES - shift, value.ndim - 1)


def down(value, shift):
    return pltpu.roll(value, shift, value.ndim - 1)


def swap(value, bit):
    if 2 * bit == LANES:
        return down(value, bit)
    flat = value.reshape(-1, LANES)
    return lane_gather(flat, iota(flat.shape, 1) ^ bit).reshape(value.shape)


def lane_gather(value, index):
    return jnp.take_along_axis(value, index, axis=1)


def segment(step, block, halo):
    low = max(0, step * block - halo)
    high = min(block, (step + 1) * block + halo)
    return low, high - low, low - step * block


def partners(level, halo):
    found = []
    for dx in (-1, 0, 1):
        for dy in range(-level.reach, level.reach + 1):
            if (dx, dy) != (0, 0):
                near = halo - 1 if dx and dy and level.span <= 2 else halo
                found.append((dx, dy, segment(dx, level.bx, near), segment(dy, level.by, near)))
    return sorted(found, key=lambda p: -abs(p[0]) - abs(p[1]))


def exchange_rows(level, halo):
    return sum(xs[1] * ys[1] for _, _, xs, ys in partners(level, halo))


class Split:
    def __init__(self, level, nx, ny, gx, gy, refs):
        self.at = level
        self.nx, self.ny, self.gx, self.gy = nx, ny, gx, gy
        (self.k, self.va, self.vb, self.g, self.cx, self.cy, self.czl, self.czh, self.w, self.d) = refs

    @staticmethod
    def scratch(level):
        x, rows = level.bx + 2 * level.hx, level.rows
        padded = pltpu.VMEM((x + 2, rows + 2 * PAD, LANES), F32)
        plain = pltpu.VMEM((x, rows, LANES), F32)
        return [
            padded,
            padded,
            padded,
            plain,
            pltpu.VMEM((x + 1, rows, LANES), F32),
            pltpu.VMEM((x, rows + PAD, LANES), F32),
            plain,
            plain,
            plain,
            plain,
        ]

    def faces(self):
        lv = self.at
        count, rows, span = lv.bx + 2 * lv.hx, lv.rows, lv.span
        y = self.gy * lv.by + iota((1, lv.cyrows, LANES), 1) - lv.first
        y_open = flag((y != 0) & (y != self.ny))
        y = y[:, :rows]
        lane = iota((1, rows, LANES), 2)
        z_open = flag(lane >= span)
        cuts = flag((y == 0) | (y == self.ny)) + flag((y == -1) | (y == self.ny - 1))
        cuts = cuts + flag(lane < span) + flag(lane >= LANES - span)
        inner = pl.ds(PAD, rows)
        all_x = pl.ds(1, count)
        here = self.k[all_x, inner, :]
        self.cx[...] = face(
            self.k[pl.ds(0, count + 1), inner, :], self.k[pl.ds(1, count + 1), inner, :]
        )
        cut_low, cut_high = flag(self.gx == 0), flag(self.gx * lv.bx + lv.bx == self.nx)
        for i, cut in ((lv.hx, cut_low), (lv.hx + lv.bx, cut_high)):
            self.cx[i] = self.cx[i] * (1.0 - cut)
        self.cy[:, pl.ds(0, lv.cyrows), :] = y_open * face(
            self.k[all_x, pl.ds(PAD - 1, lv.cyrows), :], self.k[all_x, pl.ds(PAD, lv.cyrows), :]
        )
        low_z = face(down(here, span), here) * z_open
        high_z = up(low_z, span)
        self.czl[...] = low_z
        self.czh[...] = high_z
        total = self.cx[pl.ds(0, count)] + self.cx[pl.ds(1, count)]
        total = total + (self.cy[:, pl.ds(0, rows), :] + self.cy[:, pl.ds(1, rows), :])
        self.d[...] = (total + (low_z + high_z)) + here * cuts
        for i, cut in ((lv.hx, cut_low), (lv.hx + lv.bx - 1, cut_high)):
            self.d[i] = self.d[i] + self.k[i + 1, inner, :] * cut
        self.w[...] = OMEGA * reciprocal(self.d[...])

    def beside(self, v, low, count, row, rows):
        span = self.at.span
        inner, own = pl.ds(PAD + row, rows), pl.ds(row, rows)
        x, mid = pl.ds(low, count), pl.ds(low + 1, count)
        here = v[mid, inner, :]
        along_x = self.cx[x, own, :] * v[x, inner, :] + self.cx[mid, own, :] * v[pl.ds(low + 2, count), inner, :]
        along_y = (
            self.cy[x, own, :] * v[mid, pl.ds(PAD + row - 1, rows), :]
            + self.cy[x, pl.ds(row + 1, rows), :] * v[mid, pl.ds(PAD + row + 1, rows), :]
        )
        along_z = self.czl[x, own, :] * down(here, span) + self.czh[x, own, :] * up(here, span)
        return here, (along_x + along_y) + along_z

    def first_sweep(self, dst, halo, g):
        low, count = self.at.hx - halo, self.at.bx + 2 * halo
        x = pl.ds(low, count)
        dst[pl.ds(low + 1, count), pl.ds(PAD, self.at.rows), :] = self.w[x] * g[x]

    def sweep(self, src, dst, halo, g):
        lv = self.at
        low, count = lv.hx - halo, lv.bx + 2 * halo
        here, total = self.beside(src, low, count, 0, lv.rows)
        x = pl.ds(low, count)
        dst[pl.ds(low + 1, count), pl.ds(PAD, lv.rows), :] = KEEP * here + self.w[x] * (g[x] + total)

    def last_sweep(self, src, out):
        lv = self.at
        x, own = pl.ds(lv.hx, lv.bx), pl.ds(lv.first, lv.by)
        here, total = self.beside(src, lv.hx, lv.bx, lv.first, lv.by)
        out[...] = KEEP * here + self.w[x, own, :] * (self.g[x, own, :] + total)

    def residual(self, v, halo):
        lv = self.at
        low, count = lv.hx - halo, lv.bx + 2 * halo
        row, rows = lv.first - halo, lv.by + 2 * halo
        x, own = pl.ds(low, count), pl.ds(row, rows)
        here, total = self.beside(v, low, count, row, rows)
        return self.g[x, own, :] + total - self.d[x, own, :] * here

    def correct(self, v, coarse, x0, count, wide):
        rows = self.at.rows
        half = rows // 2
        wide[:, pl.ds(0, half, stride=2), :] = coarse
        wide[:, pl.ds(1, half, stride=2), :] = coarse
        place = (pl.ds(x0, 2 * count), pl.ds(PAD, rows))
        copies = jnp.broadcast_to(wide[...][:, None], (count, 2, rows, LANES))
        v[place] = v[place] + copies.reshape(2 * count, rows, LANES)


def restrict(value, half, span, scale):
    x, y, _ = value.shape
    value = value.reshape(x // 2, 2, y, LANES)
    half[...] = value[:, 0] + value[:, 1]
    total = half[:, pl.ds(0, y // 2, stride=2), :] + half[:, pl.ds(1, y // 2, stride=2), :]
    return scale * (total + swap(total, span))


class Whole:
    def __init__(self, number, nx, ny, refs):
        self.number, self.nx, self.ny = number, nx, ny
        self.k, self.va, self.vb, self.g, self.c, self.w, self.d = refs
        self.all = (EDGE, nx)

    @staticmethod
    def scratch(nx, ny):
        x = nx + 2 * EDGE
        padded = pltpu.VMEM((x, ny + 2 * PAD, LANES), F32)
        plain = pltpu.VMEM((x, ny, LANES), F32)
        return [padded, padded, padded, plain, pltpu.VMEM((6, x, ny, LANES), F32), plain, plain]

    def clear_edges(self):
        for x in (0, EDGE + self.nx):
            layers = pl.ds(x, EDGE)
            for ref in (self.k, self.va, self.vb, self.g, self.w):
                ref[layers] = jnp.zeros((EDGE,) + ref.shape[1:], F32)
            self.c[:, layers] = jnp.zeros((6, EDGE, self.ny, LANES), F32)
        for ref in (self.k, self.va, self.vb):
            for row in (0, PAD + self.ny):
                ref[pl.ds(EDGE, self.nx), pl.ds(row, PAD), :] = jnp.zeros((self.nx, PAD, LANES), F32)

    def inside(self, ref, layers=None):
        start, count = layers or self.all
        return ref.at[pl.ds(start, count), pl.ds(PAD, self.ny), :]

    def neighbours(self, v, layers):
        start, count = layers
        inner, mid = pl.ds(PAD, self.ny), pl.ds(start, count)
        here = v[mid, inner, :]
        before = v[pl.ds(start - 1, count), inner, :]
        after = v[pl.ds(start + 1, count), inner, :]
        under = v[mid, pl.ds(PAD - 1, self.ny), :]
        over = v[mid, pl.ds(PAD + 1, self.ny), :]
        lane = iota((1, self.ny, LANES), 2)
        if self.number == 3:
            before = down(jnp.where(lane >= 96, before, here), 32)
            after = up(jnp.where(lane < 32, after, here), 32)
            odd = (lane & 16) != 0
            under = swap(jnp.where(odd, under, here), 16)
            over = swap(jnp.where(odd, here, over), 16)
            span = 1
        else:
            before = down(jnp.where(lane >= 64, before, here), 64)
            after = up(jnp.where(lane < 64, after, here), 64)
            span = 2
        return (before, after, under, over, down(here, span), up(here, span)), here

    def faces(self):
        shape = (self.nx, self.ny, LANES)
        lane, row, x = iota(shape, 2), iota(shape, 1), iota(shape, 0)
        z = lane & 15
        if self.number == 3:
            first_x, last_x, first_y, last_y = lane < 32, lane >= 96, (lane & 16) == 0, (lane & 16) != 0
            first_z, last_z = z == 0, z == 15
            first_y, last_y = (row == 0) & first_y, (row == self.ny - 1) & last_y
        else:
            first_x, last_x, first_y, last_y = lane < 64, lane >= 64, row == 0, row == self.ny - 1
            first_z, last_z = z < 2, z >= 14
        first_x, last_x = (x == 0) & first_x, (x == self.nx - 1) & last_x
        sides, here = self.neighbours(self.k, self.all)
        inside = pl.ds(*self.all)
        total = jnp.zeros(shape, F32)
        for n, cut in enumerate((first_x, last_x, first_y, last_y, first_z, last_z)):
            value = face(here, sides[n])
            self.c[n, inside] = jnp.where(cut, 0.0, value)
            total = total + jnp.where(cut, here, value)
        self.d[inside] = total
        self.w[inside] = OMEGA * reciprocal(total)

    def beside(self, v, layers):
        sides, here = self.neighbours(v, layers)
        parts = [self.c[n, pl.ds(*layers)] * sides[n] for n in range(6)]
        return here, (parts[0] + parts[1]) + (parts[2] + parts[3]) + (parts[4] + parts[5])

    def first_sweep(self, dst):
        x = pl.ds(*self.all)
        self.inside(dst)[...] = self.w[x] * self.g[x]

    def sweep(self, src, dst, layers=None):
        layers = layers or self.all
        x = pl.ds(*layers)
        here, total = self.beside(src, layers)
        self.inside(dst, layers)[...] = KEEP * here + self.w[x] * (self.g[x] + total)

    def residual(self, v):
        x = pl.ds(*self.all)
        here, total = self.beside(v, self.all)
        return self.g[x] + total - self.d[x] * here

    def correct(self, v, layers, values):
        place = self.inside(v, layers)
        place[...] = place[...] + values


def octet_3(value):
    value = value + swap(value, 1)
    value = value + swap(value, 16)
    return value + swap(value, 32)


def pack_5(ref, fill, scale, nx, ny):
    half = ny // 2
    shape = (nx, half, LANES)
    rows = ref[:, pl.ds(0, half, stride=2), :] + ref[:, pl.ds(1, half, stride=2), :]
    rows = scale * rows.reshape(nx * half, LANES)
    index = (iota((nx * half, LANES), 1) & 3) * 4
    children = [lane_gather(rows, index + child) for child in (0, 2, 64, 66)]
    rows = ((children[0] + children[1]) + (children[2] + children[3])).reshape(shape)
    packed = jnp.sum(jnp.where((iota(shape, 2) >> 2) == iota(shape, 0), rows, 0.0), axis=0)
    return packed + jnp.where(iota((half, LANES), 1) >= 4 * nx, fill, 0.0)


def faces_5(k, nx):
    shape = k.shape
    lane, row = iota(shape, 1), iota(shape, 0)
    x, z = lane >> 2, lane & 3
    cuts = (x == 0, x == nx - 1, row == 0, row == shape[0] - 1, z == 0, z == 3)
    total = jnp.zeros(shape, F32)
    faces = []
    for cut, beyond in zip(cuts, sides_5(k)):
        value = face(k, beyond)
        faces.append(jnp.where(cut, 0.0, value))
        total = total + jnp.where(cut, k, value)
    weight = OMEGA * reciprocal(total)
    return weight, [weight * value for value in faces]


def sides_5(v):
    rows = v.shape[0]
    return (down(v, 4), up(v, 4), pltpu.roll(v, 1, 0), pltpu.roll(v, rows - 1, 0), down(v, 1), up(v, 1))


def solve_5(weight, faces, g):
    start = weight * g

    v = start
    for _ in range(COARSE_SWEEPS - 1):
        parts = [c * beyond for c, beyond in zip(faces, sides_5(v))]
        v = (KEEP * v + start) + ((parts[0] + parts[1]) + (parts[2] + parts[3]) + (parts[4] + parts[5]))
    return v


N_SPLIT = 10
N_WHOLE = 7


def kernel(gx_size, gy_size, head, recharge, conductivity, out, *refs):
    refs = list(refs)
    gx, gy = lax.axis_index("gx"), lax.axis_index("gy")
    split = []
    for number, level in enumerate(SPLIT):
        nx, ny = gx_size * level.bx, gy_size * level.by
        split.append(Split(level, nx, ny, gx, gy, refs[:N_SPLIT]))
        del refs[:N_SPLIT]
    whole = []
    for number in (3, 4):
        whole.append(Whole(number, gx_size, gy_size, refs[:N_WHOLE]))
        del refs[:N_WHOLE]
    (
        half0,
        half1,
        half1_k,
        half2,
        wide_g,
        wide0,
        wide1,
        rows_k,
        rows_g,
        strip_k,
        strip_g,
        rest,
        coarse5,
        tally,
        local_sem,
        send_sem,
        recv_sem,
    ) = refs
    zero, one, two = split
    three, four = whole

    def device(dx, dy):
        return {
            "gx": lax.rem(gx + (dx + gx_size), gx_size),
            "gy": lax.rem(gy + (dy + gy_size), gy_size),
        }

    barrier = pltpu.get_barrier_semaphore()

    def greet(dx, dy):
        pl.semaphore_signal(
            barrier, inc=1, device_id=device(dx, dy), device_id_type=pl.DeviceIdType.MESH
        )

    greeted = 0
    for dx, dy, _, _ in partners(SPLIT[2], 6):
        greet(dx, dy)
        greeted += 1
    for k in range(3, gy_size - 2):
        greet(0, k)
        greeted += 1
    for k in range(2, gx_size - 1):
        greet(k, 0)
        greeted += 1

    local = [
        pltpu.make_async_copy(
            conductivity,
            zero.k.at[pl.ds(4, BLOCK_X), pl.ds(PAD + 4, BLOCK_Y), :],
            local_sem.at[0],
        ),
        pltpu.make_async_copy(
            head, zero.va.at[pl.ds(4, BLOCK_X), pl.ds(PAD + 4, BLOCK_Y), :], local_sem.at[1]
        ),
        pltpu.make_async_copy(
            recharge, zero.g.at[pl.ds(3, BLOCK_X), pl.ds(4, BLOCK_Y), :], local_sem.at[2]
        ),
    ]
    for copy in local:
        copy.start()

    pl.semaphore_wait(barrier, greeted)

    def push(src, dst, stage, dx, dy):
        pltpu.make_async_remote_copy(
            src_ref=src,
            dst_ref=dst,
            send_sem=send_sem.at[stage],
            recv_sem=recv_sem.at[stage],
            device_id=device(dx, dy),
            device_id_type=pl.DeviceIdType.MESH,
        ).start()

    def exchange(level, halo, stage, src, src_x, src_row, dst, dst_x, dst_row, far=(True, False)):
        for dx, dy, xs, ys in partners(level, halo):
            if (dx != 0 and dy != 0) in far:
                push(
                    src.at[pl.ds(src_x + xs[0], xs[1]), pl.ds(src_row + ys[0], ys[1]), :],
                    dst.at[pl.ds(dst_x + xs[2], xs[1]), pl.ds(dst_row + ys[2], ys[1]), :],
                    stage,
                    dx,
                    dy,
                )

    def arrived(stage, rows):
        block = tally.at[pl.ds(0, rows), :]
        pltpu.make_async_copy(block, block, recv_sem.at[stage]).wait()

    def sent(stage, rows):
        block = tally.at[pl.ds(0, rows), :]
        pltpu.make_async_copy(block, block, send_sem.at[stage]).wait()

    def far_first(count):
        return sorted(range(1, count), key=lambda k: -min(k, count - k))

    def gather_y(strip, stage):
        for k in far_first(gy_size):
            push(strip.at[pl.ds(gy, 1), :], strip.at[pl.ds(gy, 1), :], stage, 0, k)

    def gather_x(strip, place, stage):
        for k in far_first(gx_size):
            push(strip, place, stage, k, 0)

    lv0, lv1, lv2 = SPLIT
    for far in ((True,), (False,)):
        exchange(lv0, lv0.hk, 0, conductivity, 0, 0, zero.k, 4, PAD + 4, far)
        exchange(lv0, 4, 1, head, 0, 0, zero.va, 4, PAD + 4, far)
        exchange(lv0, lv0.hg, 2, recharge, 0, 0, zero.g, 3, 4, far)

    def pack_3(rows):
        lane, row = iota((8, LANES), 1), iota((8, LANES), 0)
        picked = lane_gather(rows[...], (lane & 15) * 8)
        return jnp.sum(jnp.where((lane >> 4) == row, picked, 0.0), axis=0, keepdims=True)

    def to_rows(value, ref):
        for x in range(4):
            ref[pl.ds(2 * x, 2), :] = value[x]

    local[0].wait()
    own0 = (pl.ds(4, BLOCK_X), pl.ds(PAD + 4, BLOCK_Y))
    own1, own2 = (pl.ds(7, 16), pl.ds(PAD + 8, 8)), (pl.ds(6, 8), pl.ds(PAD + 6, 4))
    one.k[own1] = restrict(zero.k[own0], half0, 1, 0.125)
    two.k[own2] = restrict(one.k[own1], half1_k, 2, 0.125)
    to_rows(restrict(two.k[own2], half2, 4, 0.125), rows_k)
    strip_k[pl.ds(gy, 1), :] = pack_3(rows_k)
    exchange(lv1, lv1.hk, 3, one.k, 7, PAD + 8, one.k, 7, PAD + 8)
    exchange(lv2, lv2.hk, 5, two.k, 6, PAD + 6, two.k, 6, PAD + 6)
    gather_y(strip_k, 7)

    for ref in whole:
        ref.clear_edges()

    arrived(0, exchange_rows(lv0, lv0.hk))
    zero.faces()
    local[1].wait()
    local[2].wait()
    arrived(1, exchange_rows(lv0, 4))
    arrived(2, exchange_rows(lv0, lv0.hg))
    zero.sweep(zero.va, zero.vb, 3, zero.g)
    zero.sweep(zero.vb, zero.va, 2, zero.g)
    one.g[pl.ds(6, 16), pl.ds(8, 8), :] = restrict(zero.residual(zero.va, 0), half0, 1, 0.5)

    exchange(lv1, lv1.hg, 4, one.g, 6, 8, one.g, 6, 8)
    arrived(7, gy_size - 1)
    inner = pl.ds(PAD, gy_size)
    three.k[pl.ds(gx + EDGE, 1), inner, :] = strip_k[...].reshape(1, gy_size, LANES)
    gather_x(strip_k, three.k.at[gx + EDGE, inner, :], 8)
    arrived(3, exchange_rows(lv1, lv1.hk))
    one.faces()
    arrived(5, exchange_rows(lv2, lv2.hk))
    two.faces()
    arrived(4, exchange_rows(lv1, lv1.hg))
    one.first_sweep(one.va, 6, one.g)
    one.sweep(one.va, one.vb, 5, one.g)
    two.g[pl.ds(3, 12), pl.ds(4, 8), :] = restrict(one.residual(one.vb, 4), half1, 2, 0.5)
    two.first_sweep(two.va, 2, two.g)
    two.sweep(two.va, two.vb, 1, two.g)
    to_rows(restrict(two.residual(two.vb, 0), half2, 4, 0.5), rows_g)
    strip_g[pl.ds(gy, 1), :] = pack_3(rows_g)

    gather_y(strip_g, 9)
    own_g = (pl.ds(5, 8), pl.ds(6, 4))
    wide_g[own_g] = two.g[own_g]
    exchange(lv2, lv2.hg, 6, wide_g, 5, 6, wide_g, 5, 6)
    arrived(8, (gx_size - 1) * gy_size)
    three.faces()
    k4 = 0.125 * octet_3(three.inside(three.k)[...])
    four.inside(four.k)[...] = k4
    rest[...] = k4
    weight5, faces5 = faces_5(pack_5(rest, 1.0, 0.125, gx_size, gy_size), gx_size)
    arrived(9, gy_size - 1)
    three.g[pl.ds(gx + EDGE, 1)] = strip_g[...].reshape(1, gy_size, LANES)
    gather_x(strip_g, three.g.at[gx + EDGE], 10)
    arrived(6, exchange_rows(lv2, lv2.hg))
    two.first_sweep(two.va, 5, wide_g)
    two.sweep(two.va, two.vb, 4, wide_g)
    four.faces()
    sent(0, exchange_rows(lv0, lv0.hk))
    sent(1, exchange_rows(lv0, 4))
    sent(2, exchange_rows(lv0, lv0.hg))
    sent(3, exchange_rows(lv1, lv1.hk))
    sent(4, exchange_rows(lv1, lv1.hg))
    sent(5, exchange_rows(lv2, lv2.hk))
    sent(7, gy_size - 1)
    sent(8, (gx_size - 1) * gy_size)
    arrived(10, (gx_size - 1) * gy_size)

    three.first_sweep(three.va)
    three.sweep(three.va, three.vb)
    four.g[pl.ds(*four.all)] = 0.5 * octet_3(three.residual(three.vb))
    four.first_sweep(four.va)
    four.sweep(four.va, four.vb)
    rest[...] = four.residual(four.vb)
    v5 = solve_5(weight5, faces5, pack_5(rest, 0.0, 0.5, gx_size, gy_size))

    coarse5[pl.ds(0, gy_size // 2, stride=2), :] = v5
    coarse5[pl.ds(1, gy_size // 2, stride=2), :] = v5
    def layers(reach):
        return gx + (EDGE - reach), 2 * reach + 1

    shape = (11, gy_size, LANES)
    flat = (11 * gy_size, LANES)
    index = ((gx - 5 + iota(shape, 0)) * 4 + ((iota(shape, 2) & 15) >> 2)) & (LANES - 1)
    wide5 = jnp.broadcast_to(coarse5[...][None], shape).reshape(flat)
    four.correct(four.vb, layers(5), lane_gather(wide5, index.reshape(flat)).reshape(shape))
    four.sweep(four.vb, four.va, layers(4))
    four.sweep(four.va, four.vb, layers(3))
    three.correct(three.vb, layers(3), four.inside(four.vb, layers(3))[...])
    three.sweep(three.vb, three.va, layers(2))
    three.sweep(three.va, three.vb, layers(1))

    row = iota((lv2.rows, LANES), 0)
    lane = iota((lv2.rows, LANES), 1)
    y3 = (row >> 1) - 1
    for dx in (-1, 0, 1):
        near = []
        for dy in (-1, 0, 1):
            place = (pl.ds(gx + (dx + EDGE), 1), pl.ds(gy + (dy + PAD), 1))
            near.append(three.vb[place].reshape(1, LANES))
        rows = jnp.where(y3 < 2, near[0], jnp.where(y3 < 4, near[1], near[2]))
        for x in ((2, 3), (0, 1, 2, 3), (0, 1))[dx + 1]:
            copies = lane_gather(rows, (2 * x + (y3 & 1)) * 16 + (lane >> 3))
            for child in range(2):
                place = (2 * (4 * dx + x) + child + 6, pl.ds(PAD, lv2.rows))
                two.vb[place] = two.vb[place] + copies
    two.sweep(two.vb, two.va, 3, wide_g)
    two.sweep(two.va, two.vb, 2, wide_g)

    one.correct(one.vb, two.vb[pl.ds(4, 12), pl.ds(PAD + 2, 12), :], 3, 12, wide1)
    one.sweep(one.vb, one.va, 2, one.g)
    one.sweep(one.va, one.vb, 1, one.g)
    zero.correct(zero.va, one.vb[pl.ds(6, 18), pl.ds(PAD + 6, 12), :], 2, 18, wide0)
    zero.sweep(zero.va, zero.vb, 1, zero.g)
    zero.last_sweep(zero.vb, out)

    sent(9, gy_size - 1)
    sent(6, exchange_rows(lv2, lv2.hg))
    sent(10, (gx_size - 1) * gy_size)


def on_device(gx_size, gy_size, head, recharge, conductivity):
    scratch = []
    for level in SPLIT:
        scratch += Split.scratch(level)
    for _ in range(2):
        scratch += Whole.scratch(gx_size, gy_size)
    scratch += [
        pltpu.VMEM((16, 16, LANES), F32),
        pltpu.VMEM((12, 16, LANES), F32),
        pltpu.VMEM((8, 8, LANES), F32),
        pltpu.VMEM((4, 4, LANES), F32),
        pltpu.VMEM((18, 16, LANES), F32),
        pltpu.VMEM((18, 24, LANES), F32),
        pltpu.VMEM((12, 24, LANES), F32),
        pltpu.VMEM((8, LANES), F32),
        pltpu.VMEM((8, LANES), F32),
        pltpu.VMEM((gy_size, LANES), F32),
        pltpu.VMEM((gy_size, LANES), F32),
        pltpu.VMEM((gx_size, gy_size, LANES), F32),
        pltpu.VMEM((gy_size, LANES), F32),
        pltpu.VMEM((TALLY_ROWS, LANES), F32),
        pltpu.SemaphoreType.DMA((3,)),
        pltpu.SemaphoreType.DMA((11,)),
        pltpu.SemaphoreType.DMA((11,)),
    ]

    def body(*refs):
        kernel(gx_size, gy_size, *refs)

    return pl.pallas_call(
        body,
        out_shape=jax.ShapeDtypeStruct(head.shape, F32),
        in_specs=[pl.BlockSpec(memory_space=pl.ANY)] * 3,
        out_specs=pl.BlockSpec(memory_space=pltpu.VMEM),
        scratch_shapes=scratch,
        compiler_params=pltpu.CompilerParams(
            collective_id=0, has_side_effects=True, vmem_limit_bytes=62 * 1024 * 1024
        ),
        name="vcycle",
    )(head, recharge, conductivity)


def solution(mesh):
    gx_size, gy_size = mesh.shape["gx"], mesh.shape["gy"]

    def one_device(head, recharge, conductivity):
        return on_device(gx_size, gy_size, head, recharge, conductivity)

    spec = P("gx", "gy", None)
    return jax.shard_map(
        one_device, mesh=mesh, in_specs=(spec, spec, spec), out_specs=spec, check_vma=False
    )
```

```python
from typing import NamedTuple

import jax
import jax.numpy as jnp
from jax import lax
from jax.experimental import pallas as pl
from jax.experimental.pallas import tpu as pltpu
from jax.sharding import PartitionSpec as P

F32 = jnp.float32
LANES = 128
PAD = 8
EDGE = 6
OMEGA = 0.8
KEEP = 1.0 - OMEGA
COARSE_SWEEPS = 16
BLOCK_X = 32
BLOCK_Y = 16
TALLY_ROWS = 512

class Level(NamedTuple):
    bx: int
    by: int
    hx: int
    rows: int
    first: int
    span: int
    reach: int
    hk: int
    hg: int
    cyrows: int


SPLIT = (
    Level(32, 16, 3, 24, 4, 1, 1, 4, 3, 24),
    Level(16, 8, 6, 24, 8, 2, 1, 7, 6, 24),
    Level(8, 4, 5, 16, 6, 4, 2, 6, 5, 16),
)


def reciprocal(x):
    guess = pltpu.reciprocal(x, approx=True)
    return guess * (2.0 - x * guess)


def face(a, b):
    return (2.0 * a * b) * reciprocal(a + b)


def iota(shape, dim):
    return lax.broadcasted_iota(jnp.int32, shape, dim)


def flag(condition):
    return jnp.where(condition, 1.0, 0.0).astype(F32)


def up(value, shift):
    return pltpu.roll(value, LANES - shift, value.ndim - 1)


def down(value, shift):
    return pltpu.roll(value, shift, value.ndim - 1)


def swap(value, bit):
    if 2 * bit == LANES:
        return down(value, bit)
    flat = value.reshape(-1, LANES)
    return lane_gather(flat, iota(flat.shape, 1) ^ bit).reshape(value.shape)


def lane_gather(value, index):
    return jnp.take_along_axis(value, index, axis=1)


def segment(step, block, halo):
    low = max(0, step * block - halo)
    high = min(block, (step + 1) * block + halo)
    return low, high - low, low - step * block


def partners(level, halo):
    found = []
    for dx in (-1, 0, 1):
        for dy in range(-level.reach, level.reach + 1):
            if (dx, dy) != (0, 0):
                near = halo - 1 if dx and dy and level.span <= 2 else halo
                found.append((dx, dy, segment(dx, level.bx, near), segment(dy, level.by, near)))
    return sorted(found, key=lambda p: -abs(p[0]) - abs(p[1]))


def exchange_rows(level, halo):
    return sum(xs[1] * ys[1] for _, _, xs, ys in partners(level, halo))


class Split:
    def __init__(self, level, nx, ny, gx, gy, refs):
        self.at = level
        self.nx, self.ny, self.gx, self.gy = nx, ny, gx, gy
        (self.k, self.va, self.vb, self.g, self.cx, self.cy, self.czl, self.czh, self.w, self.d) = refs

    @staticmethod
    def scratch(level):
        x, rows = level.bx + 2 * level.hx, level.rows
        padded = pltpu.VMEM((x + 2, rows + 2 * PAD, LANES), F32)
        plain = pltpu.VMEM((x, rows, LANES), F32)
        return [
            padded,
            padded,
            padded,
            plain,
            pltpu.VMEM((x + 1, rows, LANES), F32),
            pltpu.VMEM((x, rows + PAD, LANES), F32),
            plain,
            plain,
            plain,
            plain,
        ]

    def faces(self):
        lv = self.at
        count, rows, span = lv.bx + 2 * lv.hx, lv.rows, lv.span
        y = self.gy * lv.by + iota((1, lv.cyrows, LANES), 1) - lv.first
        y_open = flag((y != 0) & (y != self.ny))
        y = y[:, :rows]
        lane = iota((1, rows, LANES), 2)
        z_open = flag(lane >= span)
        cuts = flag((y == 0) | (y == self.ny)) + flag((y == -1) | (y == self.ny - 1))
        cuts = cuts + flag(lane < span) + flag(lane >= LANES - span)
        inner = pl.ds(PAD, rows)
        all_x = pl.ds(1, count)
        here = self.k[all_x, inner, :]
        self.cx[...] = face(
            self.k[pl.ds(0, count + 1), inner, :], self.k[pl.ds(1, count + 1), inner, :]
        )
        cut_low, cut_high = flag(self.gx == 0), flag(self.gx * lv.bx + lv.bx == self.nx)
        for i, cut in ((lv.hx, cut_low), (lv.hx + lv.bx, cut_high)):
            self.cx[i] = self.cx[i] * (1.0 - cut)
        self.cy[:, pl.ds(0, lv.cyrows), :] = y_open * face(
            self.k[all_x, pl.ds(PAD - 1, lv.cyrows), :], self.k[all_x, pl.ds(PAD, lv.cyrows), :]
        )
        low_z = face(down(here, span), here) * z_open
        high_z = up(low_z, span)
        self.czl[...] = low_z
        self.czh[...] = high_z
        total = self.cx[pl.ds(0, count)] + self.cx[pl.ds(1, count)]
        total = total + (self.cy[:, pl.ds(0, rows), :] + self.cy[:, pl.ds(1, rows), :])
        self.d[...] = (total + (low_z + high_z)) + here * cuts
        for i, cut in ((lv.hx, cut_low), (lv.hx + lv.bx - 1, cut_high)):
            self.d[i] = self.d[i] + self.k[i + 1, inner, :] * cut
        self.w[...] = OMEGA * reciprocal(self.d[...])

    def beside(self, v, low, count, row, rows):
        span = self.at.span
        inner, own = pl.ds(PAD + row, rows), pl.ds(row, rows)
        x, mid = pl.ds(low, count), pl.ds(low + 1, count)
        here = v[mid, inner, :]
        along_x = self.cx[x, own, :] * v[x, inner, :] + self.cx[mid, own, :] * v[pl.ds(low + 2, count), inner, :]
        along_y = (
            self.cy[x, own, :] * v[mid, pl.ds(PAD + row - 1, rows), :]
            + self.cy[x, pl.ds(row + 1, rows), :] * v[mid, pl.ds(PAD + row + 1, rows), :]
        )
        along_z = self.czl[x, own, :] * down(here, span) + self.czh[x, own, :] * up(here, span)
        return here, (along_x + along_y) + along_z

    def first_sweep(self, dst, halo, g):
        low, count = self.at.hx - halo, self.at.bx + 2 * halo
        x = pl.ds(low, count)
        dst[pl.ds(low + 1, count), pl.ds(PAD, self.at.rows), :] = self.w[x] * g[x]

    def sweep(self, src, dst, halo, g):
        lv = self.at
        low, count = lv.hx - halo, lv.bx + 2 * halo
        here, total = self.beside(src, low, count, 0, lv.rows)
        x = pl.ds(low, count)
        dst[pl.ds(low + 1, count), pl.ds(PAD, lv.rows), :] = KEEP * here + self.w[x] * (g[x] + total)

    def last_sweep(self, src, out):
        lv = self.at
        x, own = pl.ds(lv.hx, lv.bx), pl.ds(lv.first, lv.by)
        here, total = self.beside(src, lv.hx, lv.bx, lv.first, lv.by)
        out[...] = KEEP * here + self.w[x, own, :] * (self.g[x, own, :] + total)

    def residual(self, v, halo):
        lv = self.at
        low, count = lv.hx - halo, lv.bx + 2 * halo
        row, rows = lv.first - halo, lv.by + 2 * halo
        x, own = pl.ds(low, count), pl.ds(row, rows)
        here, total = self.beside(v, low, count, row, rows)
        return self.g[x, own, :] + total - self.d[x, own, :] * here

    def correct(self, v, coarse, x0, count, wide):
        rows = self.at.rows
        half = rows // 2
        wide[:, pl.ds(0, half, stride=2), :] = coarse
        wide[:, pl.ds(1, half, stride=2), :] = coarse
        place = (pl.ds(x0, 2 * count), pl.ds(PAD, rows))
        copies = jnp.broadcast_to(wide[...][:, None], (count, 2, rows, LANES))
        v[place] = v[place] + copies.reshape(2 * count, rows, LANES)


def restrict(value, half, span, scale):
    x, y, _ = value.shape
    value = value.reshape(x // 2, 2, y, LANES)
    half[...] = value[:, 0] + value[:, 1]
    total = half[:, pl.ds(0, y // 2, stride=2), :] + half[:, pl.ds(1, y // 2, stride=2), :]
    return scale * (total + swap(total, span))


class Whole:
    def __init__(self, number, nx, ny, refs):
        self.number, self.nx, self.ny = number, nx, ny
        self.k, self.va, self.vb, self.g, self.c, self.w, self.d = refs
        self.all = (EDGE, nx)

    @staticmethod
    def scratch(nx, ny):
        x = nx + 2 * EDGE
        padded = pltpu.VMEM((x, ny + 2 * PAD, LANES), F32)
        plain = pltpu.VMEM((x, ny, LANES), F32)
        return [padded, padded, padded, plain, pltpu.VMEM((6, x, ny, LANES), F32), plain, plain]

    def clear_edges(self):
        for x in (0, EDGE + self.nx):
            layers = pl.ds(x, EDGE)
            for ref in (self.k, self.va, self.vb, self.g, self.w):
                ref[layers] = jnp.zeros((EDGE,) + ref.shape[1:], F32)
            self.c[:, layers] = jnp.zeros((6, EDGE, self.ny, LANES), F32)
        for ref in (self.k, self.va, self.vb):
            for row in (0, PAD + self.ny):
                ref[pl.ds(EDGE, self.nx), pl.ds(row, PAD), :] = jnp.zeros((self.nx, PAD, LANES), F32)

    def inside(self, ref, layers=None):
        start, count = layers or self.all
        return ref.at[pl.ds(start, count), pl.ds(PAD, self.ny), :]

    def neighbours(self, v, layers):
        start, count = layers
        inner, mid = pl.ds(PAD, self.ny), pl.ds(start, count)
        here = v[mid, inner, :]
        before = v[pl.ds(start - 1, count), inner, :]
        after = v[pl.ds(start + 1, count), inner, :]
        under = v[mid, pl.ds(PAD - 1, self.ny), :]
        over = v[mid, pl.ds(PAD + 1, self.ny), :]
        lane = iota((1, self.ny, LANES), 2)
        if self.number == 3:
            before = down(jnp.where(lane >= 96, before, here), 32)
            after = up(jnp.where(lane < 32, after, here), 32)
            odd = (lane & 16) != 0
            under = swap(jnp.where(odd, under, here), 16)
            over = swap(jnp.where(odd, here, over), 16)
            span = 1
        else:
            before = down(jnp.where(lane >= 64, before, here), 64)
            after = up(jnp.where(lane < 64, after, here), 64)
            span = 2
        return (before, after, under, over, down(here, span), up(here, span)), here

    def faces(self):
        shape = (self.nx, self.ny, LANES)
        lane, row, x = iota(shape, 2), iota(shape, 1), iota(shape, 0)
        z = lane & 15
        if self.number == 3:
            first_x, last_x, first_y, last_y = lane < 32, lane >= 96, (lane & 16) == 0, (lane & 16) != 0
            first_z, last_z = z == 0, z == 15
            first_y, last_y = (row == 0) & first_y, (row == self.ny - 1) & last_y
        else:
            first_x, last_x, first_y, last_y = lane < 64, lane >= 64, row == 0, row == self.ny - 1
            first_z, last_z = z < 2, z >= 14
        first_x, last_x = (x == 0) & first_x, (x == self.nx - 1) & last_x
        sides, here = self.neighbours(self.k, self.all)
        inside = pl.ds(*self.all)
        total = jnp.zeros(shape, F32)
        for n, cut in enumerate((first_x, last_x, first_y, last_y, first_z, last_z)):
            value = face(here, sides[n])
            self.c[n, inside] = jnp.where(cut, 0.0, value)
            total = total + jnp.where(cut, here, value)
        self.d[inside] = total
        self.w[inside] = OMEGA * reciprocal(total)

    def beside(self, v, layers):
        sides, here = self.neighbours(v, layers)
        parts = [self.c[n, pl.ds(*layers)] * sides[n] for n in range(6)]
        return here, (parts[0] + parts[1]) + (parts[2] + parts[3]) + (parts[4] + parts[5])

    def first_sweep(self, dst):
        x = pl.ds(*self.all)
        self.inside(dst)[...] = self.w[x] * self.g[x]

    def sweep(self, src, dst, layers=None):
        layers = layers or self.all
        x = pl.ds(*layers)
        here, total = self.beside(src, layers)
        self.inside(dst, layers)[...] = KEEP * here + self.w[x] * (self.g[x] + total)

    def residual(self, v):
        x = pl.ds(*self.all)
        here, total = self.beside(v, self.all)
        return self.g[x] + total - self.d[x] * here

    def correct(self, v, layers, values):
        place = self.inside(v, layers)
        place[...] = place[...] + values


def octet_3(value):
    value = value + swap(value, 1)
    value = value + swap(value, 16)
    return value + swap(value, 32)


def pack_5(ref, fill, scale, nx, ny):
    half = ny // 2
    shape = (nx, half, LANES)
    rows = ref[:, pl.ds(0, half, stride=2), :] + ref[:, pl.ds(1, half, stride=2), :]
    rows = scale * rows.reshape(nx * half, LANES)
    index = (iota((nx * half, LANES), 1) & 3) * 4
    children = [lane_gather(rows, index + child) for child in (0, 2, 64, 66)]
    rows = ((children[0] + children[1]) + (children[2] + children[3])).reshape(shape)
    packed = jnp.sum(jnp.where((iota(shape, 2) >> 2) == iota(shape, 0), rows, 0.0), axis=0)
    return packed + jnp.where(iota((half, LANES), 1) >= 4 * nx, fill, 0.0)


def faces_5(k, nx):
    shape = k.shape
    lane, row = iota(shape, 1), iota(shape, 0)
    x, z = lane >> 2, lane & 3
    cuts = (x == 0, x == nx - 1, row == 0, row == shape[0] - 1, z == 0, z == 3)
    total = jnp.zeros(shape, F32)
    faces = []
    for cut, beyond in zip(cuts, sides_5(k)):
        value = face(k, beyond)
        faces.append(jnp.where(cut, 0.0, value))
        total = total + jnp.where(cut, k, value)
    weight = OMEGA * reciprocal(total)
    return weight, [weight * value for value in faces]


def sides_5(v):
    rows = v.shape[0]
    return (down(v, 4), up(v, 4), pltpu.roll(v, 1, 0), pltpu.roll(v, rows - 1, 0), down(v, 1), up(v, 1))


def solve_5(weight, faces, g):
    start = weight * g

    v = start
    for _ in range(COARSE_SWEEPS - 1):
        parts = [c * beyond for c, beyond in zip(faces, sides_5(v))]
        v = (KEEP * v + start) + ((parts[0] + parts[1]) + (parts[2] + parts[3]) + (parts[4] + parts[5]))
    return v


N_SPLIT = 10
N_WHOLE = 7


def kernel(gx_size, gy_size, head, recharge, conductivity, out, *refs):
    refs = list(refs)
    gx, gy = lax.axis_index("gx"), lax.axis_index("gy")
    split = []
    for number, level in enumerate(SPLIT):
        nx, ny = gx_size * level.bx, gy_size * level.by
        split.append(Split(level, nx, ny, gx, gy, refs[:N_SPLIT]))
        del refs[:N_SPLIT]
    whole = []
    for number in (3, 4):
        whole.append(Whole(number, gx_size, gy_size, refs[:N_WHOLE]))
        del refs[:N_WHOLE]
    (
        half0,
        half1,
        half1_k,
        half2,
        wide_g,
        wide0,
        wide1,
        rows_k,
        rows_g,
        strip_k,
        strip_g,
        rest,
        coarse5,
        tally,
        local_sem,
        send_sem,
        recv_sem,
    ) = refs
    zero, one, two = split
    three, four = whole

    def device(dx, dy):
        return {
            "gx": lax.rem(gx + (dx + gx_size), gx_size),
            "gy": lax.rem(gy + (dy + gy_size), gy_size),
        }

    barrier = pltpu.get_barrier_semaphore()

    def greet(dx, dy):
        pl.semaphore_signal(
            barrier, inc=1, device_id=device(dx, dy), device_id_type=pl.DeviceIdType.MESH
        )

    guests = [(0, k) for k in range(3, gy_size - 2)] + [(k, 0) for k in range(2, gx_size - 1)]
    guests.sort(key=lambda g: -min(g[0], gx_size - g[0]) - min(g[1], gy_size - g[1]))
    guests += [(dx, dy) for dx, dy, _, _ in partners(SPLIT[2], 6)]
    for dx, dy in guests:
        greet(dx, dy)

    local = [
        pltpu.make_async_copy(
            conductivity,
            zero.k.at[pl.ds(4, BLOCK_X), pl.ds(PAD + 4, BLOCK_Y), :],
            local_sem.at[0],
        ),
        pltpu.make_async_copy(
            head, zero.va.at[pl.ds(4, BLOCK_X), pl.ds(PAD + 4, BLOCK_Y), :], local_sem.at[1]
        ),
        pltpu.make_async_copy(
            recharge, zero.g.at[pl.ds(3, BLOCK_X), pl.ds(4, BLOCK_Y), :], local_sem.at[2]
        ),
    ]
    for copy in local:
        copy.start()

    pl.semaphore_wait(barrier, len(guests))

    def push(src, dst, stage, dx, dy):
        pltpu.make_async_remote_copy(
            src_ref=src,
            dst_ref=dst,
            send_sem=send_sem.at[stage],
            recv_sem=recv_sem.at[stage],
            device_id=device(dx, dy),
            device_id_type=pl.DeviceIdType.MESH,
        ).start()

    def exchange(level, halo, stage, src, src_x, src_row, dst, dst_x, dst_row, far=(True, False)):
        for dx, dy, xs, ys in partners(level, halo):
            if (dx != 0 and dy != 0) in far:
                push(
                    src.at[pl.ds(src_x + xs[0], xs[1]), pl.ds(src_row + ys[0], ys[1]), :],
                    dst.at[pl.ds(dst_x + xs[2], xs[1]), pl.ds(dst_row + ys[2], ys[1]), :],
                    stage,
                    dx,
                    dy,
                )

    def arrived(stage, rows):
        block = tally.at[pl.ds(0, rows), :]
        pltpu.make_async_copy(block, block, recv_sem.at[stage]).wait()

    def sent(stage, rows):
        block = tally.at[pl.ds(0, rows), :]
        pltpu.make_async_copy(block, block, send_sem.at[stage]).wait()

    def far_first(count):
        return sorted(range(1, count), key=lambda k: -min(k, count - k))

    def gather_y(strip, stage):
        for k in far_first(gy_size):
            push(strip.at[pl.ds(gy, 1), :], strip.at[pl.ds(gy, 1), :], stage, 0, k)

    def gather_x(strip, place, stage):
        for k in far_first(gx_size):
            push(strip, place, stage, k, 0)

    lv0, lv1, lv2 = SPLIT
    for far in ((True,), (False,)):
        exchange(lv0, lv0.hk, 0, conductivity, 0, 0, zero.k, 4, PAD + 4, far)
        exchange(lv0, 4, 1, head, 0, 0, zero.va, 4, PAD + 4, far)
        exchange(lv0, lv0.hg, 2, recharge, 0, 0, zero.g, 3, 4, far)

    def pack_3(rows):
        lane, row = iota((8, LANES), 1), iota((8, LANES), 0)
        picked = lane_gather(rows[...], (lane & 15) * 8)
        return jnp.sum(jnp.where((lane >> 4) == row, picked, 0.0), axis=0, keepdims=True)

    def to_rows(value, ref):
        for x in range(4):
            ref[pl.ds(2 * x, 2), :] = value[x]

    local[0].wait()
    own0 = (pl.ds(4, BLOCK_X), pl.ds(PAD + 4, BLOCK_Y))
    own1, own2 = (pl.ds(7, 16), pl.ds(PAD + 8, 8)), (pl.ds(6, 8), pl.ds(PAD + 6, 4))
    one.k[own1] = restrict(zero.k[own0], half0, 1, 0.125)
    two.k[own2] = restrict(one.k[own1], half1_k, 2, 0.125)
    to_rows(restrict(two.k[own2], half2, 4, 0.125), rows_k)
    strip_k[pl.ds(gy, 1), :] = pack_3(rows_k)
    exchange(lv1, lv1.hk, 3, one.k, 7, PAD + 8, one.k, 7, PAD + 8)
    exchange(lv2, lv2.hk, 5, two.k, 6, PAD + 6, two.k, 6, PAD + 6)


    arrived(0, exchange_rows(lv0, lv0.hk))
    zero.faces()
    local[1].wait()
    local[2].wait()
    arrived(1, exchange_rows(lv0, 4))
    arrived(2, exchange_rows(lv0, lv0.hg))
    zero.sweep(zero.va, zero.vb, 3, zero.g)
    zero.sweep(zero.vb, zero.va, 2, zero.g)
    one.g[pl.ds(6, 16), pl.ds(8, 8), :] = restrict(zero.residual(zero.va, 0), half0, 1, 0.5)

    exchange(lv1, lv1.hg, 4, one.g, 6, 8, one.g, 6, 8)
    gather_y(strip_k, 7)
    for ref in whole:
        ref.clear_edges()
    arrived(3, exchange_rows(lv1, lv1.hk))
    one.faces()
    arrived(5, exchange_rows(lv2, lv2.hk))
    two.faces()
    arrived(4, exchange_rows(lv1, lv1.hg))
    one.first_sweep(one.va, 6, one.g)
    one.sweep(one.va, one.vb, 5, one.g)
    two.g[pl.ds(3, 12), pl.ds(4, 8), :] = restrict(one.residual(one.vb, 4), half1, 2, 0.5)
    two.first_sweep(two.va, 2, two.g)
    two.sweep(two.va, two.vb, 1, two.g)
    to_rows(restrict(two.residual(two.vb, 0), half2, 4, 0.5), rows_g)
    strip_g[pl.ds(gy, 1), :] = pack_3(rows_g)

    gather_y(strip_g, 9)
    arrived(7, gy_size - 1)
    inner = pl.ds(PAD, gy_size)
    three.k[pl.ds(gx + EDGE, 1), inner, :] = strip_k[...].reshape(1, gy_size, LANES)
    gather_x(strip_k, three.k.at[gx + EDGE, inner, :], 8)
    own_g = (pl.ds(5, 8), pl.ds(6, 4))
    wide_g[own_g] = two.g[own_g]
    exchange(lv2, lv2.hg, 6, wide_g, 5, 6, wide_g, 5, 6)
    arrived(9, gy_size - 1)
    three.g[pl.ds(gx + EDGE, 1)] = strip_g[...].reshape(1, gy_size, LANES)
    gather_x(strip_g, three.g.at[gx + EDGE], 10)
    arrived(8, (gx_size - 1) * gy_size)
    three.faces()
    k4 = 0.125 * octet_3(three.inside(three.k)[...])
    four.inside(four.k)[...] = k4
    rest[...] = k4
    weight5, faces5 = faces_5(pack_5(rest, 1.0, 0.125, gx_size, gy_size), gx_size)
    four.faces()
    arrived(6, exchange_rows(lv2, lv2.hg))
    two.first_sweep(two.va, 5, wide_g)
    two.sweep(two.va, two.vb, 4, wide_g)
    sent(0, exchange_rows(lv0, lv0.hk))
    sent(1, exchange_rows(lv0, 4))
    sent(2, exchange_rows(lv0, lv0.hg))
    sent(3, exchange_rows(lv1, lv1.hk))
    sent(4, exchange_rows(lv1, lv1.hg))
    sent(5, exchange_rows(lv2, lv2.hk))
    sent(7, gy_size - 1)
    sent(8, (gx_size - 1) * gy_size)
    arrived(10, (gx_size - 1) * gy_size)

    three.first_sweep(three.va)
    three.sweep(three.va, three.vb)
    four.g[pl.ds(*four.all)] = 0.5 * octet_3(three.residual(three.vb))
    four.first_sweep(four.va)
    four.sweep(four.va, four.vb)
    rest[...] = four.residual(four.vb)
    v5 = solve_5(weight5, faces5, pack_5(rest, 0.0, 0.5, gx_size, gy_size))

    coarse5[pl.ds(0, gy_size // 2, stride=2), :] = v5
    coarse5[pl.ds(1, gy_size // 2, stride=2), :] = v5
    def layers(reach):
        return gx + (EDGE - reach), 2 * reach + 1

    shape = (11, gy_size, LANES)
    flat = (11 * gy_size, LANES)
    index = ((gx - 5 + iota(shape, 0)) * 4 + ((iota(shape, 2) & 15) >> 2)) & (LANES - 1)
    wide5 = jnp.broadcast_to(coarse5[...][None], shape).reshape(flat)
    four.correct(four.vb, layers(5), lane_gather(wide5, index.reshape(flat)).reshape(shape))
    four.sweep(four.vb, four.va, layers(4))
    four.sweep(four.va, four.vb, layers(3))
    three.correct(three.vb, layers(3), four.inside(four.vb, layers(3))[...])
    three.sweep(three.vb, three.va, layers(2))
    three.sweep(three.va, three.vb, layers(1))

    row = iota((lv2.rows, LANES), 0)
    lane = iota((lv2.rows, LANES), 1)
    y3 = (row >> 1) - 1
    for dx in (-1, 0, 1):
        near = []
        for dy in (-1, 0, 1):
            place = (pl.ds(gx + (dx + EDGE), 1), pl.ds(gy + (dy + PAD), 1))
            near.append(three.vb[place].reshape(1, LANES))
        rows = jnp.where(y3 < 2, near[0], jnp.where(y3 < 4, near[1], near[2]))
        for x in ((2, 3), (0, 1, 2, 3), (0, 1))[dx + 1]:
            copies = lane_gather(rows, (2 * x + (y3 & 1)) * 16 + (lane >> 3))
            for child in range(2):
                place = (2 * (4 * dx + x) + child + 6, pl.ds(PAD, lv2.rows))
                two.vb[place] = two.vb[place] + copies
    two.sweep(two.vb, two.va, 3, wide_g)
    two.sweep(two.va, two.vb, 2, wide_g)

    one.correct(one.vb, two.vb[pl.ds(4, 12), pl.ds(PAD + 2, 12), :], 3, 12, wide1)
    one.sweep(one.vb, one.va, 2, one.g)
    one.sweep(one.va, one.vb, 1, one.g)
    zero.correct(zero.va, one.vb[pl.ds(6, 18), pl.ds(PAD + 6, 12), :], 2, 18, wide0)
    zero.sweep(zero.va, zero.vb, 1, zero.g)
    zero.last_sweep(zero.vb, out)

    sent(9, gy_size - 1)
    sent(6, exchange_rows(lv2, lv2.hg))
    sent(10, (gx_size - 1) * gy_size)


def on_device(gx_size, gy_size, head, recharge, conductivity):
    scratch = []
    for level in SPLIT:
        scratch += Split.scratch(level)
    for _ in range(2):
        scratch += Whole.scratch(gx_size, gy_size)
    scratch += [
        pltpu.VMEM((16, 16, LANES), F32),
        pltpu.VMEM((12, 16, LANES), F32),
        pltpu.VMEM((8, 8, LANES), F32),
        pltpu.VMEM((4, 4, LANES), F32),
        pltpu.VMEM((18, 16, LANES), F32),
        pltpu.VMEM((18, 24, LANES), F32),
        pltpu.VMEM((12, 24, LANES), F32),
        pltpu.VMEM((8, LANES), F32),
        pltpu.VMEM((8, LANES), F32),
        pltpu.VMEM((gy_size, LANES), F32),
        pltpu.VMEM((gy_size, LANES), F32),
        pltpu.VMEM((gx_size, gy_size, LANES), F32),
        pltpu.VMEM((gy_size, LANES), F32),
        pltpu.VMEM((TALLY_ROWS, LANES), F32),
        pltpu.SemaphoreType.DMA((3,)),
        pltpu.SemaphoreType.DMA((11,)),
        pltpu.SemaphoreType.DMA((11,)),
    ]

    def body(*refs):
        kernel(gx_size, gy_size, *refs)

    return pl.pallas_call(
        body,
        out_shape=jax.ShapeDtypeStruct(head.shape, F32),
        in_specs=[pl.BlockSpec(memory_space=pl.ANY)] * 3,
        out_specs=pl.BlockSpec(memory_space=pltpu.VMEM),
        scratch_shapes=scratch,
        compiler_params=pltpu.CompilerParams(
            collective_id=0, has_side_effects=True, vmem_limit_bytes=62 * 1024 * 1024
        ),
        name="vcycle",
    )(head, recharge, conductivity)


def solution(mesh):
    gx_size, gy_size = mesh.shape["gx"], mesh.shape["gy"]

    def one_device(head, recharge, conductivity):
        return on_device(gx_size, gy_size, head, recharge, conductivity)

    spec = P("gx", "gy", None)
    return jax.shard_map(
        one_device, mesh=mesh, in_specs=(spec, spec, spec), out_specs=spec, check_vma=False
    )
```

```python
from typing import NamedTuple

import jax
import jax.numpy as jnp
from jax import lax
from jax.experimental import pallas as pl
from jax.experimental.pallas import tpu as pltpu
from jax.sharding import PartitionSpec as P

F32 = jnp.float32
LANES = 128
PAD = 8
EDGE = 6
OMEGA = 0.8
KEEP = 1.0 - OMEGA
COARSE_SWEEPS = 16
BLOCK_X = 32
BLOCK_Y = 16
TALLY_ROWS = 512

class Level(NamedTuple):
    bx: int
    by: int
    hx: int
    rows: int
    first: int
    span: int
    reach: int
    hk: int
    hg: int
    cyrows: int


SPLIT = (
    Level(32, 16, 3, 24, 4, 1, 1, 4, 3, 24),
    Level(16, 8, 6, 24, 8, 2, 1, 7, 6, 24),
    Level(8, 4, 5, 16, 6, 4, 2, 6, 5, 16),
)


def reciprocal(x):
    guess = pltpu.reciprocal(x, approx=True)
    return guess * (2.0 - x * guess)


def face(a, b):
    return (2.0 * a * b) * reciprocal(a + b)


def iota(shape, dim):
    return lax.broadcasted_iota(jnp.int32, shape, dim)


def flag(condition):
    return jnp.where(condition, 1.0, 0.0).astype(F32)


def up(value, shift):
    return pltpu.roll(value, LANES - shift, value.ndim - 1)


def down(value, shift):
    return pltpu.roll(value, shift, value.ndim - 1)


def swap(value, bit):
    if 2 * bit == LANES:
        return down(value, bit)
    flat = value.reshape(-1, LANES)
    return lane_gather(flat, iota(flat.shape, 1) ^ bit).reshape(value.shape)


def lane_gather(value, index):
    return jnp.take_along_axis(value, index, axis=1)


def segment(step, block, halo):
    low = max(0, step * block - halo)
    high = min(block, (step + 1) * block + halo)
    return low, high - low, low - step * block


def partners(level, halo):
    found = []
    for dx in (-1, 0, 1):
        for dy in range(-level.reach, level.reach + 1):
            if (dx, dy) != (0, 0):
                near = halo - 1 if dx and dy and level.span <= 2 else halo
                found.append((dx, dy, segment(dx, level.bx, near), segment(dy, level.by, near)))
    return sorted(found, key=lambda p: -abs(p[0]) - abs(p[1]))


def exchange_rows(level, halo):
    return sum(xs[1] * ys[1] for _, _, xs, ys in partners(level, halo))


class Split:
    def __init__(self, level, nx, ny, gx, gy, refs):
        self.at = level
        self.nx, self.ny, self.gx, self.gy = nx, ny, gx, gy
        (self.k, self.va, self.vb, self.g, self.cx, self.cy, self.czl, self.czh, self.w, self.d) = refs

    @staticmethod
    def scratch(level):
        x, rows = level.bx + 2 * level.hx, level.rows
        padded = pltpu.VMEM((x + 2, rows + 2 * PAD, LANES), F32)
        plain = pltpu.VMEM((x, rows, LANES), F32)
        return [
            padded,
            padded,
            padded,
            plain,
            pltpu.VMEM((x + 1, rows, LANES), F32),
            pltpu.VMEM((x, rows + PAD, LANES), F32),
            plain,
            plain,
            plain,
            plain,
        ]

    def faces(self):
        lv = self.at
        count, rows, span = lv.bx + 2 * lv.hx, lv.rows, lv.span
        y = self.gy * lv.by + iota((1, lv.cyrows, LANES), 1) - lv.first
        y_open = flag((y != 0) & (y != self.ny))
        y = y[:, :rows]
        lane = iota((1, rows, LANES), 2)
        z_open = flag(lane >= span)
        cuts = flag((y == 0) | (y == self.ny)) + flag((y == -1) | (y == self.ny - 1))
        cuts = cuts + flag(lane < span) + flag(lane >= LANES - span)
        inner = pl.ds(PAD, rows)
        all_x = pl.ds(1, count)
        here = self.k[all_x, inner, :]
        self.cx[...] = face(
            self.k[pl.ds(0, count + 1), inner, :], self.k[pl.ds(1, count + 1), inner, :]
        )
        cut_low, cut_high = flag(self.gx == 0), flag(self.gx * lv.bx + lv.bx == self.nx)
        for i, cut in ((lv.hx, cut_low), (lv.hx + lv.bx, cut_high)):
            self.cx[i] = self.cx[i] * (1.0 - cut)
        self.cy[:, pl.ds(0, lv.cyrows), :] = y_open * face(
            self.k[all_x, pl.ds(PAD - 1, lv.cyrows), :], self.k[all_x, pl.ds(PAD, lv.cyrows), :]
        )
        low_z = face(down(here, span), here) * z_open
        high_z = up(low_z, span)
        self.czl[...] = low_z
        self.czh[...] = high_z
        total = self.cx[pl.ds(0, count)] + self.cx[pl.ds(1, count)]
        total = total + (self.cy[:, pl.ds(0, rows), :] + self.cy[:, pl.ds(1, rows), :])
        self.d[...] = (total + (low_z + high_z)) + here * cuts
        for i, cut in ((lv.hx, cut_low), (lv.hx + lv.bx - 1, cut_high)):
            self.d[i] = self.d[i] + self.k[i + 1, inner, :] * cut
        self.w[...] = OMEGA * reciprocal(self.d[...])

    def beside(self, v, low, count, row, rows):
        span = self.at.span
        inner, own = pl.ds(PAD + row, rows), pl.ds(row, rows)
        x, mid = pl.ds(low, count), pl.ds(low + 1, count)
        here = v[mid, inner, :]
        along_x = self.cx[x, own, :] * v[x, inner, :] + self.cx[mid, own, :] * v[pl.ds(low + 2, count), inner, :]
        along_y = (
            self.cy[x, own, :] * v[mid, pl.ds(PAD + row - 1, rows), :]
            + self.cy[x, pl.ds(row + 1, rows), :] * v[mid, pl.ds(PAD + row + 1, rows), :]
        )
        along_z = self.czl[x, own, :] * down(here, span) + self.czh[x, own, :] * up(here, span)
        return here, (along_x + along_y) + along_z

    def first_sweep(self, dst, halo, g):
        low, count = self.at.hx - halo, self.at.bx + 2 * halo
        x = pl.ds(low, count)
        dst[pl.ds(low + 1, count), pl.ds(PAD, self.at.rows), :] = self.w[x] * g[x]

    def sweep(self, src, dst, halo, g):
        lv = self.at
        low, count = lv.hx - halo, lv.bx + 2 * halo
        here, total = self.beside(src, low, count, 0, lv.rows)
        x = pl.ds(low, count)
        dst[pl.ds(low + 1, count), pl.ds(PAD, lv.rows), :] = KEEP * here + self.w[x] * (g[x] + total)

    def last_sweep(self, src, out):
        lv = self.at
        x, own = pl.ds(lv.hx, lv.bx), pl.ds(lv.first, lv.by)
        here, total = self.beside(src, lv.hx, lv.bx, lv.first, lv.by)
        out[...] = KEEP * here + self.w[x, own, :] * (self.g[x, own, :] + total)

    def residual(self, v, halo):
        lv = self.at
        low, count = lv.hx - halo, lv.bx + 2 * halo
        row, rows = lv.first - halo, lv.by + 2 * halo
        x, own = pl.ds(low, count), pl.ds(row, rows)
        here, total = self.beside(v, low, count, row, rows)
        return self.g[x, own, :] + total - self.d[x, own, :] * here

    def correct(self, v, coarse, x0, count, wide):
        rows = self.at.rows
        half = rows // 2
        wide[:, pl.ds(0, half, stride=2), :] = coarse
        wide[:, pl.ds(1, half, stride=2), :] = coarse
        place = (pl.ds(x0, 2 * count), pl.ds(PAD, rows))
        copies = jnp.broadcast_to(wide[:, pl.ds(0, rows), :][:, None], (count, 2, rows, LANES))
        v[place] = v[place] + copies.reshape(2 * count, rows, LANES)


def restrict(value, half, span, scale):
    x, y, _ = value.shape
    value = value.reshape(x // 2, 2, y, LANES)
    half[:, pl.ds(0, y), :] = value[:, 0] + value[:, 1]
    total = half[:, pl.ds(0, y // 2, stride=2), :] + half[:, pl.ds(1, y // 2, stride=2), :]
    return scale * (total + swap(total, span))


class Whole:
    def __init__(self, number, nx, ny, refs):
        self.number, self.nx, self.ny = number, nx, ny
        self.k, self.va, self.vb, self.g, self.c, self.w, self.d = refs
        self.all = (EDGE, nx)

    @staticmethod
    def scratch(nx, ny):
        x = nx + 2 * EDGE
        padded = pltpu.VMEM((x, ny + 2 * PAD, LANES), F32)
        plain = pltpu.VMEM((x, ny, LANES), F32)
        return [padded, padded, padded, plain, pltpu.VMEM((6, x, ny, LANES), F32), plain, plain]

    def clear_edges(self):
        for x in (0, EDGE + self.nx):
            layers = pl.ds(x, EDGE)
            for ref in (self.k, self.va, self.vb, self.g, self.w):
                ref[layers] = jnp.zeros((EDGE,) + ref.shape[1:], F32)
            self.c[:, layers] = jnp.zeros((6, EDGE, self.ny, LANES), F32)
        for ref in (self.k, self.va, self.vb):
            for row in (0, PAD + self.ny):
                ref[pl.ds(EDGE, self.nx), pl.ds(row, PAD), :] = jnp.zeros((self.nx, PAD, LANES), F32)

    def inside(self, ref, layers=None):
        start, count = layers or self.all
        return ref.at[pl.ds(start, count), pl.ds(PAD, self.ny), :]

    def neighbours(self, v, layers):
        start, count = layers
        inner, mid = pl.ds(PAD, self.ny), pl.ds(start, count)
        here = v[mid, inner, :]
        before = v[pl.ds(start - 1, count), inner, :]
        after = v[pl.ds(start + 1, count), inner, :]
        under = v[mid, pl.ds(PAD - 1, self.ny), :]
        over = v[mid, pl.ds(PAD + 1, self.ny), :]
        lane = iota((1, self.ny, LANES), 2)
        if self.number == 3:
            before = down(jnp.where(lane >= 96, before, here), 32)
            after = up(jnp.where(lane < 32, after, here), 32)
            odd = (lane & 16) != 0
            under = swap(jnp.where(odd, under, here), 16)
            over = swap(jnp.where(odd, here, over), 16)
            span = 1
        else:
            before = down(jnp.where(lane >= 64, before, here), 64)
            after = up(jnp.where(lane < 64, after, here), 64)
            span = 2
        return (before, after, under, over, down(here, span), up(here, span)), here

    def faces(self):
        shape = (self.nx, self.ny, LANES)
        lane, row, x = iota(shape, 2), iota(shape, 1), iota(shape, 0)
        z = lane & 15
        if self.number == 3:
            first_x, last_x, first_y, last_y = lane < 32, lane >= 96, (lane & 16) == 0, (lane & 16) != 0
            first_z, last_z = z == 0, z == 15
            first_y, last_y = (row == 0) & first_y, (row == self.ny - 1) & last_y
        else:
            first_x, last_x, first_y, last_y = lane < 64, lane >= 64, row == 0, row == self.ny - 1
            first_z, last_z = z < 2, z >= 14
        first_x, last_x = (x == 0) & first_x, (x == self.nx - 1) & last_x
        sides, here = self.neighbours(self.k, self.all)
        inside = pl.ds(*self.all)
        total = jnp.zeros(shape, F32)
        for n, cut in enumerate((first_x, last_x, first_y, last_y, first_z, last_z)):
            value = face(here, sides[n])
            self.c[n, inside] = jnp.where(cut, 0.0, value)
            total = total + jnp.where(cut, here, value)
        self.d[inside] = total
        self.w[inside] = OMEGA * reciprocal(total)

    def beside(self, v, layers):
        sides, here = self.neighbours(v, layers)
        parts = [self.c[n, pl.ds(*layers)] * sides[n] for n in range(6)]
        return here, (parts[0] + parts[1]) + (parts[2] + parts[3]) + (parts[4] + parts[5])

    def first_sweep(self, dst):
        x = pl.ds(*self.all)
        self.inside(dst)[...] = self.w[x] * self.g[x]

    def sweep(self, src, dst, layers=None):
        layers = layers or self.all
        x = pl.ds(*layers)
        here, total = self.beside(src, layers)
        self.inside(dst, layers)[...] = KEEP * here + self.w[x] * (self.g[x] + total)

    def residual(self, v):
        x = pl.ds(*self.all)
        here, total = self.beside(v, self.all)
        return self.g[x] + total - self.d[x] * here

    def correct(self, v, layers, values):
        place = self.inside(v, layers)
        place[...] = place[...] + values


def octet_3(value):
    value = value + swap(value, 1)
    value = value + swap(value, 16)
    return value + swap(value, 32)


def pack_5(ref, fill, scale, nx, ny):
    half = ny // 2
    shape = (nx, half, LANES)
    rows = ref[:, pl.ds(0, half, stride=2), :] + ref[:, pl.ds(1, half, stride=2), :]
    rows = scale * rows.reshape(nx * half, LANES)
    index = (iota((nx * half, LANES), 1) & 3) * 4
    children = [lane_gather(rows, index + child) for child in (0, 2, 64, 66)]
    rows = ((children[0] + children[1]) + (children[2] + children[3])).reshape(shape)
    packed = jnp.sum(jnp.where((iota(shape, 2) >> 2) == iota(shape, 0), rows, 0.0), axis=0)
    return packed + jnp.where(iota((half, LANES), 1) >= 4 * nx, fill, 0.0)


def faces_5(k, nx):
    shape = k.shape
    lane, row = iota(shape, 1), iota(shape, 0)
    x, z = lane >> 2, lane & 3
    cuts = (x == 0, x == nx - 1, row == 0, row == shape[0] - 1, z == 0, z == 3)
    total = jnp.zeros(shape, F32)
    faces = []
    for cut, beyond in zip(cuts, sides_5(k)):
        value = face(k, beyond)
        faces.append(jnp.where(cut, 0.0, value))
        total = total + jnp.where(cut, k, value)
    weight = OMEGA * reciprocal(total)
    return weight, [weight * value for value in faces]


def sides_5(v):
    rows = v.shape[0]
    return (down(v, 4), up(v, 4), pltpu.roll(v, 1, 0), pltpu.roll(v, rows - 1, 0), down(v, 1), up(v, 1))


def solve_5(weight, faces, g):
    start = weight * g

    v = start
    for _ in range(COARSE_SWEEPS - 1):
        parts = [c * beyond for c, beyond in zip(faces, sides_5(v))]
        v = (KEEP * v + start) + ((parts[0] + parts[1]) + (parts[2] + parts[3]) + (parts[4] + parts[5]))
    return v


N_SPLIT = 10
N_WHOLE = 7


def kernel(gx_size, gy_size, head, recharge, conductivity, out, *refs):
    refs = list(refs)
    gx, gy = lax.axis_index("gx"), lax.axis_index("gy")
    split = []
    for number, level in enumerate(SPLIT):
        nx, ny = gx_size * level.bx, gy_size * level.by
        split.append(Split(level, nx, ny, gx, gy, refs[:N_SPLIT]))
        del refs[:N_SPLIT]
    whole = []
    for number in (3, 4):
        whole.append(Whole(number, gx_size, gy_size, refs[:N_WHOLE]))
        del refs[:N_WHOLE]
    (
        half0,
        half1,
        half1_k,
        half2,
        wide_g,
        wide0,
        wide1,
        rows_k,
        rows_g,
        strip_k,
        strip_g,
        rest,
        coarse5,
        tally,
        local_sem,
        send_sem,
        recv_sem,
    ) = refs
    zero, one, two = split
    three, four = whole

    def device(dx, dy):
        return {
            "gx": lax.rem(gx + (dx + gx_size), gx_size),
            "gy": lax.rem(gy + (dy + gy_size), gy_size),
        }

    barrier = pltpu.get_barrier_semaphore()

    def greet(dx, dy):
        pl.semaphore_signal(
            barrier, inc=1, device_id=device(dx, dy), device_id_type=pl.DeviceIdType.MESH
        )

    guests = [(0, k) for k in range(3, gy_size - 2)] + [(k, 0) for k in range(2, gx_size - 1)]
    guests.sort(key=lambda g: -min(g[0], gx_size - g[0]) - min(g[1], gy_size - g[1]))
    guests += [(dx, dy) for dx, dy, _, _ in partners(SPLIT[2], 6)]
    for dx, dy in guests:
        greet(dx, dy)

    local = [
        pltpu.make_async_copy(
            conductivity,
            zero.k.at[pl.ds(4, BLOCK_X), pl.ds(PAD + 4, BLOCK_Y), :],
            local_sem.at[0],
        ),
        pltpu.make_async_copy(
            head, zero.va.at[pl.ds(4, BLOCK_X), pl.ds(PAD + 4, BLOCK_Y), :], local_sem.at[1]
        ),
        pltpu.make_async_copy(
            recharge, zero.g.at[pl.ds(3, BLOCK_X), pl.ds(4, BLOCK_Y), :], local_sem.at[2]
        ),
    ]
    for copy in local:
        copy.start()

    pl.semaphore_wait(barrier, len(guests))

    def push(src, dst, stage, dx, dy):
        pltpu.make_async_remote_copy(
            src_ref=src,
            dst_ref=dst,
            send_sem=send_sem.at[stage],
            recv_sem=recv_sem.at[stage],
            device_id=device(dx, dy),
            device_id_type=pl.DeviceIdType.MESH,
        ).start()

    def exchange(level, halo, stage, src, src_x, src_row, dst, dst_x, dst_row, far=(True, False)):
        for dx, dy, xs, ys in partners(level, halo):
            if (dx != 0 and dy != 0) in far:
                push(
                    src.at[pl.ds(src_x + xs[0], xs[1]), pl.ds(src_row + ys[0], ys[1]), :],
                    dst.at[pl.ds(dst_x + xs[2], xs[1]), pl.ds(dst_row + ys[2], ys[1]), :],
                    stage,
                    dx,
                    dy,
                )

    def arrived(stage, rows):
        block = tally.at[pl.ds(0, rows), :]
        pltpu.make_async_copy(block, block, recv_sem.at[stage]).wait()

    def sent(stage, rows):
        block = tally.at[pl.ds(0, rows), :]
        pltpu.make_async_copy(block, block, send_sem.at[stage]).wait()

    def far_first(count):
        return sorted(range(1, count), key=lambda k: -min(k, count - k))

    def gather_y(strip, stage):
        for k in far_first(gy_size):
            push(strip.at[pl.ds(gy, 1), :], strip.at[pl.ds(gy, 1), :], stage, 0, k)

    def gather_x(strip, place, stage):
        for k in far_first(gx_size):
            push(strip.at[pl.ds(0, gy_size), :], place, stage, k, 0)

    lv0, lv1, lv2 = SPLIT
    for far in ((True,), (False,)):
        exchange(lv0, lv0.hk, 0, conductivity, 0, 0, zero.k, 4, PAD + 4, far)
        exchange(lv0, 4, 1, head, 0, 0, zero.va, 4, PAD + 4, far)
        exchange(lv0, lv0.hg, 2, recharge, 0, 0, zero.g, 3, 4, far)

    def pack_3(rows):
        lane, row = iota((8, LANES), 1), iota((8, LANES), 0)
        picked = lane_gather(rows[pl.ds(0, 8), :], (lane & 15) * 8)
        return jnp.sum(jnp.where((lane >> 4) == row, picked, 0.0), axis=0, keepdims=True)

    def to_rows(value, ref):
        for x in range(4):
            ref[pl.ds(2 * x, 2), :] = value[x]

    local[0].wait()
    own0 = (pl.ds(4, BLOCK_X), pl.ds(PAD + 4, BLOCK_Y))
    own1, own2 = (pl.ds(7, 16), pl.ds(PAD + 8, 8)), (pl.ds(6, 8), pl.ds(PAD + 6, 4))
    one.k[own1] = restrict(zero.k[own0], half0, 1, 0.125)
    two.k[own2] = restrict(one.k[own1], half1_k, 2, 0.125)
    to_rows(restrict(two.k[own2], half2, 4, 0.125), rows_k)
    strip_k[pl.ds(gy, 1), :] = pack_3(rows_k)
    exchange(lv1, lv1.hk, 3, one.k, 7, PAD + 8, one.k, 7, PAD + 8)
    exchange(lv2, lv2.hk, 5, two.k, 6, PAD + 6, two.k, 6, PAD + 6)

    arrived(0, exchange_rows(lv0, lv0.hk))
    zero.faces()
    local[1].wait()
    local[2].wait()
    arrived(1, exchange_rows(lv0, 4))
    arrived(2, exchange_rows(lv0, lv0.hg))
    zero.sweep(zero.va, zero.vb, 3, zero.g)
    zero.sweep(zero.vb, zero.va, 2, zero.g)
    one.g[pl.ds(6, 16), pl.ds(8, 8), :] = restrict(zero.residual(zero.va, 0), half0, 1, 0.5)

    exchange(lv1, lv1.hg, 4, one.g, 6, 8, one.g, 6, 8)
    gather_y(strip_k, 7)
    for ref in whole:
        ref.clear_edges()
    arrived(3, exchange_rows(lv1, lv1.hk))
    one.faces()
    arrived(5, exchange_rows(lv2, lv2.hk))
    two.faces()
    arrived(4, exchange_rows(lv1, lv1.hg))
    one.first_sweep(one.va, 6, one.g)
    one.sweep(one.va, one.vb, 5, one.g)
    two.g[pl.ds(3, 12), pl.ds(4, 8), :] = restrict(one.residual(one.vb, 4), half1, 2, 0.5)
    two.first_sweep(two.va, 2, two.g)
    two.sweep(two.va, two.vb, 1, two.g)
    to_rows(restrict(two.residual(two.vb, 0), half2, 4, 0.5), rows_g)
    strip_g[pl.ds(gy, 1), :] = pack_3(rows_g)

    gather_y(strip_g, 9)
    arrived(7, gy_size - 1)
    inner = pl.ds(PAD, gy_size)
    three.k[pl.ds(gx + EDGE, 1), inner, :] = strip_k[pl.ds(0, gy_size), :].reshape(1, gy_size, LANES)
    gather_x(strip_k, three.k.at[gx + EDGE, inner, :], 8)
    own_g = (pl.ds(5, 8), pl.ds(6, 4))
    wide_g[own_g] = two.g[own_g]
    exchange(lv2, lv2.hg, 6, wide_g, 5, 6, wide_g, 5, 6)
    arrived(9, gy_size - 1)
    three.g[pl.ds(gx + EDGE, 1)] = strip_g[pl.ds(0, gy_size), :].reshape(1, gy_size, LANES)
    gather_x(strip_g, three.g.at[gx + EDGE], 10)
    arrived(8, (gx_size - 1) * gy_size)
    three.faces()
    k4 = 0.125 * octet_3(three.inside(three.k)[...])
    four.inside(four.k)[...] = k4
    rest[...] = k4
    weight5, faces5 = faces_5(pack_5(rest, 1.0, 0.125, gx_size, gy_size), gx_size)
    four.faces()
    arrived(6, exchange_rows(lv2, lv2.hg))
    two.first_sweep(two.va, 5, wide_g)
    two.sweep(two.va, two.vb, 4, wide_g)
    sent(0, exchange_rows(lv0, lv0.hk))
    sent(1, exchange_rows(lv0, 4))
    sent(2, exchange_rows(lv0, lv0.hg))
    sent(3, exchange_rows(lv1, lv1.hk))
    sent(4, exchange_rows(lv1, lv1.hg))
    sent(5, exchange_rows(lv2, lv2.hk))
    sent(7, gy_size - 1)
    sent(8, (gx_size - 1) * gy_size)
    arrived(10, (gx_size - 1) * gy_size)

    three.first_sweep(three.va)
    three.sweep(three.va, three.vb)
    four.g[pl.ds(*four.all)] = 0.5 * octet_3(three.residual(three.vb))
    four.first_sweep(four.va)
    four.sweep(four.va, four.vb)
    rest[...] = four.residual(four.vb)
    v5 = solve_5(weight5, faces5, pack_5(rest, 0.0, 0.5, gx_size, gy_size))

    coarse5[pl.ds(0, gy_size // 2, stride=2), :] = v5
    coarse5[pl.ds(1, gy_size // 2, stride=2), :] = v5
    def layers(reach):
        return gx + (EDGE - reach), 2 * reach + 1

    shape = (11, gy_size, LANES)
    flat = (11 * gy_size, LANES)
    index = ((gx - 5 + iota(shape, 0)) * 4 + ((iota(shape, 2) & 15) >> 2)) & (LANES - 1)
    wide5 = jnp.broadcast_to(coarse5[...][None], shape).reshape(flat)
    four.correct(four.vb, layers(5), lane_gather(wide5, index.reshape(flat)).reshape(shape))
    four.sweep(four.vb, four.va, layers(4))
    four.sweep(four.va, four.vb, layers(3))
    three.correct(three.vb, layers(3), four.inside(four.vb, layers(3))[...])
    three.sweep(three.vb, three.va, layers(2))
    three.sweep(three.va, three.vb, layers(1))

    row = iota((lv2.rows, LANES), 0)
    lane = iota((lv2.rows, LANES), 1)
    y3 = (row >> 1) - 1
    for dx in (-1, 0, 1):
        near = []
        for dy in (-1, 0, 1):
            place = (pl.ds(gx + (dx + EDGE), 1), pl.ds(gy + (dy + PAD), 1))
            near.append(three.vb[place].reshape(1, LANES))
        rows = jnp.where(y3 < 2, near[0], jnp.where(y3 < 4, near[1], near[2]))
        for x in ((2, 3), (0, 1, 2, 3), (0, 1))[dx + 1]:
            copies = lane_gather(rows, (2 * x + (y3 & 1)) * 16 + (lane >> 3))
            for child in range(2):
                place = (2 * (4 * dx + x) + child + 6, pl.ds(PAD, lv2.rows))
                two.vb[place] = two.vb[place] + copies
    two.sweep(two.vb, two.va, 3, wide_g)
    two.sweep(two.va, two.vb, 2, wide_g)

    one.correct(one.vb, two.vb[pl.ds(4, 12), pl.ds(PAD + 2, 12), :], 3, 12, wide1)
    one.sweep(one.vb, one.va, 2, one.g)
    one.sweep(one.va, one.vb, 1, one.g)
    zero.correct(zero.va, one.vb[pl.ds(6, 18), pl.ds(PAD + 6, 12), :], 2, 18, wide0)
    zero.sweep(zero.va, zero.vb, 1, zero.g)
    zero.last_sweep(zero.vb, out)

    sent(9, gy_size - 1)
    sent(6, exchange_rows(lv2, lv2.hg))
    sent(10, (gx_size - 1) * gy_size)


def on_device(gx_size, gy_size, head, recharge, conductivity):
    scratch = []
    for level in SPLIT:
        scratch += Split.scratch(level)
    for _ in range(2):
        scratch += Whole.scratch(gx_size, gy_size)
    scratch += [
        pltpu.VMEM((16, 16, LANES), F32),
        pltpu.VMEM((12, 16, LANES), F32),
        pltpu.VMEM((8, 16, LANES), F32),
        pltpu.VMEM((4, 16, LANES), F32),
        pltpu.VMEM((18, 16, LANES), F32),
        pltpu.VMEM((18, 32, LANES), F32),
        pltpu.VMEM((12, 32, LANES), F32),
        pltpu.VMEM((16, LANES), F32),
        pltpu.VMEM((16, LANES), F32),
        pltpu.VMEM((gy_size + PAD, LANES), F32),
        pltpu.VMEM((gy_size + PAD, LANES), F32),
        pltpu.VMEM((gx_size, gy_size, LANES), F32),
        pltpu.VMEM((gy_size, LANES), F32),
        pltpu.VMEM((TALLY_ROWS, LANES), F32),
        pltpu.SemaphoreType.DMA((3,)),
        pltpu.SemaphoreType.DMA((11,)),
        pltpu.SemaphoreType.DMA((11,)),
    ]

    def body(*refs):
        kernel(gx_size, gy_size, *refs)

    return pl.pallas_call(
        body,
        out_shape=jax.ShapeDtypeStruct(head.shape, F32),
        in_specs=[pl.BlockSpec(memory_space=pl.ANY)] * 3,
        out_specs=pl.BlockSpec(memory_space=pltpu.VMEM),
        scratch_shapes=scratch,
        compiler_params=pltpu.CompilerParams(
            collective_id=0, has_side_effects=True, vmem_limit_bytes=62 * 1024 * 1024
        ),
        name="vcycle",
    )(head, recharge, conductivity)


def solution(mesh):
    gx_size, gy_size = mesh.shape["gx"], mesh.shape["gy"]

    def one_device(head, recharge, conductivity):
        return on_device(gx_size, gy_size, head, recharge, conductivity)

    spec = P("gx", "gy", None)
    return jax.shard_map(
        one_device, mesh=mesh, in_specs=(spec, spec, spec), out_specs=spec, check_vma=False
    )
```
